32 devices in a mesh: ctx: 8 (over y, x, core), head: 4 (over z).
Axes of the slice: x: 2, y: 2, z: 4, core: 2. Of those that a mesh axis runs over, the one named last changes fastest.
Arguments:
- query: bfloat16 [512, 64, 128], P('ctx', 'head'), may hold values from -6 to 6
- weights: bfloat16 [512, 64], P('ctx', 'head'), as said below
- keys: bfloat16 [16384, 128], P('ctx'), may hold values from -6 to 6
- main_logits: bfloat16 [512, 16384], P(None, 'ctx'), as said below
- row_weight: float32 [512], replicated, may hold values from 4 to 40
- offset: int32 [1], replicated, may hold values from 15360 to 15872
Outputs:
- query_grad: float32 [512, 64, 128], P('ctx', 'head')
- key_grad: float32 [16384, 128], P(('ctx', 'head'))
- weight_grad: float32 [512, 64], P('ctx', 'head')
The draws below stay inside these ranges and needn't reach their ends.
Inputs may be any that keep to these rules, and one draw needn't show every extreme that they name: query row t of the block sits at position offset + t. Finite weights. `main_logits`: finite logits.
All inputs are finite; a program needn't handle non-finite values.
Results may differ from the reference program's by a relative error of at most 0.0065.
Values may be sent and summed in bfloat16 or wider, within the bound.
No kernel may reach another device: no remote copies, remote signals or barrier semaphores. Data moves between devices by JAX's collectives and lax.ppermute only.
A program may use at most 64 MiB of HBM per device.

```python
import math
import jax
import jax.numpy as jnp
from jax import lax

H = 64
DH = 128
Q_ROWS = 512
KEYS = 16384


def draw_weights(key, part):
    key = jax.random.fold_in(key, 11)
    values = jnp.clip(jax.random.normal(jax.random.fold_in(key, 1), (Q_ROWS, H), jnp.float32), -6.0, 6.0) * H ** (-0.5)
    return values.astype(jnp.bfloat16)


def draw_main_logits(key, part):
    key = jax.random.fold_in(key, 12)
    values = 1.5 * jnp.clip(jax.random.normal(jax.random.fold_in(key, 1), (Q_ROWS, KEYS), jnp.float32), -6.0, 6.0)
    return values.astype(jnp.bfloat16)


def block_levels(key, dims, split, low, top_value):
    def one(axis_at, blocks):
        draws = jax.random.uniform(jax.random.fold_in(jax.random.fold_in(key, 6), axis_at), (blocks,), jnp.float32, low / len(split), top_value / len(split))
        return jnp.repeat(jnp.exp(draws), dims[axis_at] // blocks).reshape((-1,) + (1,) * (len(dims) - axis_at - 1))

    gain = one(*split[0])
    for cut in split[1:]:
        gain = gain * one(*cut)
    return gain


def noise(key, extent, scale, reach, pieces=(), held_as=jnp.bfloat16):
    entries = jax.random.normal(key, extent, jnp.float32) * scale
    if len(pieces) > 0:
        entries = block_levels(key, extent, pieces, -0.22, 0.18) * entries
    return jnp.clip(entries, min=-reach, max=reach).astype(held_as)


def setup_inputs(seed: int = 0) -> dict:
    splits = jax.random.split(jax.random.key(seed), 7)
    return {
        "query": noise(splits[0], (Q_ROWS, H, DH), 1.0, 6.0, ((0, 8), (1, 4))),
        "weights": draw_weights(jax.random.fold_in(splits[6], 71), 0),
        "keys": noise(splits[2], (KEYS, DH), 1.0, 6.0, ((0, 8),)),
        "main_logits": draw_main_logits(jax.random.fold_in(splits[6], 71), 0),
        "row_weight": jnp.clip(jnp.exp(jax.random.uniform(splits[4], (Q_ROWS,), jnp.float32, math.log(4.0), math.log(40.0))), 4.0, 40.0),
        "offset": jax.random.randint(splits[5], (1,), KEYS - 2 * Q_ROWS, KEYS - Q_ROWS + 1).astype(jnp.int32),
    }


masked_value = -1e30


def softmax_rows(values, allowed):
    masked = jnp.where(allowed, values, masked_value)
    peak = jnp.max(masked, axis=1, keepdims=True)
    expd = jnp.where(allowed, jnp.exp(masked - peak), 0.0)
    return expd / jnp.sum(expd, axis=1, keepdims=True)


def reference(query, weights, keys, main_logits, row_weight, offset):
    head_scale = DH ** -0.5
    loss_scale = KEYS ** 0.5
    block_len = min(1024, KEYS)
    nblocks = KEYS // block_len
    query_f = query.astype(jnp.float32)
    weight_f = weights.astype(jnp.float32)
    key_blocks = keys.reshape(nblocks, block_len, DH)
    high = lax.Precision.HIGHEST

    def forward_block(key_block):
        dotted = jnp.einsum('thd,sd->ths', query_f, key_block.astype(jnp.float32), precision=high)
        active = jnp.maximum(dotted, 0.0) * head_scale
        return jnp.einsum('th,ths->ts', weight_f, active, precision=high)

    score = jnp.moveaxis(lax.map(forward_block, key_blocks), 0, 1).reshape(Q_ROWS, KEYS)
    row_ids = jnp.arange(Q_ROWS, dtype=jnp.int32)[:, None]
    columns = jnp.arange(KEYS, dtype=jnp.int32)[None, :]
    allowed = columns <= offset[0] + row_ids
    index_prob = softmax_rows(score, allowed)
    target = softmax_rows(main_logits.astype(jnp.float32), allowed)
    score_grad = jnp.where(allowed, row_weight[:, None] * loss_scale * (index_prob - target), 0.0).astype(jnp.bfloat16)
    grad_blocks = jnp.moveaxis(score_grad.reshape(Q_ROWS, nblocks, block_len), 1, 0)

    def backward_block(carry, inputs):
        query_acc, weight_acc = carry
        key_block, grad_block = inputs
        key_f = key_block.astype(jnp.float32)
        dotted = jnp.einsum('thd,sd->ths', query_f, key_f, precision=high)
        active = jnp.maximum(dotted, 0.0) * head_scale
        grad_f = grad_block.astype(jnp.float32)
        pre_grad = jnp.where(dotted > 0, grad_f[:, None, :] * weight_f[:, :, None] * head_scale, 0.0)
        pre_grad = pre_grad.astype(jnp.bfloat16).astype(jnp.float32)
        query_acc = query_acc + jnp.einsum('ths,sd->thd', pre_grad, key_f, precision=high)
        weight_acc = weight_acc + jnp.einsum('ts,ths->th', grad_f, active, precision=high)
        key_part = jnp.einsum('ths,thd->sd', pre_grad, query_f, precision=high)
        return (query_acc, weight_acc), key_part

    start_carry = (jnp.zeros((Q_ROWS, H, DH), jnp.float32), jnp.zeros((Q_ROWS, H), jnp.float32))
    (query_grad, weight_grad), key_parts = lax.scan(backward_block, start_carry, (key_blocks, grad_blocks))
    return query_grad, key_parts.reshape(KEYS, DH), weight_grad
```

```python
import functools

import jax
import jax.numpy as jnp
from jax import lax
from jax.experimental import pallas as pl
from jax.experimental.pallas import tpu as pltpu
from jax.sharding import PartitionSpec as P

masked_value = -1e30
lanes = 128
stat_rows = 8
vmem_bytes = 26 * 1024 * 1024
contract_last = (((1,), (1,)), ((), ()))


def swap(value, axis, distance):
    size = lax.axis_size(axis)
    return lax.ppermute(value, axis, [(i, i ^ distance) for i in range(size)])


def in_pairs(count, first, step):
    first(0, 0)

    def body(i, _):
        step(0, 2 * i, 2 * i + 1)
        step(1, 2 * i + 1, 2 * i + 2)
        return 0

    lax.fori_loop(0, count // 2 - 1, body, 0)
    step(0, count - 2, count - 1)
    step(1, count - 1, None)


def row_limits(meta_ref, rows_here):
    row = lax.broadcasted_iota(jnp.int32, (rows_here, 1), 0)
    return meta_ref[0] + meta_ref[1] * rows_here + row


def piece_allowed(meta_ref, limit, k, kc, chunk):
    first = (meta_ref[1] ^ k) * kc + meta_ref[2] * chunk
    position = first + lax.broadcasted_iota(jnp.int32, (limit.shape[0], chunk), 1)
    return position <= limit


def forward_kernel(cfg, meta_ref, *refs):
    n, nh, rows_here, hh, depth, kc, chunk, scale = cfg
    q_refs, k_refs = refs[:nh], refs[nh : nh + n]
    logits_ref, score_ref, keys_ref, qw_ref, stats_ref = refs[nh + n : nh + n + 5]
    q_all, wb, dots, cols = refs[nh + n + 5 :]
    groups, rows = q_all.shape[0], q_all.shape[1]
    bt = rows_here // groups
    part = bt * hh
    tile = dots.shape[3]
    for k in range(n):
        keys_ref[k * chunk : (k + 1) * chunk, :] = k_refs[k][...]
    eye = (
        lax.broadcasted_iota(jnp.int32, (hh, lanes), 0)
        == lax.broadcasted_iota(jnp.int32, (hh, lanes), 1)
    ).astype(jnp.float32)
    for j in range(nh):
        slab = q_refs[j][rows_here:].reshape(rows_here, lanes).astype(jnp.float32)
        for g in range(groups):
            w = slab[g * bt : (g + 1) * bt]
            picked = jnp.sum(w[:, None, :] * eye[None], axis=-1, keepdims=True)
            wide = jnp.broadcast_to(picked, (bt, hh, lanes)).reshape(part, lanes)
            q = q_refs[j][g * bt : (g + 1) * bt].reshape(part, depth)
            q_all[g, j * part : (j + 1) * part, :] = q
            wb[g, j * part : (j + 1) * part, :] = wide
            scaled = (q.astype(jnp.float32) * (wide * scale)).T.astype(jnp.bfloat16)
            qw_ref[j, :, g * part : (g + 1) * part] = scaled

    def key_tile(s):
        return keys_ref[pl.ds(pl.multiple_of(s * tile, tile), tile), :]

    def products(buffer, s, g, keys):
        dots[buffer, g] = lax.dot_general(
            q_all[g], keys, contract_last, preferred_element_type=jnp.float32
        )

    def first(buffer, s):
        keys = key_tile(s)
        for g in range(groups):
            products(buffer, s, g, keys)

    def step(buffer, s, following):
        if following is not None:
            keys = key_tile(following)
        for g in range(groups):
            if following is not None:
                products(1 - buffer, following, g, keys)
            for i in range(tile // lanes):
                total = None
                for j in range(nh):
                    at = slice(j * part, (j + 1) * part)
                    value = dots[buffer, g, at, i * lanes : (i + 1) * lanes]
                    value = jnp.maximum(value, 0.0) * wb[g, at, :]
                    total = value if total is None else total + value
                summed = jnp.sum(total.reshape(bt, hh, lanes), axis=1) * scale
                column = pl.multiple_of(s * tile + i * lanes, lanes)
                score_ref[g * bt : (g + 1) * bt, pl.ds(column, lanes)] = summed

    in_pairs(n * chunk // tile, first, step)

    limit = row_limits(meta_ref, rows_here)
    lane = lax.broadcasted_iota(jnp.int32, (rows_here, lanes), 1)
    out = jnp.zeros((rows_here, lanes), jnp.float32)

    def piece(i, k):
        if i == 0:
            return score_ref[:, k * chunk : (k + 1) * chunk]
        return logits_ref[meta_ref[1] ^ k].astype(jnp.float32)

    for i in range(2):
        peak = None
        for k in range(n):
            allowed = piece_allowed(meta_ref, limit, k, kc, chunk)
            here = jnp.max(jnp.where(allowed, piece(i, k), masked_value), axis=1, keepdims=True)
            peak = here if peak is None else jnp.maximum(peak, here)
        total = None
        for k in range(n):
            allowed = piece_allowed(meta_ref, limit, k, kc, chunk)
            here = jnp.where(allowed, jnp.exp(piece(i, k) - peak), 0.0)
            here = jnp.sum(here, axis=1, keepdims=True)
            total = here if total is None else total + here
        out = jnp.where(lane == 2 * i, peak, out)
        out = jnp.where(lane == 2 * i + 1, total, out)
    cols[...] = jnp.zeros_like(cols)
    cols[:rows_here, :] = out
    stats_ref[0] = cols[...].T[:stat_rows]


def score_gradient(cfg, meta_ref, stats, rw_ref, logits_ref, score_ref, cols, grad_ref):
    n, nh, rows_here, hh, depth, kc, chunk, scale = cfg
    for i in range(2):
        peak = functools.reduce(jnp.maximum, [st[2 * i : 2 * i + 1] for st in stats])
        total = functools.reduce(
            jnp.add,
            [st[2 * i + 1 : 2 * i + 2] * jnp.exp(st[2 * i : 2 * i + 1] - peak) for st in stats],
        )
        cols[2 * i : 2 * i + 1, :] = peak
        cols[2 * i + 1 : 2 * i + 2, :] = rw_ref[...] / total
    cols[4:, :] = jnp.zeros((cols.shape[0] - 4, cols.shape[1]), jnp.float32)
    st = cols[...].T[:rows_here]
    limit = row_limits(meta_ref, rows_here)
    for k in range(n):
        logits = logits_ref[meta_ref[1] ^ k].astype(jnp.float32)
        score = score_ref[:, k * chunk : (k + 1) * chunk]
        g = jnp.exp(score - st[:, 0:1]) * st[:, 1:2] - jnp.exp(logits - st[:, 2:3]) * st[:, 3:4]
        g = jnp.where(piece_allowed(meta_ref, limit, k, kc, chunk), g, 0.0)
        grad_ref[:, k * chunk : (k + 1) * chunk] = g.astype(jnp.bfloat16)


def backward_kernel(cfg, is_first, is_last, meta_ref, *refs):
    n, nh, rows_here, hh, depth, kc, chunk, scale = cfg
    refs = list(refs)
    take = lambda count: [refs.pop(0) for _ in range(count)]
    q_ref, qw_ref, keys_ref = take(3)
    if is_first:
        stat_refs = take(nh)
        rw_ref, logits_ref, score_ref = take(3)
    else:
        grad_ref, kg_in_ref = take(2)
    (u_ref,) = take(1)
    if is_last:
        even_refs = take(n // 2)
        odd_refs = take(1)
    else:
        (kg_ref,) = take(1)
    if is_first:
        (grad_ref,) = take(1)
    masks, u_acc = take(2)
    if is_first:
        (cols,) = take(1)
    if is_last:
        (kg_ref,) = take(1)
    tile = masks.shape[2]
    rows = rows_here * hh
    if is_first:
        stats = [ref[0] for ref in stat_refs]
        score_gradient(cfg, meta_ref, stats, rw_ref, logits_ref, score_ref, cols, grad_ref)

    def tile_at(s):
        return pl.ds(pl.multiple_of(s * tile, tile), tile)

    def mask(buffer, s):
        dotted = lax.dot_general(
            q_ref[:rows_here].reshape(rows, depth),
            keys_ref[tile_at(s), :],
            contract_last,
            preferred_element_type=jnp.float32,
        )
        g = grad_ref[:, tile_at(s)].astype(jnp.float32)
        wide = jnp.broadcast_to(g[:, None, :], (rows_here, hh, tile)).reshape(rows, tile)
        masks[buffer] = jnp.where(dotted > 0, wide, 0.0).astype(jnp.bfloat16)

    def step(buffer, s, following):
        if following is not None:
            mask(1 - buffer, following)
        masked = masks[buffer]
        u_acc[...] += jnp.dot(
            masked, keys_ref[tile_at(s), :], preferred_element_type=jnp.float32
        )
        more = jnp.dot(qw_ref[0], masked, preferred_element_type=jnp.float32)
        if is_first:
            kg_ref[:, tile_at(s)] = more
        else:
            kg_ref[:, tile_at(s)] = kg_in_ref[:, tile_at(s)] + more

    u_acc[...] = jnp.zeros_like(u_acc)
    in_pairs(n * chunk // tile, mask, step)
    u_ref[...] = u_acc[...].reshape(rows_here, hh, depth).astype(u_ref.dtype)
    if is_last:
        for i in range(n // 2):
            k = 2 * i
            even_refs[i][...] = kg_ref[:, k * chunk : (k + 1) * chunk]
            odd_refs[0][i] = kg_ref[:, (k + 1) * chunk : (k + 2) * chunk].astype(jnp.bfloat16)


def per_device(query, weights, keys, main_logits, row_weight, offset):
    n = lax.axis_size("ctx")
    nh = lax.axis_size("head")
    c = lax.axis_index("ctx")
    h = lax.axis_index("head")
    rows_here, hh, depth = query.shape
    kc = keys.shape[0]
    chunk = kc // nh
    rows = rows_here * hh
    scale = depth ** (-0.5)
    loss_scale = float(kc * n) ** 0.5
    bf16, f32 = jnp.bfloat16, jnp.float32

    w_slab = jnp.pad(weights, ((0, 0), (0, lanes - hh))).reshape(rows_here // hh, hh, lanes)
    message = jnp.concatenate([query, w_slab], axis=0)
    q_blocks = [message] + [swap(message, "head", j) for j in range(1, nh)]

    k_pieces = [None] * n
    k_pieces[0] = lax.dynamic_slice_in_dim(keys, h * chunk, chunk, 0)
    for k in range(0, n, 2):
        if k > 0:
            k_pieces[k] = swap(k_pieces[0], "ctx", k)
        k_pieces[k + 1] = swap(k_pieces[k], "ctx", 1)

    logits = lax.dynamic_slice_in_dim(main_logits, h * chunk, chunk, 1)
    logits = lax.all_to_all(logits.reshape(n, rows_here, chunk), "ctx", 0, 0, tiled=True)

    meta = jnp.concatenate([offset, jnp.stack([c, h]).astype(jnp.int32)])
    rw = lax.dynamic_slice_in_dim(row_weight, c * rows_here, rows_here, 0)[None, :]
    padded = -(-rows_here // lanes) * lanes
    rw = jnp.pad(rw * loss_scale, ((0, 0), (0, padded - rows_here)))

    cfg = (n, nh, rows_here, hh, depth, kc, chunk, scale)
    total_keys = n * chunk
    groups = max(1, rows_here // 16)
    smem = pl.BlockSpec(memory_space=pltpu.SMEM)
    vmem = pl.BlockSpec(memory_space=pltpu.VMEM)
    macs = rows * total_keys * depth
    params = pltpu.CompilerParams(vmem_limit_bytes=vmem_bytes)
    tile = 256
    score, keys_all, qw, stats = pl.pallas_call(
        functools.partial(forward_kernel, cfg),
        out_shape=[
            jax.ShapeDtypeStruct((rows_here, total_keys), f32),
            jax.ShapeDtypeStruct((total_keys, depth), bf16),
            jax.ShapeDtypeStruct((nh, depth, rows), bf16),
            jax.ShapeDtypeStruct((1, stat_rows, padded), f32),
        ],
        in_specs=[smem] + [vmem] * (nh + n + 1),
        out_specs=[vmem] * 4,
        scratch_shapes=[
            pltpu.VMEM((groups, nh * rows // groups, depth), bf16),
            pltpu.VMEM((groups, nh * rows // groups, lanes), f32),
            pltpu.VMEM((2, groups, nh * rows // groups, tile), f32),
            pltpu.VMEM((padded, lanes), f32),
        ],
        compiler_params=params,
        cost_estimate=pl.CostEstimate(
            flops=4 * nh * macs, bytes_accessed=6 * 1024 * 1024, transcendentals=0
        ),
        name="forward",
    )(meta, *q_blocks, *k_pieces, logits)

    all_stats = [stats] + [swap(stats, "head", j) for j in range(1, nh)]

    tile = 512
    grad = kg = None
    sent = []
    for j in reversed(range(nh)):
        is_first, is_last = j == nh - 1, j == 0
        operands = [meta, q_blocks[j], lax.slice_in_dim(qw, j, j + 1, axis=0), keys_all]
        u_type = f32 if is_last else bf16
        out_shape = [jax.ShapeDtypeStruct((rows_here, hh, depth), u_type)]
        scratch = [pltpu.VMEM((2, rows, tile), bf16), pltpu.VMEM((rows, depth), f32)]
        if is_first:
            operands += all_stats + [rw, logits, score]
        else:
            operands += [grad, kg]
        if is_last:
            out_shape += [jax.ShapeDtypeStruct((depth, chunk), f32) for _ in range(n // 2)]
            out_shape += [jax.ShapeDtypeStruct((n // 2, depth, chunk), bf16)]
            scratch += [pltpu.VMEM((depth, total_keys), f32)]
        else:
            out_shape += [jax.ShapeDtypeStruct((depth, total_keys), f32)]
        if is_first:
            out_shape += [jax.ShapeDtypeStruct((rows_here, total_keys), bf16)]
            scratch += [pltpu.VMEM((padded, lanes), f32)]
        outs = pl.pallas_call(
            functools.partial(backward_kernel, cfg, is_first, is_last),
            out_shape=out_shape,
            in_specs=[smem] + [vmem] * (len(operands) - 1),
            out_specs=[vmem] * len(out_shape),
            scratch_shapes=scratch,
            compiler_params=params,
            cost_estimate=pl.CostEstimate(
                flops=12 * macs, bytes_accessed=4 * 1024 * 1024, transcendentals=0
            ),
            name=f"backward{j}",
        )(*operands)
        if is_last:
            u_mine, even, odd = outs[0], outs[1 : 1 + n // 2], outs[1 + n // 2]
        else:
            sent.append(swap(outs[0], "head", j))
            kg = outs[1]
        if is_first:
            grad = outs[2]

    other = swap(odd, "ctx", 1)
    even = [even[i] + other[i].astype(f32) for i in range(n // 2)]
    key_grad = even[0]
    for i in range(1, n // 2):
        key_grad = key_grad + swap(even[i].astype(bf16), "ctx", 2 * i).astype(f32)
    key_grad = key_grad.T

    total = u_mine
    for value in sent:
        total = total + value.astype(f32)
    weight_f = weights.astype(f32)
    query_grad = total * (weight_f * scale)[:, :, None]
    weight_grad = jnp.sum(total * query.astype(f32), axis=-1) * scale
    return query_grad, key_grad, weight_grad


def solution(mesh):
    in_specs = (P("ctx", "head", None), P("ctx", "head"), P("ctx", None), P(None, "ctx"), P(), P())
    out_specs = (P("ctx", "head", None), P(("ctx", "head"), None), P("ctx", "head"))
    return jax.shard_map(
        per_device, mesh=mesh, in_specs=in_specs, out_specs=out_specs, check_vma=False
    )
```

```python
import functools

import jax
import jax.numpy as jnp
from jax import lax
from jax.experimental import pallas as pl
from jax.experimental.pallas import tpu as pltpu
from jax.sharding import PartitionSpec as P

masked_value = -1e30
lanes = 128
stat_rows = 8
vmem_bytes = 14 * 1024 * 1024
contract_last = (((1,), (1,)), ((), ()))


def swap(value, axis, distance):
    size = lax.axis_size(axis)
    return lax.ppermute(value, axis, [(i, i ^ distance) for i in range(size)])


def ring_next(value, axis):
    size = lax.axis_size(axis)
    ring = list(range(0, size, 2)) + list(range(1, size, 2))[::-1]
    return lax.ppermute(value, axis, [(ring[i], ring[(i + 1) % size]) for i in range(size)])


def in_pairs(count, first, step):
    first(0, 0)

    def body(i, _):
        step(0, 2 * i, 2 * i + 1)
        step(1, 2 * i + 1, 2 * i + 2)
        return 0

    lax.fori_loop(0, count // 2 - 1, body, 0)
    step(0, count - 2, count - 1)
    step(1, count - 1, None)


def row_limits(meta_ref, rows_here):
    row = lax.broadcasted_iota(jnp.int32, (rows_here, 1), 0)
    return meta_ref[0] + meta_ref[1] * rows_here + row


def piece_allowed(meta_ref, limit, k, kc, chunk):
    first = (meta_ref[1] ^ k) * kc + meta_ref[2] * chunk
    position = first + lax.broadcasted_iota(jnp.int32, (limit.shape[0], chunk), 1)
    return position <= limit


def forward_kernel(cfg, count, is_first, is_last, meta_ref, *refs):
    order, nh, rows_here, hh, depth, kc, chunk, scale = cfg
    n = len(order)
    rows = rows_here * hh
    refs = list(refs)
    take = lambda count: [refs.pop(0) for _ in range(count)]
    q_refs = take(count)
    if is_first:
        k_refs = take(n)
    else:
        keys_ref, before_ref = take(2)
    if is_last:
        (logits_ref,) = take(1)
    (score_ref,) = take(1)
    qw_refs = take(count)
    if is_first:
        (keys_ref,) = take(1)
    if is_last:
        (stats_ref,) = take(1)
    q_all, wb, dots = take(3)
    tile = dots.shape[3]
    tiles = n * chunk // tile
    wide_by = tile // lanes
    if is_first:
        for i in range(n):
            keys_ref[i * chunk : (i + 1) * chunk, :] = k_refs[i][...]

    eye = (
        lax.broadcasted_iota(jnp.int32, (rows_here, lanes), 0)
        == lax.broadcasted_iota(jnp.int32, (rows_here, lanes), 1)
    ).astype(jnp.float32)
    for j, q_ref in enumerate(q_refs):
        q_all[j] = q_ref[:rows, :]
        slab = q_ref[rows:, :].astype(jnp.float32)
        for head in range(hh):
            picked = jnp.sum(slab[head : head + 1] * eye, axis=1, keepdims=True)
            wb[j, head] = jnp.broadcast_to(picked, (rows_here, lanes))
        for head in range(0, hh, 2):
            at = slice(head * rows_here, (head + 2) * rows_here)
            q = q_ref[at, :].astype(jnp.float32)
            w = wb[j, head : head + 2].reshape(2 * rows_here, lanes) * scale
            qw_refs[j][:, at] = (q * w).T.astype(jnp.bfloat16)

    def dot_tile(buffer, s):
        j, s = s // tiles, s % tiles
        keys = keys_ref[pl.ds(pl.multiple_of(s * tile, tile), tile), :]
        dots[buffer] = lax.dot_general(
            q_all[j], keys, contract_last, preferred_element_type=jnp.float32
        ).reshape(hh, rows_here, tile)

    def step(buffer, s, following):
        if following is not None:
            dot_tile(1 - buffer, following)
        j, s = s // tiles, s % tiles
        columns = pl.ds(pl.multiple_of(s * tile, tile), tile)
        for t in range(0, rows_here, 8):
            total = None
            for head in range(hh):
                value = jnp.maximum(dots[buffer, head, t : t + 8, :], 0.0)
                w = wb[j, head, t : t + 8, :]
                value = value * jnp.concatenate([w] * wide_by, axis=1)
                total = value if total is None else total + value
            total = total * scale
            if is_first:
                score_ref[t : t + 8, columns] += total
            else:
                score_ref[t : t + 8, columns] = before_ref[t : t + 8, columns] + total

    if is_first:
        score_ref[...] = jnp.zeros_like(score_ref)
    in_pairs(count * tiles, dot_tile, step)
    if not is_last:
        return

    limit = row_limits(meta_ref, rows_here)
    lane = lax.broadcasted_iota(jnp.int32, (rows_here, lanes), 1)
    out = jnp.zeros((rows_here, lanes), jnp.float32)

    def piece(i, at):
        if i == 0:
            return score_ref[:, at * chunk : (at + 1) * chunk]
        return logits_ref[meta_ref[1] ^ order[at]].astype(jnp.float32)

    for i in range(2):
        peak = None
        for at, k in enumerate(order):
            allowed = piece_allowed(meta_ref, limit, k, kc, chunk)
            here = jnp.max(jnp.where(allowed, piece(i, at), masked_value), axis=1, keepdims=True)
            peak = here if peak is None else jnp.maximum(peak, here)
        total = None
        for at, k in enumerate(order):
            allowed = piece_allowed(meta_ref, limit, k, kc, chunk)
            here = jnp.where(allowed, jnp.exp(piece(i, at) - peak), 0.0)
            here = jnp.sum(here, axis=1, keepdims=True)
            total = here if total is None else total + here
        out = jnp.where(lane == 2 * i, peak, out)
        out = jnp.where(lane == 2 * i + 1, total, out)
    padded = stats_ref.shape[2]
    if padded > rows_here:
        out = jnp.concatenate([out, jnp.zeros((padded - rows_here, lanes), jnp.float32)], axis=0)
    stats_ref[0] = out.T[:stat_rows]


def score_gradient(cfg, meta_ref, stats, rw_ref, logits_ref, score_ref, cols, grad_ref):
    order, nh, rows_here, hh, depth, kc, chunk, scale = cfg
    for i in range(2):
        peak = functools.reduce(jnp.maximum, [st[2 * i : 2 * i + 1] for st in stats])
        total = functools.reduce(
            jnp.add,
            [st[2 * i + 1 : 2 * i + 2] * jnp.exp(st[2 * i : 2 * i + 1] - peak) for st in stats],
        )
        cols[2 * i : 2 * i + 1, :] = peak
        cols[2 * i + 1 : 2 * i + 2, :] = rw_ref[...] / total
    cols[4:, :] = jnp.zeros((cols.shape[0] - 4, cols.shape[1]), jnp.float32)
    st = cols[...].T[:rows_here]
    limit = row_limits(meta_ref, rows_here)
    for at, k in enumerate(order):
        logits = logits_ref[meta_ref[1] ^ k].astype(jnp.float32)
        score = score_ref[:, at * chunk : (at + 1) * chunk]
        g = jnp.exp(score - st[:, 0:1]) * st[:, 1:2] - jnp.exp(logits - st[:, 2:3]) * st[:, 3:4]
        g = jnp.where(piece_allowed(meta_ref, limit, k, kc, chunk), g, 0.0)
        grad_ref[:, at * chunk : (at + 1) * chunk] = g.astype(jnp.bfloat16)


def backward_kernel(cfg, is_first, half, meta_ref, *refs):
    order, nh, rows_here, hh, depth, kc, chunk, scale = cfg
    n = len(order)
    rows = rows_here * hh
    refs = list(refs)
    take = lambda count: [refs.pop(0) for _ in range(count)]
    q_ref, keys_ref = take(2)
    kg_in_ref = None
    (qw_ref,) = take(1)
    if is_first:
        stat_refs = take(nh)
        rw_ref, logits_ref, score_ref = take(3)
    else:
        (grad_ref,) = take(1)
        (kg_in_ref,) = take(1)
    if half == "second":
        (u_in_ref,) = take(1)
    (u_ref,) = take(1)
    if half in ("first", "second"):
        kg_refs = take(1) if half == "first" else take(n // 2)
    elif half == "all":
        (kg_ref,) = take(1)
    if is_first:
        (grad_ref,) = take(1)
    masks, u_acc = take(2)
    if half == "second":
        u_acc[...] = u_in_ref[...]
    else:
        u_acc[...] = jnp.zeros_like(u_acc)
    if half in ("first", "second"):
        (kg_acc,) = take(1)
    if is_first:
        (cols,) = take(1)
        stats = [ref[0] for ref in stat_refs]
        score_gradient(cfg, meta_ref, stats, rw_ref, logits_ref, score_ref, cols, grad_ref)
    tile = masks.shape[2]
    tiles = n * chunk // tile
    if half in ("first", "second"):
        tiles = tiles // 2
    offset = tiles if half == "second" else 0

    def tile_at(s):
        return pl.ds(pl.multiple_of((s + offset) * tile, tile), tile)

    def mask(buffer, s):
        dotted = lax.dot_general(
            q_ref[:rows, :],
            keys_ref[tile_at(s), :],
            contract_last,
            preferred_element_type=jnp.float32,
        )
        g = grad_ref[:, tile_at(s)].astype(jnp.float32)
        wide = jnp.broadcast_to(g[None], (hh, rows_here, tile)).reshape(rows, tile)
        masks[buffer] = jnp.where(dotted > 0, wide, 0.0).astype(jnp.bfloat16)

    def step(buffer, s, following):
        if following is not None:
            mask(1 - buffer, following)
        masked = masks[buffer]
        u_acc[...] += jnp.dot(
            masked, keys_ref[tile_at(s), :], preferred_element_type=jnp.float32
        )
        more = jnp.dot(qw_ref[...], masked, preferred_element_type=jnp.float32)
        if kg_in_ref is not None:
            more = kg_in_ref[:, tile_at(s)] + more
        if half == "all":
            kg_ref[:, tile_at(s)] = more
        else:
            kg_acc[:, pl.ds(pl.multiple_of(s * tile, tile), tile)] = more

    in_pairs(tiles, mask, step)
    u_ref[...] = u_acc[...].astype(u_ref.dtype)
    if half in ("first", "second"):
        for i in range(n // 2):
            value = kg_acc[:, i * chunk : (i + 1) * chunk].T
            if half == "first":
                kg_refs[0][i] = value.astype(kg_refs[0].dtype)
            else:
                kg_refs[i][...] = value


def finish_kernel(cfg, u_ref, moving_ref, q_ref, query_grad_ref, weight_grad_ref):
    order, nh, rows_here, hh, depth, kc, chunk, scale = cfg
    rows = rows_here * hh
    eye = (
        lax.broadcasted_iota(jnp.int32, (rows_here, lanes), 0)
        == lax.broadcasted_iota(jnp.int32, (rows_here, lanes), 1)
    ).astype(jnp.float32)
    lane = lax.broadcasted_iota(jnp.int32, (lanes, lanes), 1)[:rows_here]
    slab = q_ref[rows:, :].astype(jnp.float32)
    out = jnp.zeros((rows_here, lanes), jnp.float32)
    for head in range(hh):
        at = slice(head * rows_here, (head + 1) * rows_here)
        total = u_ref[at, :] + moving_ref[at, :].astype(jnp.float32)
        w = jnp.sum(slab[head : head + 1] * eye, axis=1, keepdims=True) * scale
        query_grad_ref[:, head, :] = total * w
        along = jnp.sum(total * q_ref[at, :].astype(jnp.float32), axis=1, keepdims=True)
        out = jnp.where(lane == head, along * scale, out)
    if rows_here < lanes:
        out = jnp.concatenate([out, jnp.zeros((lanes - rows_here, lanes), jnp.float32)], axis=0)
    weight_grad_ref[...] = out.T[:hh, :rows_here]


def per_device(query, weights, keys, main_logits, row_weight, offset):
    n = lax.axis_size("ctx")
    nh = lax.axis_size("head")
    c = lax.axis_index("ctx")
    h = lax.axis_index("head")
    rows_here, hh, depth = query.shape
    kc = keys.shape[0]
    chunk = kc // nh
    rows = rows_here * hh
    scale = depth ** (-0.5)
    loss_scale = float(kc * n) ** 0.5
    bf16, f32 = jnp.bfloat16, jnp.float32

    q_mine = jnp.swapaxes(query, 0, 1).reshape(rows, depth)
    slab_rows = -(-hh // 16) * 16
    w_slab = jnp.pad(weights.T, ((0, slab_rows - hh), (0, lanes - rows_here)))
    q_blocks = [jnp.concatenate([q_mine, w_slab], axis=0)]
    q_blocks.append(ring_next(q_blocks[0], "head"))

    k_mine = lax.dynamic_slice_in_dim(keys, h * chunk, chunk, 0)
    k_pieces = [None] * n
    k_pieces[0::2] = [k_mine] + [swap(k_mine, "ctx", k) for k in range(2, n, 2)]
    k_pieces[4], q_blocks[1] = lax.optimization_barrier((k_pieces[4], q_blocks[1]))
    k_pieces[1::2] = [swap(piece, "ctx", 1) for piece in k_pieces[0::2]]
    order = list(range(1, n, 2)) + list(range(0, n, 2))
    for j in range(2, nh):
        q_blocks.append(ring_next(q_blocks[-1], "head"))

    logits = lax.dynamic_slice_in_dim(main_logits, h * chunk, chunk, 1)
    logits = lax.optimization_barrier((logits, k_pieces[6]))[0]
    logits = lax.all_to_all(logits.reshape(n, rows_here, chunk), "ctx", 0, 0, tiled=True)
    logits, k_pieces[1] = lax.optimization_barrier((logits, k_pieces[1]))

    meta = jnp.concatenate([offset, jnp.stack([c, h]).astype(jnp.int32)])
    rw = lax.dynamic_slice_in_dim(row_weight, c * rows_here, rows_here, 0)[None, :]
    padded = -(-rows_here // lanes) * lanes
    rw = jnp.pad(rw * loss_scale, ((0, 0), (0, padded - rows_here)))

    cfg = (order, nh, rows_here, hh, depth, kc, chunk, scale)
    total_keys = n * chunk
    smem = pl.BlockSpec(memory_space=pltpu.SMEM)
    vmem = pl.BlockSpec(memory_space=pltpu.VMEM)
    macs = rows * total_keys * depth
    tile = 512

    def call(kernel, operands, out_shape, scratch, products, name, aliases={}):
        return pl.pallas_call(
            kernel,
            out_shape=out_shape,
            input_output_aliases=aliases,
            in_specs=[smem] + [vmem] * len(operands),
            out_specs=[vmem] * len(out_shape),
            scratch_shapes=scratch,
            compiler_params=pltpu.CompilerParams(vmem_limit_bytes=vmem_bytes),
            cost_estimate=pl.CostEstimate(
                flops=int(4 * products * macs), bytes_accessed=4 * 1024 * 1024, transcendentals=0
            ),
            name=name,
        )(meta, *operands)

    near = lambda x: pltpu.with_memory_space_constraint(x, pltpu.VMEM)

    score = keys_all = stats = None
    qw = []
    for js in (range(nh - 1), range(nh - 1, nh)):
        is_first, is_last = js[0] == 0, js[-1] == nh - 1
        operands = [q_blocks[j] for j in js]
        operands += [k_pieces[k] for k in order] if is_first else [near(keys_all), near(score)]
        operands += [logits] if is_last else []
        out_shape = [pltpu.VMEM((rows_here, total_keys), f32)]
        out_shape += [pltpu.VMEM((depth, rows), bf16)] * len(js)
        if is_first:
            out_shape += [pltpu.VMEM((total_keys, depth), bf16)]
        if is_last:
            out_shape += [jax.ShapeDtypeStruct((1, stat_rows, padded), f32)]
        scratch = [
            pltpu.VMEM((len(js), rows, depth), bf16),
            pltpu.VMEM((len(js), hh, rows_here, lanes), f32),
            pltpu.VMEM((2, hh, rows_here, tile), f32),
        ]
        kernel = functools.partial(forward_kernel, cfg, len(js), is_first, is_last)
        aliases = {} if is_first else {len(js) + 2: 0}
        outs = call(kernel, operands, out_shape, scratch, len(js), f"forward{js[0]}", aliases)
        score = outs[0]
        qw += outs[1 : 1 + len(js)]
        keys_all = outs[-1] if is_first else keys_all
        stats = outs[-1] if is_last else stats

    all_stats = [stats] + [swap(stats, "head", j) for j in range(1, nh)]

    grad = kg = moving = None
    mask_scratch = pltpu.VMEM((2, rows, tile), bf16)
    u_scratch = pltpu.VMEM((rows, depth), f32)
    u_shape = jax.ShapeDtypeStruct((rows, depth), f32)
    for j in range(1, nh):
        is_first = j == 1
        operands = [q_blocks[j], near(keys_all), near(qw[j])]
        if is_first:
            operands += all_stats + [rw, logits, near(score)]
        else:
            operands += [near(grad), near(kg)]
        out_shape = [
            jax.ShapeDtypeStruct((rows, depth), bf16) if is_first else u_shape,
            pltpu.VMEM((depth, total_keys), f32),
        ]
        scratch = [mask_scratch, u_scratch]
        if is_first:
            out_shape += [pltpu.VMEM((rows_here, total_keys), bf16)]
            scratch += [pltpu.VMEM((padded, lanes), f32)]
        kernel = functools.partial(backward_kernel, cfg, is_first, "all")
        aliases = {} if is_first else {5: 1}
        outs = call(kernel, operands, out_shape, scratch, 3, f"backward{j}", aliases)
        kg = outs[1]
        if is_first:
            grad = outs[2]
            part = outs[0]
        else:
            part = (outs[0] + moving.astype(f32)).astype(bf16)
            kg, part = lax.optimization_barrier((kg, part))
        moving = ring_next(part, "head")

    half_scratch = [mask_scratch, u_scratch, pltpu.VMEM((depth, total_keys // 2), f32)]
    operands = [q_blocks[0], near(keys_all), near(qw[0]), near(grad), near(kg)]
    u_mine, odd = call(
        functools.partial(backward_kernel, cfg, False, "first"),
        operands,
        [pltpu.VMEM((rows, depth), f32), jax.ShapeDtypeStruct((n // 2, chunk, depth), bf16)],
        half_scratch,
        1.5,
        "backward0_first",
    )
    other = swap(odd, "ctx", 1)
    u_mine, *even = call(
        functools.partial(backward_kernel, cfg, False, "second"),
        operands + [near(u_mine)],
        [u_shape] + [jax.ShapeDtypeStruct((chunk, depth), f32)] * (n // 2),
        half_scratch,
        1.5,
        "backward0_second",
    )

    even = [even[i] + other[i].astype(f32) for i in range(n // 2)]
    key_grad = even[0]
    sends = [even[i].astype(bf16) for i in range(1, n // 2)]
    u_mine, *sends = lax.optimization_barrier((u_mine, *sends))
    for i in range(1, n // 2):
        key_grad = key_grad + swap(sends[i - 1], "ctx", 2 * i).astype(f32)

    query_grad, weight_grad = pl.pallas_call(
        functools.partial(finish_kernel, cfg),
        out_shape=[
            jax.ShapeDtypeStruct((rows_here, hh, depth), f32),
            jax.ShapeDtypeStruct((hh, rows_here), f32),
        ],
        in_specs=[vmem] * 3,
        out_specs=[vmem] * 2,
        compiler_params=pltpu.CompilerParams(vmem_limit_bytes=vmem_bytes),
        cost_estimate=pl.CostEstimate(
            flops=8 * rows * depth, bytes_accessed=14 * rows * depth, transcendentals=0
        ),
        name="finish",
    )(u_mine, moving, q_blocks[0])
    return query_grad, key_grad, weight_grad.T


def solution(mesh):
    in_specs = (P("ctx", "head", None), P("ctx", "head"), P("ctx", None), P(None, "ctx"), P(), P())
    out_specs = (P("ctx", "head", None), P(("ctx", "head"), None), P("ctx", "head"))
    return jax.shard_map(
        per_device, mesh=mesh, in_specs=in_specs, out_specs=out_specs, check_vma=False
    )
```

```python
import functools

import jax
import jax.numpy as jnp
from jax import lax
from jax.experimental import pallas as pl
from jax.experimental.pallas import tpu as pltpu
from jax.sharding import PartitionSpec as P

masked_value = -1e30
lanes = 128
stat_rows = 8
vmem_bytes = 6 * 1024 * 1024
contract_last = (((1,), (1,)), ((), ()))


def swap(value, axis, distance):
    size = lax.axis_size(axis)
    return lax.ppermute(value, axis, [(i, i ^ distance) for i in range(size)])


def ring_next(value, axis):
    size = lax.axis_size(axis)
    ring = list(range(0, size, 2)) + list(range(1, size, 2))[::-1]
    return lax.ppermute(value, axis, [(ring[i], ring[(i + 1) % size]) for i in range(size)])


def in_pairs(count, first, step):
    first(0, 0)

    def body(i, _):
        step(0, 2 * i, 2 * i + 1)
        step(1, 2 * i + 1, 2 * i + 2)
        return 0

    lax.fori_loop(0, count // 2 - 1, body, 0)
    step(0, count - 2, count - 1)
    step(1, count - 1, None)


def row_limits(meta_ref, rows_here):
    row = lax.broadcasted_iota(jnp.int32, (rows_here, 1), 0)
    return meta_ref[0] + meta_ref[1] * rows_here + row


def piece_allowed(meta_ref, limit, k, kc, chunk):
    first = (meta_ref[1] ^ k) * kc + meta_ref[2] * chunk
    position = first + lax.broadcasted_iota(jnp.int32, (limit.shape[0], chunk), 1)
    return position <= limit


def forward_kernel(cfg, count, is_first, is_last, meta_ref, *refs):
    order, nh, rows_here, hh, depth, kc, chunk, scale = cfg
    n = len(order)
    rows = rows_here * hh
    refs = list(refs)
    take = lambda count: [refs.pop(0) for _ in range(count)]
    q_refs = take(count)
    if is_first:
        message_refs = take(n)
    else:
        keys_ref, before_ref, logits_ref = take(3)
    (score_ref,) = take(1)
    qw_refs = take(count)
    active_refs = [None] * is_first + take(count - is_first)
    if is_first:
        keys_ref, logits_ref = take(2)
    if is_last:
        (stats_ref,) = take(1)
    (wb,) = take(1)
    side = min(256, n * chunk)
    tile = min(4 * side, n * chunk)
    tiles = n * chunk // tile
    if is_first:
        for at, k in enumerate(order):
            keys_ref[at * chunk : (at + 1) * chunk, :] = message_refs[at][:chunk, :]
            for i in range(chunk // lanes):
                first = chunk + (chunk // lanes * (k % 2) + i) * rows_here
                column = at * chunk + i * lanes
                logits_ref[:, column : column + lanes] = message_refs[at][
                    first : first + rows_here, :
                ]

    eye = (
        lax.broadcasted_iota(jnp.int32, (rows_here, lanes), 0)
        == lax.broadcasted_iota(jnp.int32, (rows_here, lanes), 1)
    ).astype(jnp.float32)
    for j, q_ref in enumerate(q_refs):
        slab = q_ref[rows:, :].astype(jnp.float32)
        for head in range(hh):
            picked = jnp.sum(slab[head : head + 1] * eye, axis=1, keepdims=True)
            wb[j, head] = jnp.broadcast_to(picked, (rows_here, lanes))
        for head in range(0, hh, 2):
            at = slice(head * rows_here, (head + 2) * rows_here)
            q = q_ref[at, :].astype(jnp.float32)
            w = wb[j, head : head + 2].reshape(2 * rows_here, lanes) * scale
            qw_refs[j][:, at] = (q * w).T.astype(jnp.bfloat16)

    def step(j, s):
        for first in range(0, tile, side):
            columns = pl.ds(pl.multiple_of(s * tile + first, side), side)
            dots = lax.dot_general(
                q_refs[j][:rows, :],
                keys_ref[columns, :],
                contract_last,
                preferred_element_type=jnp.float32,
            )
            total = [None] * (rows_here // 16)
            for head in range(hh):
                for t in range(rows_here // 16):
                    row = head * rows_here + t * 16
                    w = wb[j, head, t * 16 : t * 16 + 16, :]
                    w = jnp.concatenate([w] * (side // lanes), axis=1)
                    active = jnp.maximum(dots[row : row + 16, :], 0.0)
                    if active_refs[j] is not None:
                        active_refs[j][row : row + 16, columns] = active.astype(jnp.bfloat16)
                    value = active * w
                    total[t] = value if head == 0 else total[t] + value
            for t, value in enumerate(total):
                at = slice(t * 16, t * 16 + 16)
                value = value * scale
                if j > 0:
                    value = score_ref[at, columns] + value
                elif not is_first:
                    value = before_ref[at, columns] + value
                score_ref[at, columns] = value
        return 0

    for j in range(count):
        lax.fori_loop(0, tiles, lambda s, _, j=j: step(j, s), 0)
    if not is_last:
        return

    limit = row_limits(meta_ref, rows_here)
    lane = lax.broadcasted_iota(jnp.int32, (rows_here, lanes), 1)
    out = jnp.zeros((rows_here, lanes), jnp.float32)

    def piece(i, at):
        if i == 0:
            return score_ref[:, at * chunk : (at + 1) * chunk]
        return logits_ref[:, at * chunk : (at + 1) * chunk].astype(jnp.float32)

    for i in range(2):
        peak = None
        for at, k in enumerate(order):
            allowed = piece_allowed(meta_ref, limit, k, kc, chunk)
            here = jnp.max(jnp.where(allowed, piece(i, at), masked_value), axis=1, keepdims=True)
            peak = here if peak is None else jnp.maximum(peak, here)
        total = None
        for at, k in enumerate(order):
            allowed = piece_allowed(meta_ref, limit, k, kc, chunk)
            here = jnp.where(allowed, jnp.exp(piece(i, at) - peak), 0.0)
            here = jnp.sum(here, axis=1, keepdims=True)
            total = here if total is None else total + here
        out = jnp.where(lane == 2 * i, peak, out)
        out = jnp.where(lane == 2 * i + 1, total, out)
    padded = stats_ref.shape[2]
    if padded > rows_here:
        out = jnp.concatenate([out, jnp.zeros((padded - rows_here, lanes), jnp.float32)], axis=0)
    stats_ref[0] = out.T[:stat_rows]


def score_gradient(cfg, meta_ref, stats, rw_ref, logits_ref, score_ref, cols, grad_ref):
    order, nh, rows_here, hh, depth, kc, chunk, scale = cfg
    for i in range(2):
        peak = functools.reduce(jnp.maximum, [st[2 * i : 2 * i + 1] for st in stats])
        total = functools.reduce(
            jnp.add,
            [st[2 * i + 1 : 2 * i + 2] * jnp.exp(st[2 * i : 2 * i + 1] - peak) for st in stats],
        )
        cols[2 * i : 2 * i + 1, :] = peak
        cols[2 * i + 1 : 2 * i + 2, :] = rw_ref[...] / total
    cols[4:, :] = jnp.zeros((cols.shape[0] - 4, cols.shape[1]), jnp.float32)
    st = cols[...].T[:rows_here]
    limit = row_limits(meta_ref, rows_here)
    for at, k in enumerate(order):
        logits = logits_ref[:, at * chunk : (at + 1) * chunk].astype(jnp.float32)
        score = score_ref[:, at * chunk : (at + 1) * chunk]
        g = jnp.exp(score - st[:, 0:1]) * st[:, 1:2] - jnp.exp(logits - st[:, 2:3]) * st[:, 3:4]
        g = jnp.where(piece_allowed(meta_ref, limit, k, kc, chunk), g, 0.0)
        grad_ref[:, at * chunk : (at + 1) * chunk] = g.astype(jnp.bfloat16)


def backward_kernel(cfg, items, has_before, meta_ref, *refs):
    order, nh, rows_here, hh, depth, kc, chunk, scale = cfg
    n = len(order)
    rows = rows_here * hh
    refs = list(refs)
    take = lambda count: [refs.pop(0) for _ in range(count)]
    is_first = items[0][0] == 1 and items[0][2] is None
    makes_u = any(item[1] for item in items)
    ranges = [item[2] for item in items if item[2] is not None]
    half = ranges[0] if ranges and ranges[0] != "all" else None
    source_refs = take(len(items))
    qw_refs = [take(1)[0] if item[2] is not None else None for item in items]
    (keys_ref,) = take(1)
    if is_first:
        stat_refs = take(nh)
        rw_ref, logits_ref, score_ref = take(3)
    else:
        (grad_ref,) = take(1)
    before_ref = take(1)[0] if has_before else None
    if makes_u:
        (u_ref,) = take(1)
    if ranges:
        kg_refs = take(n // 2 if half == "second" else 1)
    if is_first:
        (grad_ref,) = take(1)
    if half is not None:
        mask_ref, kg_acc = take(2)
    else:
        masks = take(2)
        (u_acc,) = take(1)
    if is_first:
        (cols,) = take(1)
        stats = [ref[0] for ref in stat_refs]
        score_gradient(cfg, meta_ref, stats, rw_ref, logits_ref, score_ref, cols, grad_ref)
    tile = min(512, n * chunk // 4)
    chunks = max(1, min(4, hh))
    heads = hh // chunks
    part = heads * rows_here
    side = tile // 2

    for index, (_, is_u, keys_range) in enumerate(items):
        tiles = n * chunk // tile
        if half is not None:
            tiles = tiles // 2
        offset = tiles if half == "second" else 0
        source_ref, qw_ref = source_refs[index], qw_refs[index]
        is_start = index == 0 or items[index - 1][2] is None

        def tile_at(s, first=0, size=tile, offset=offset):
            return pl.ds(pl.multiple_of((s + offset) * tile + first, size), size)

        def mask_at(buffer, s, at, first=0, size=tile):
            if half is None:
                return masks[buffer].at[at, first : first + size]
            return mask_ref.at[at, pl.ds(pl.multiple_of(s * tile + first, size), size)]

        def mask_part(buffer, s, i, source_ref=source_ref):
            at = slice(i * part, (i + 1) * part)
            if half is None:
                g = grad_ref[:, tile_at(s)]
                value = source_ref[at, tile_at(s)]
            else:
                g = grad_ref[:, tile_at(s)].astype(jnp.float32)
                value = lax.dot_general(
                    source_ref[at, :],
                    keys_ref[tile_at(s), :],
                    contract_last,
                    preferred_element_type=jnp.float32,
                )
            wide = jnp.broadcast_to(g[None], (heads, rows_here, tile)).reshape(part, tile)
            value = jnp.where(value > 0, wide, jnp.zeros_like(wide))
            mask_at(buffer, s, at)[...] = value.astype(jnp.bfloat16)

        def mask(buffer, s):
            for i in range(chunks):
                mask_part(buffer, s, i)

        def step(buffer, s, following):
            for i in range(chunks):
                if following is not None:
                    mask_part(1 - buffer, following, i)
                if is_u:
                    at = slice(i * part, (i + 1) * part)
                    u_acc[at, :] += jnp.dot(
                        mask_at(buffer, s, at)[...],
                        keys_ref[tile_at(s), :],
                        preferred_element_type=jnp.float32,
                    )
                if keys_range is None or i % (chunks // 2) != chunks // 2 - 1:
                    continue
                first = i // (chunks // 2) * side
                more = jnp.dot(
                    qw_ref[...],
                    mask_at(buffer, s, slice(0, rows), first, side)[...],
                    preferred_element_type=jnp.float32,
                )
                here = tile_at(s, first, side)
                if not is_start:
                    more = kg_refs[0][:, here] + more
                elif before_ref is not None:
                    more = before_ref[:, here] + more
                if half is None:
                    kg_refs[0][:, here] = more
                else:
                    kg_acc[:, pl.ds(pl.multiple_of(s * tile + first, side), side)] = more

        if is_u:
            u_acc[...] = jnp.zeros_like(u_acc)
        in_pairs(tiles, mask, step)
        if is_u:
            u_ref[...] = u_acc[...].astype(u_ref.dtype)

    if half is not None:
        for i in range(n // 2):
            value = kg_acc[:, i * chunk : (i + 1) * chunk].T
            if half == "first":
                kg_refs[0][i] = value.astype(kg_refs[0].dtype)
            else:
                kg_refs[i][...] = value


def query_kernel(cfg, mask_refs, keys_ref, u_ref, u_acc):
    count = mask_refs[0].shape[1]
    tile = min(512, count)
    u_acc[...] = jnp.zeros_like(u_acc)
    for half, mask_ref in enumerate(mask_refs):

        def step(s, _, half=half, mask_ref=mask_ref):
            at = pl.multiple_of(s * tile, tile)
            u_acc[...] += jnp.dot(
                mask_ref[:, pl.ds(at, tile)],
                keys_ref[pl.ds(half * count + at, tile), :],
                preferred_element_type=jnp.float32,
            )
            return 0

        lax.fori_loop(0, count // tile, step, 0)
    u_ref[...] = u_acc[...]


def prepare_kernel(cfg, meta_ref, query_ref, weights_ref, rw_ref, keys_ref, logits_ref, *refs):
    order, nh, rows_here, hh, depth, kc, chunk, scale = cfg
    sends = len(order) // 2
    rows = rows_here * hh
    parts = chunk // lanes
    message_ref, rw_out_ref, key_refs = refs[0], refs[1], refs[2 : 2 + sends]
    wide, sems = refs[-2], refs[-1]
    share = pl.multiple_of(meta_ref[2] * chunk, chunk)
    copies = []

    def copy(source, target):
        copies.append(pltpu.make_async_copy(source, target, sems.at[len(copies)]))
        copies[-1].start()

    for i in reversed(range(sends)):
        copy(keys_ref.at[pl.ds(share, chunk), :], key_refs[i].at[:chunk, :])
        for core in range(2):
            row = pl.multiple_of((meta_ref[1] ^ (2 * i) ^ core) * rows_here, rows_here)
            for part in range(parts):
                first = chunk + (parts * core + part) * rows_here
                copy(
                    logits_ref.at[pl.ds(row, rows_here), pl.ds(share + part * lanes, lanes)],
                    key_refs[i].at[first : first + rows_here, :],
                )
    every = jnp.broadcast_to(rw_ref[...], (8, rw_ref.shape[1]))
    shift = every.shape[1] - meta_ref[1] * rows_here
    here = pltpu.roll(every, shift, 1)[:1, : rw_out_ref.shape[1]]
    rw_out_ref[...] = here * float(kc * len(order)) ** 0.5
    wide[...] = query_ref[...].astype(jnp.float32)
    for head in range(hh):
        at = slice(head * rows_here, (head + 1) * rows_here)
        message_ref[at, :] = wide[:, head, :].astype(jnp.bfloat16)
    message_ref[rows:, :] = jnp.zeros((message_ref.shape[0] - rows, lanes), jnp.bfloat16)
    message_ref[rows : rows + hh, :rows_here] = weights_ref[...]
    for item in copies:
        item.wait()


def add_kernel(u_ref, moving_ref, out_ref):
    out_ref[...] = (u_ref[...] + moving_ref[...].astype(jnp.float32)).astype(out_ref.dtype)


def finish_kernel(cfg, u_ref, moving_ref, q_ref, query_grad_ref, weight_grad_ref):
    order, nh, rows_here, hh, depth, kc, chunk, scale = cfg
    rows = rows_here * hh
    eye = (
        lax.broadcasted_iota(jnp.int32, (rows_here, lanes), 0)
        == lax.broadcasted_iota(jnp.int32, (rows_here, lanes), 1)
    ).astype(jnp.float32)
    lane = lax.broadcasted_iota(jnp.int32, (lanes, lanes), 1)[:rows_here]
    slab = q_ref[rows:, :].astype(jnp.float32)
    out = jnp.zeros((rows_here, lanes), jnp.float32)
    for head in range(hh):
        at = slice(head * rows_here, (head + 1) * rows_here)
        total = u_ref[at, :] + moving_ref[at, :].astype(jnp.float32)
        w = jnp.sum(slab[head : head + 1] * eye, axis=1, keepdims=True) * scale
        query_grad_ref[:, head, :] = total * w
        along = jnp.sum(total * q_ref[at, :].astype(jnp.float32), axis=1, keepdims=True)
        out = jnp.where(lane == head, along * scale, out)
    if rows_here < lanes:
        out = jnp.concatenate([out, jnp.zeros((lanes - rows_here, lanes), jnp.float32)], axis=0)
    weight_grad_ref[...] = out.T[:hh, :rows_here]


def per_device(query, weights, keys, main_logits, row_weight, offset):
    n = lax.axis_size("ctx")
    nh = lax.axis_size("head")
    c = lax.axis_index("ctx")
    h = lax.axis_index("head")
    rows_here, hh, depth = query.shape
    kc = keys.shape[0]
    chunk = kc // nh
    rows = rows_here * hh
    scale = depth ** (-0.5)
    bf16, f32 = jnp.bfloat16, jnp.float32

    order = list(range(1, n, 2)) + list(range(0, n, 2))
    cfg = (order, nh, rows_here, hh, depth, kc, chunk, scale)
    smem = pl.BlockSpec(memory_space=pltpu.SMEM)
    vmem = pl.BlockSpec(memory_space=pltpu.VMEM)
    padded = -(-rows_here // lanes) * lanes
    meta = jnp.concatenate([offset, jnp.stack([c, h]).astype(jnp.int32)])

    far = lambda x: pltpu.with_memory_space_constraint(x, pltpu.HBM)

    slab_rows = -(-hh // 16) * 16
    parts = chunk // lanes
    message, rw, *key_messages = pl.pallas_call(
        functools.partial(prepare_kernel, cfg),
        out_shape=[
            jax.ShapeDtypeStruct((rows + slab_rows, depth), bf16),
            jax.ShapeDtypeStruct((1, padded), f32),
        ]
        + [jax.ShapeDtypeStruct((chunk + 2 * parts * rows_here, depth), bf16)] * (n // 2),
        in_specs=[smem, vmem, vmem, vmem] + [pl.BlockSpec(memory_space=pltpu.HBM)] * 2,
        out_specs=[vmem] * (2 + n // 2),
        scratch_shapes=[
            pltpu.VMEM((rows_here, hh, depth), f32),
            pltpu.SemaphoreType.DMA((n // 2 * (1 + 2 * parts),)),
        ],
        compiler_params=pltpu.CompilerParams(vmem_limit_bytes=vmem_bytes),
        cost_estimate=pl.CostEstimate(
            flops=rows * depth, bytes_accessed=4 * 1024 * 1024, transcendentals=0
        ),
        name="prepare",
    )(meta, far(query), far(weights.T), row_weight[None, :], far(keys), far(main_logits))
    q_blocks = [message, ring_next(message, "head")]

    k_pieces = [None] * n
    k_pieces[0::2] = [key_messages[0]] + [
        swap(key_messages[k // 2], "ctx", k) for k in range(2, n, 2)
    ]
    k_pieces[4], q_blocks[1] = lax.optimization_barrier((k_pieces[4], q_blocks[1]))
    k_pieces[1::2] = [swap(piece, "ctx", 1) for piece in k_pieces[0::2]]
    for j in range(2, nh):
        q_blocks.append(ring_next(q_blocks[-1], "head"))

    total_keys = n * chunk
    macs = rows * total_keys * depth
    tile = 512

    def call(kernel, operands, out_shape, scratch, products, name, aliases={}):
        return pl.pallas_call(
            kernel,
            out_shape=out_shape,
            input_output_aliases=aliases,
            in_specs=[smem] + [vmem] * len(operands),
            out_specs=[vmem] * len(out_shape),
            scratch_shapes=scratch,
            compiler_params=pltpu.CompilerParams(vmem_limit_bytes=vmem_bytes),
            cost_estimate=pl.CostEstimate(
                flops=int(4 * products * macs), bytes_accessed=4 * 1024 * 1024, transcendentals=0
            ),
            name=name,
        )(meta, *operands)

    near = lambda x: pltpu.with_memory_space_constraint(x, pltpu.VMEM)

    score = keys_all = stats = None
    qw, active = [], []
    for js in (range(nh - 1), range(nh - 1, nh)):
        is_first, is_last = js[0] == 0, js[-1] == nh - 1
        operands = [q_blocks[j] for j in js]
        if is_first:
            operands += [k_pieces[k] for k in order]
        else:
            operands += [near(keys_all), near(score), near(logits)]
        out_shape = [pltpu.VMEM((rows_here, total_keys), f32)]
        out_shape += [pltpu.VMEM((depth, rows), bf16)] * len(js)
        kept = len(js) - is_first
        out_shape += [pltpu.VMEM((rows, total_keys), bf16)] * kept
        if is_first:
            out_shape += [pltpu.VMEM((total_keys, depth), bf16)]
            out_shape += [pltpu.VMEM((rows_here, total_keys), bf16)]
        if is_last:
            out_shape += [jax.ShapeDtypeStruct((1, stat_rows, padded), f32)]
        scratch = [
            pltpu.VMEM((len(js), hh, rows_here, lanes), f32),
        ]
        kernel = functools.partial(forward_kernel, cfg, len(js), is_first, is_last)
        aliases = {} if is_first else {len(js) + 2: 0}
        outs = call(kernel, operands, out_shape, scratch, len(js), f"forward{js[0]}", aliases)
        score = outs[0]
        qw += outs[1 : 1 + len(js)]
        active += [None] * is_first + list(outs[1 + len(js) : 1 + len(js) + kept])
        if is_first:
            keys_all, logits = outs[-2:]
        stats = outs[-1] if is_last else stats

    all_stats = [stats] + [swap(stats, "head", j) for j in range(1, nh)]

    grad = kg = None

    def backward(items, name):
        nonlocal grad, kg
        is_first = grad is None
        ranges = [item[2] for item in items if item[2] is not None]
        makes_u = any(item[1] for item in items)
        has_before = bool(ranges) and kg is not None
        halved = ranges != [] and ranges[0] != "all"
        operands = [q_blocks[0] if halved else near(active[item[0]]) for item in items]
        operands += [near(qw[item[0]]) for item in items if item[2] is not None]
        operands += [near(keys_all)]
        operands += all_stats + [rw, near(logits), near(score)] if is_first else [near(grad)]
        aliases = {}
        out_shape = [jax.ShapeDtypeStruct((rows, depth), bf16 if is_first else f32)]
        out_shape = out_shape if makes_u else []
        scratch = [pltpu.VMEM((rows, tile), bf16)] * 2 + [pltpu.VMEM((rows, depth), f32)]
        if not halved:
            if ranges:
                if has_before:
                    aliases = {len(operands) + 1: len(out_shape)}
                out_shape += [pltpu.VMEM((depth, total_keys), f32)]
        else:
            if ranges[0] == "first":
                out_shape += [jax.ShapeDtypeStruct((n // 2, chunk, depth), bf16)]
            else:
                out_shape += [jax.ShapeDtypeStruct((chunk, depth), f32)] * (n // 2)
            out_shape += [pltpu.VMEM((rows, total_keys // 2), bf16)]
            scratch = [pltpu.VMEM((depth, total_keys // 2), f32)]
        if has_before:
            operands += [near(kg)]
        if is_first:
            out_shape += [pltpu.VMEM((rows_here, total_keys), bf16)]
            scratch += [pltpu.VMEM((padded, lanes), f32)]
        kernel = functools.partial(backward_kernel, cfg, items, has_before)
        products = 1 if halved else makes_u + len(ranges)
        outs = call(kernel, operands, out_shape, scratch, products, name, aliases)
        if is_first:
            grad = outs[-1]
        if ranges and ranges[0] == "all":
            kg = outs[1 if makes_u else 0]
        return outs

    part = backward([(1, True, None)], "backward_1")[0]
    moving = ring_next(part, "head")
    for j in range(2, nh):
        items = [(j - 1, False, "all"), (j, True, "all" if j == nh - 1 else None)]
        part = backward(items, f"backward_{j}")[0]
        part = pl.pallas_call(
            add_kernel,
            out_shape=jax.ShapeDtypeStruct((rows, depth), bf16),
            in_specs=[vmem] * 2,
            out_specs=vmem,
            compiler_params=pltpu.CompilerParams(vmem_limit_bytes=vmem_bytes),
            cost_estimate=pl.CostEstimate(
                flops=rows * depth, bytes_accessed=8 * rows * depth, transcendentals=0
            ),
            name=f"add_{j}",
        )(part, moving)
        kg, part = lax.optimization_barrier((kg, part))
        moving = ring_next(part, "head")

    odd, mask_first = backward([(0, False, "first")], "backward_0_first")
    other = swap(odd, "ctx", 1)
    *even, mask_second = backward([(0, False, "second")], "backward_0_second")
    even = [even[i] + other[i].astype(f32) for i in range(n // 2)]
    key_grad = even[0]
    sends = [even[i].astype(bf16) for i in range(1, n // 2)]
    keys_all, *sends = lax.optimization_barrier((keys_all, *sends))
    for i in range(1, n // 2):
        key_grad = key_grad + swap(sends[i - 1], "ctx", 2 * i).astype(f32)
    (u_mine,) = call(
        lambda meta_ref, *refs: query_kernel(cfg, refs[:2], *refs[2:]),
        [near(mask_first), near(mask_second), near(keys_all)],
        [jax.ShapeDtypeStruct((rows, depth), f32)],
        [pltpu.VMEM((rows, depth), f32)],
        1,
        "backward_0",
    )

    query_grad, weight_grad = pl.pallas_call(
        functools.partial(finish_kernel, cfg),
        out_shape=[
            jax.ShapeDtypeStruct((rows_here, hh, depth), f32),
            jax.ShapeDtypeStruct((hh, rows_here), f32),
        ],
        in_specs=[vmem] * 3,
        out_specs=[vmem] * 2,
        compiler_params=pltpu.CompilerParams(vmem_limit_bytes=vmem_bytes),
        cost_estimate=pl.CostEstimate(
            flops=8 * rows * depth, bytes_accessed=14 * rows * depth, transcendentals=0
        ),
        name="finish",
    )(u_mine, moving, q_blocks[0])
    return query_grad, key_grad, weight_grad.T


def solution(mesh):
    in_specs = (P("ctx", "head", None), P("ctx", "head"), P("ctx", None), P(None, "ctx"), P(), P())
    out_specs = (P("ctx", "head", None), P(("ctx", "head"), None), P("ctx", "head"))
    return jax.shard_map(
        per_device, mesh=mesh, in_specs=in_specs, out_specs=out_specs, check_vma=False
    )
```

```python
import functools

import jax
import jax.numpy as jnp
from jax import lax
from jax.experimental import pallas as pl
from jax.experimental.pallas import tpu as pltpu
from jax.sharding import PartitionSpec as P

masked_value = -1e30
lanes = 128
stat_rows = 8
vmem_bytes = 6 * 1024 * 1024
contract_last = (((1,), (1,)), ((), ()))


def swap(value, axis, distance):
    size = lax.axis_size(axis)
    return lax.ppermute(value, axis, [(i, i ^ distance) for i in range(size)])


def ring_next(value, axis):
    size = lax.axis_size(axis)
    ring = list(range(0, size, 2)) + list(range(1, size, 2))[::-1]
    return lax.ppermute(value, axis, [(ring[i], ring[(i + 1) % size]) for i in range(size)])


def in_pairs(count, first, step):
    first(0, 0)

    def body(i, _):
        step(0, 2 * i, 2 * i + 1)
        step(1, 2 * i + 1, 2 * i + 2)
        return 0

    lax.fori_loop(0, count // 2 - 1, body, 0)
    step(0, count - 2, count - 1)
    step(1, count - 1, None)


def row_limits(meta_ref, rows_here):
    row = lax.broadcasted_iota(jnp.int32, (rows_here, 1), 0)
    return meta_ref[0] + meta_ref[1] * rows_here + row


def piece_allowed(meta_ref, limit, k, kc, chunk):
    first = (meta_ref[1] ^ k) * kc + meta_ref[2] * chunk
    position = first + lax.broadcasted_iota(jnp.int32, (limit.shape[0], chunk), 1)
    return position <= limit


def forward_kernel(cfg, count, is_first, is_last, meta_ref, *refs):
    order, nh, rows_here, hh, depth, kc, chunk, scale = cfg
    n = len(order)
    rows = rows_here * hh
    refs = list(refs)
    take = lambda count: [refs.pop(0) for _ in range(count)]
    q_refs = take(count)
    if is_first:
        message_refs = take(n)
    else:
        keys_t_ref, before_ref, logits_ref = take(3)
    (score_ref,) = take(1)
    qw_refs = take(count)
    active_refs = [None] * is_first + take(count - is_first)
    if is_first:
        keys_t_ref, logits_ref = take(2)
    if is_last:
        (stats_ref,) = take(1)
    (wb,) = take(1)
    side = min(256, n * chunk)
    tile = min(4 * side, n * chunk)
    tiles = n * chunk // tile
    if is_first:
        for at, k in enumerate(order):
            keys = message_refs[at][:chunk, :].astype(jnp.float32)
            keys_t_ref[:, at * chunk : (at + 1) * chunk] = keys.T.astype(jnp.bfloat16)
            for i in range(chunk // lanes):
                first = chunk + (chunk // lanes * (k % 2) + i) * rows_here
                column = at * chunk + i * lanes
                logits_ref[:, column : column + lanes] = message_refs[at][
                    first : first + rows_here, :
                ]

    eye = (
        lax.broadcasted_iota(jnp.int32, (rows_here, lanes), 0)
        == lax.broadcasted_iota(jnp.int32, (rows_here, lanes), 1)
    ).astype(jnp.float32)
    for j, q_ref in enumerate(q_refs):
        slab = q_ref[rows:, :].astype(jnp.float32)
        for head in range(hh):
            picked = jnp.sum(slab[head : head + 1] * eye, axis=1, keepdims=True)
            wb[j, head] = jnp.broadcast_to(picked, (rows_here, lanes))
        for head in range(0, hh, 2):
            at = slice(head * rows_here, (head + 2) * rows_here)
            q = q_ref[at, :].astype(jnp.float32)
            w = wb[j, head : head + 2].reshape(2 * rows_here, lanes) * scale
            qw_refs[j][:, at] = (q * w).T.astype(jnp.bfloat16)

    def step(j, s):
        for first in range(0, tile, side):
            columns = pl.ds(pl.multiple_of(s * tile + first, side), side)
            dots = jnp.dot(
                q_refs[j][:rows, :], keys_t_ref[:, columns], preferred_element_type=jnp.float32
            )
            total = [None] * (rows_here // 16)
            for head in range(hh):
                for t in range(rows_here // 16):
                    row = head * rows_here + t * 16
                    w = wb[j, head, t * 16 : t * 16 + 16, :]
                    w = jnp.concatenate([w] * (side // lanes), axis=1)
                    active = jnp.maximum(dots[row : row + 16, :], 0.0)
                    if active_refs[j] is not None:
                        active_refs[j][row : row + 16, columns] = active.astype(jnp.bfloat16)
                    value = active * w
                    total[t] = value if head == 0 else total[t] + value
            for t, value in enumerate(total):
                at = slice(t * 16, t * 16 + 16)
                value = value * scale
                if j > 0:
                    value = score_ref[at, columns] + value
                elif not is_first:
                    value = before_ref[at, columns] + value
                score_ref[at, columns] = value
        return 0

    for j in range(count):
        lax.fori_loop(0, tiles, lambda s, _, j=j: step(j, s), 0)
    if not is_last:
        return

    limit = row_limits(meta_ref, rows_here)
    lane = lax.broadcasted_iota(jnp.int32, (rows_here, lanes), 1)
    out = jnp.zeros((rows_here, lanes), jnp.float32)

    def piece(i, at):
        if i == 0:
            return score_ref[:, at * chunk : (at + 1) * chunk]
        return logits_ref[:, at * chunk : (at + 1) * chunk].astype(jnp.float32)

    for i in range(2):
        peak = None
        for at, k in enumerate(order):
            allowed = piece_allowed(meta_ref, limit, k, kc, chunk)
            here = jnp.max(jnp.where(allowed, piece(i, at), masked_value), axis=1, keepdims=True)
            peak = here if peak is None else jnp.maximum(peak, here)
        total = None
        for at, k in enumerate(order):
            allowed = piece_allowed(meta_ref, limit, k, kc, chunk)
            here = jnp.where(allowed, jnp.exp(piece(i, at) - peak), 0.0)
            here = jnp.sum(here, axis=1, keepdims=True)
            total = here if total is None else total + here
        out = jnp.where(lane == 2 * i, peak, out)
        out = jnp.where(lane == 2 * i + 1, total, out)
    padded = stats_ref.shape[2]
    if padded > rows_here:
        out = jnp.concatenate([out, jnp.zeros((padded - rows_here, lanes), jnp.float32)], axis=0)
    stats_ref[0] = out.T[:stat_rows]


def score_gradient(cfg, meta_ref, stats, rw_ref, logits_ref, score_ref, cols, grad_ref):
    order, nh, rows_here, hh, depth, kc, chunk, scale = cfg
    for i in range(2):
        peak = functools.reduce(jnp.maximum, [st[2 * i : 2 * i + 1] for st in stats])
        total = functools.reduce(
            jnp.add,
            [st[2 * i + 1 : 2 * i + 2] * jnp.exp(st[2 * i : 2 * i + 1] - peak) for st in stats],
        )
        cols[2 * i : 2 * i + 1, :] = peak
        cols[2 * i + 1 : 2 * i + 2, :] = rw_ref[...] / total
    cols[4:, :] = jnp.zeros((cols.shape[0] - 4, cols.shape[1]), jnp.float32)
    st = cols[...].T[:rows_here]
    limit = row_limits(meta_ref, rows_here)
    for at, k in enumerate(order):
        logits = logits_ref[:, at * chunk : (at + 1) * chunk].astype(jnp.float32)
        score = score_ref[:, at * chunk : (at + 1) * chunk]
        g = jnp.exp(score - st[:, 0:1]) * st[:, 1:2] - jnp.exp(logits - st[:, 2:3]) * st[:, 3:4]
        g = jnp.where(piece_allowed(meta_ref, limit, k, kc, chunk), g, 0.0)
        grad_ref[:, at * chunk : (at + 1) * chunk] = g.astype(jnp.bfloat16)


def backward_kernel(cfg, items, has_before, meta_ref, *refs):
    order, nh, rows_here, hh, depth, kc, chunk, scale = cfg
    n = len(order)
    rows = rows_here * hh
    refs = list(refs)
    take = lambda count: [refs.pop(0) for _ in range(count)]
    is_first = items[0][0] == 1 and items[0][2] is None
    makes_u = any(item[1] for item in items)
    ranges = [item[2] for item in items if item[2] is not None]
    half = ranges[0] if ranges and ranges[0] != "all" else None
    source_refs = take(len(items))
    qw_refs = [take(1)[0] if item[2] is not None else None for item in items]
    (keys_t_ref,) = take(1)
    if is_first:
        stat_refs = take(nh)
        rw_ref, logits_ref, score_ref = take(3)
    else:
        (grad_ref,) = take(1)
    before_ref = take(1)[0] if has_before else None
    if makes_u:
        (u_ref,) = take(1)
    if ranges:
        kg_refs = take(n // 2 if half == "second" else 1)
    if is_first:
        (grad_ref,) = take(1)
    if half is not None:
        mask_ref, kg_acc = take(2)
    else:
        masks = take(2)
        (u_acc,) = take(1)
    if is_first:
        (cols,) = take(1)
        stats = [ref[0] for ref in stat_refs]
        score_gradient(cfg, meta_ref, stats, rw_ref, logits_ref, score_ref, cols, grad_ref)
    tile = min(512, n * chunk // 4)
    chunks = max(1, min(4, hh))
    heads = hh // chunks
    part = heads * rows_here
    side = tile // 2

    for index, (_, is_u, keys_range) in enumerate(items):
        tiles = n * chunk // tile
        if half is not None:
            tiles = tiles // 2
        offset = tiles if half == "second" else 0
        source_ref, qw_ref = source_refs[index], qw_refs[index]
        is_start = index == 0 or items[index - 1][2] is None

        def tile_at(s, first=0, size=tile, offset=offset):
            return pl.ds(pl.multiple_of((s + offset) * tile + first, size), size)

        def mask_at(buffer, s, at, first=0, size=tile):
            if half is None:
                return masks[buffer].at[at, first : first + size]
            return mask_ref.at[at, pl.ds(pl.multiple_of(s * tile + first, size), size)]

        def mask_part(buffer, s, i, source_ref=source_ref):
            at = slice(i * part, (i + 1) * part)
            if half is None:
                g = grad_ref[:, tile_at(s)]
                value = source_ref[at, tile_at(s)]
            else:
                g = grad_ref[:, tile_at(s)].astype(jnp.float32)
                value = jnp.dot(
                    source_ref[at, :], keys_t_ref[:, tile_at(s)], preferred_element_type=jnp.float32
                )
            wide = jnp.broadcast_to(g[None], (heads, rows_here, tile)).reshape(part, tile)
            value = jnp.where(value > 0, wide, jnp.zeros_like(wide))
            mask_at(buffer, s, at)[...] = value.astype(jnp.bfloat16)

        def mask(buffer, s):
            for i in range(chunks):
                mask_part(buffer, s, i)

        def step(buffer, s, following):
            for i in range(chunks):
                if following is not None:
                    mask_part(1 - buffer, following, i)
                if is_u:
                    at = slice(i * part, (i + 1) * part)
                    u_acc[:, at] += lax.dot_general(
                        keys_t_ref[:, tile_at(s)],
                        mask_at(buffer, s, at)[...],
                        contract_last,
                        preferred_element_type=jnp.float32,
                    )
                if keys_range is None or i % (chunks // 2) != chunks // 2 - 1:
                    continue
                first = i // (chunks // 2) * side
                more = jnp.dot(
                    qw_ref[...],
                    mask_at(buffer, s, slice(0, rows), first, side)[...],
                    preferred_element_type=jnp.float32,
                )
                here = tile_at(s, first, side)
                if not is_start:
                    more = kg_refs[0][:, here] + more
                elif before_ref is not None:
                    more = before_ref[:, here] + more
                if half is None:
                    kg_refs[0][:, here] = more
                else:
                    kg_acc[:, pl.ds(pl.multiple_of(s * tile + first, side), side)] = more

        if is_u:
            u_acc[...] = jnp.zeros_like(u_acc)
        in_pairs(tiles, mask, step)
        if is_u:
            u_ref[...] = u_acc[...].T.astype(u_ref.dtype)

    if half is not None:
        for i in range(n // 2):
            value = kg_acc[:, i * chunk : (i + 1) * chunk].T
            if half == "first":
                kg_refs[0][i] = value.astype(kg_refs[0].dtype)
            else:
                kg_refs[i][...] = value


def query_kernel(cfg, mask_refs, keys_t_ref, u_ref, u_acc):
    count = mask_refs[0].shape[1]
    tile = min(512, count)
    u_acc[...] = jnp.zeros_like(u_acc)
    for half, mask_ref in enumerate(mask_refs):

        def step(s, _, half=half, mask_ref=mask_ref):
            at = pl.multiple_of(s * tile, tile)
            u_acc[...] += lax.dot_general(
                keys_t_ref[:, pl.ds(pl.multiple_of(half * count + at, tile), tile)],
                mask_ref[:, pl.ds(at, tile)],
                contract_last,
                preferred_element_type=jnp.float32,
            )
            return 0

        lax.fori_loop(0, count // tile, step, 0)
    u_ref[...] = u_acc[...].T


def prepare_kernel(cfg, meta_ref, query_ref, weights_ref, rw_ref, keys_ref, logits_ref, *refs):
    order, nh, rows_here, hh, depth, kc, chunk, scale = cfg
    sends = len(order) // 2
    rows = rows_here * hh
    parts = chunk // lanes
    message_ref, rw_out_ref, key_refs = refs[0], refs[1], refs[2 : 2 + sends]
    wide, sems = refs[-2], refs[-1]
    share = pl.multiple_of(meta_ref[2] * chunk, chunk)
    copies = []

    def copy(source, target):
        copies.append(pltpu.make_async_copy(source, target, sems.at[len(copies)]))
        copies[-1].start()

    for i in reversed(range(sends)):
        copy(keys_ref.at[pl.ds(share, chunk), :], key_refs[i].at[:chunk, :])
        for core in range(2):
            row = pl.multiple_of((meta_ref[1] ^ (2 * i) ^ core) * rows_here, rows_here)
            for part in range(parts):
                first = chunk + (parts * core + part) * rows_here
                copy(
                    logits_ref.at[pl.ds(row, rows_here), pl.ds(share + part * lanes, lanes)],
                    key_refs[i].at[first : first + rows_here, :],
                )
    every = jnp.broadcast_to(rw_ref[...], (8, rw_ref.shape[1]))
    shift = every.shape[1] - meta_ref[1] * rows_here
    here = pltpu.roll(every, shift, 1)[:1, : rw_out_ref.shape[1]]
    rw_out_ref[...] = here * float(kc * len(order)) ** 0.5
    wide[...] = query_ref[...].astype(jnp.float32)
    for head in range(hh):
        at = slice(head * rows_here, (head + 1) * rows_here)
        message_ref[at, :] = wide[:, head, :].astype(jnp.bfloat16)
    message_ref[rows:, :] = jnp.zeros((message_ref.shape[0] - rows, lanes), jnp.bfloat16)
    message_ref[rows : rows + hh, :rows_here] = weights_ref[...]
    for item in copies:
        item.wait()


def add_kernel(u_ref, moving_ref, out_ref):
    out_ref[...] = (u_ref[...] + moving_ref[...].astype(jnp.float32)).astype(out_ref.dtype)


def finish_kernel(cfg, u_ref, moving_ref, q_ref, query_grad_ref, weight_grad_ref):
    order, nh, rows_here, hh, depth, kc, chunk, scale = cfg
    rows = rows_here * hh
    eye = (
        lax.broadcasted_iota(jnp.int32, (rows_here, lanes), 0)
        == lax.broadcasted_iota(jnp.int32, (rows_here, lanes), 1)
    ).astype(jnp.float32)
    lane = lax.broadcasted_iota(jnp.int32, (lanes, lanes), 1)[:rows_here]
    slab = q_ref[rows:, :].astype(jnp.float32)
    out = jnp.zeros((rows_here, lanes), jnp.float32)
    for head in range(hh):
        at = slice(head * rows_here, (head + 1) * rows_here)
        total = u_ref[at, :] + moving_ref[at, :].astype(jnp.float32)
        w = jnp.sum(slab[head : head + 1] * eye, axis=1, keepdims=True) * scale
        query_grad_ref[:, head, :] = total * w
        along = jnp.sum(total * q_ref[at, :].astype(jnp.float32), axis=1, keepdims=True)
        out = jnp.where(lane == head, along * scale, out)
    if rows_here < lanes:
        out = jnp.concatenate([out, jnp.zeros((lanes - rows_here, lanes), jnp.float32)], axis=0)
    weight_grad_ref[...] = out.T[:hh, :rows_here]


def per_device(query, weights, keys, main_logits, row_weight, offset):
    n = lax.axis_size("ctx")
    nh = lax.axis_size("head")
    c = lax.axis_index("ctx")
    h = lax.axis_index("head")
    rows_here, hh, depth = query.shape
    kc = keys.shape[0]
    chunk = kc // nh
    rows = rows_here * hh
    scale = depth ** (-0.5)
    bf16, f32 = jnp.bfloat16, jnp.float32

    order = list(range(1, n, 2)) + list(range(0, n, 2))
    cfg = (order, nh, rows_here, hh, depth, kc, chunk, scale)
    smem = pl.BlockSpec(memory_space=pltpu.SMEM)
    vmem = pl.BlockSpec(memory_space=pltpu.VMEM)
    padded = -(-rows_here // lanes) * lanes
    meta = jnp.concatenate([offset, jnp.stack([c, h]).astype(jnp.int32)])

    far = lambda x: pltpu.with_memory_space_constraint(x, pltpu.HBM)

    slab_rows = -(-hh // 16) * 16
    parts = chunk // lanes
    message, rw, *key_messages = pl.pallas_call(
        functools.partial(prepare_kernel, cfg),
        out_shape=[
            jax.ShapeDtypeStruct((rows + slab_rows, depth), bf16),
            jax.ShapeDtypeStruct((1, padded), f32),
        ]
        + [jax.ShapeDtypeStruct((chunk + 2 * parts * rows_here, depth), bf16)] * (n // 2),
        in_specs=[smem, vmem, vmem, vmem] + [pl.BlockSpec(memory_space=pltpu.HBM)] * 2,
        out_specs=[vmem] * (2 + n // 2),
        scratch_shapes=[
            pltpu.VMEM((rows_here, hh, depth), f32),
            pltpu.SemaphoreType.DMA((n // 2 * (1 + 2 * parts),)),
        ],
        compiler_params=pltpu.CompilerParams(vmem_limit_bytes=vmem_bytes),
        cost_estimate=pl.CostEstimate(
            flops=rows * depth, bytes_accessed=4 * 1024 * 1024, transcendentals=0
        ),
        name="prepare",
    )(meta, far(query), far(weights.T), far(row_weight[None, :]), far(keys), far(main_logits))
    q_blocks = [message, ring_next(message, "head")]

    k_pieces = [None] * n
    k_pieces[0::2] = [key_messages[0]] + [
        swap(key_messages[k // 2], "ctx", k) for k in range(2, n, 2)
    ]
    k_pieces[4], q_blocks[1] = lax.optimization_barrier((k_pieces[4], q_blocks[1]))
    k_pieces[1::2] = [swap(piece, "ctx", 1) for piece in k_pieces[0::2]]
    for j in range(2, nh):
        q_blocks.append(ring_next(q_blocks[-1], "head"))

    total_keys = n * chunk
    macs = rows * total_keys * depth
    tile = 512

    def call(kernel, operands, out_shape, scratch, products, name, aliases={}):
        return pl.pallas_call(
            kernel,
            out_shape=out_shape,
            input_output_aliases=aliases,
            in_specs=[smem] + [vmem] * len(operands),
            out_specs=[vmem] * len(out_shape),
            scratch_shapes=scratch,
            compiler_params=pltpu.CompilerParams(vmem_limit_bytes=vmem_bytes),
            cost_estimate=pl.CostEstimate(
                flops=int(4 * products * macs), bytes_accessed=4 * 1024 * 1024, transcendentals=0
            ),
            name=name,
        )(meta, *operands)

    near = lambda x: pltpu.with_memory_space_constraint(x, pltpu.VMEM)

    score = keys_t = stats = None
    qw, active = [], []
    for js in (range(nh - 1), range(nh - 1, nh)):
        is_first, is_last = js[0] == 0, js[-1] == nh - 1
        operands = [q_blocks[j] for j in js]
        if is_first:
            operands += [k_pieces[k] for k in order]
        else:
            operands += [near(keys_t), near(score), near(logits)]
        out_shape = [pltpu.VMEM((rows_here, total_keys), f32)]
        out_shape += [pltpu.VMEM((depth, rows), bf16)] * len(js)
        kept = len(js) - is_first
        out_shape += [pltpu.VMEM((rows, total_keys), bf16)] * kept
        if is_first:
            out_shape += [pltpu.VMEM((depth, total_keys), bf16)]
            out_shape += [pltpu.VMEM((rows_here, total_keys), bf16)]
        if is_last:
            out_shape += [jax.ShapeDtypeStruct((1, stat_rows, padded), f32)]
        scratch = [
            pltpu.VMEM((len(js), hh, rows_here, lanes), f32),
        ]
        kernel = functools.partial(forward_kernel, cfg, len(js), is_first, is_last)
        aliases = {} if is_first else {len(js) + 2: 0}
        outs = call(kernel, operands, out_shape, scratch, len(js), f"forward{js[0]}", aliases)
        score = outs[0]
        qw += outs[1 : 1 + len(js)]
        active += [None] * is_first + list(outs[1 + len(js) : 1 + len(js) + kept])
        if is_first:
            keys_t, logits = outs[-2:]
        stats = outs[-1] if is_last else stats

    all_stats = [stats] + [swap(stats, "head", j) for j in range(1, nh)]

    grad = kg = None

    def backward(items, name):
        nonlocal grad, kg
        is_first = grad is None
        ranges = [item[2] for item in items if item[2] is not None]
        makes_u = any(item[1] for item in items)
        has_before = bool(ranges) and kg is not None
        halved = ranges != [] and ranges[0] != "all"
        operands = [q_blocks[0] if halved else near(active[item[0]]) for item in items]
        operands += [near(qw[item[0]]) for item in items if item[2] is not None]
        operands += [near(keys_t)]
        operands += all_stats + [rw, near(logits), near(score)] if is_first else [near(grad)]
        aliases = {}
        out_shape = [jax.ShapeDtypeStruct((rows, depth), bf16 if is_first else f32)]
        out_shape = out_shape if makes_u else []
        scratch = [pltpu.VMEM((rows, tile), bf16)] * 2 + [pltpu.VMEM((depth, rows), f32)]
        if not halved:
            if ranges:
                if has_before:
                    aliases = {len(operands) + 1: len(out_shape)}
                out_shape += [pltpu.VMEM((depth, total_keys), f32)]
        else:
            if ranges[0] == "first":
                out_shape += [jax.ShapeDtypeStruct((n // 2, chunk, depth), bf16)]
            else:
                out_shape += [jax.ShapeDtypeStruct((chunk, depth), f32)] * (n // 2)
            out_shape += [pltpu.VMEM((rows, total_keys // 2), bf16)]
            scratch = [pltpu.VMEM((depth, total_keys // 2), f32)]
        if has_before:
            operands += [near(kg)]
        if is_first:
            out_shape += [pltpu.VMEM((rows_here, total_keys), bf16)]
            scratch += [pltpu.VMEM((padded, lanes), f32)]
        kernel = functools.partial(backward_kernel, cfg, items, has_before)
        products = 1 if halved else makes_u + len(ranges)
        outs = call(kernel, operands, out_shape, scratch, products, name, aliases)
        if is_first:
            grad = outs[-1]
        if ranges and ranges[0] == "all":
            kg = outs[1 if makes_u else 0]
        return outs

    part = backward([(1, True, None)], "backward_1")[0]
    moving = ring_next(part, "head")
    for j in range(2, nh):
        items = [(j - 1, False, "all"), (j, True, "all" if j == nh - 1 else None)]
        part = backward(items, f"backward_{j}")[0]
        part = pl.pallas_call(
            add_kernel,
            out_shape=jax.ShapeDtypeStruct((rows, depth), bf16),
            in_specs=[vmem] * 2,
            out_specs=vmem,
            compiler_params=pltpu.CompilerParams(vmem_limit_bytes=vmem_bytes),
            cost_estimate=pl.CostEstimate(
                flops=rows * depth, bytes_accessed=8 * rows * depth, transcendentals=0
            ),
            name=f"add_{j}",
        )(part, moving)
        kg, part = lax.optimization_barrier((kg, part))
        moving = ring_next(part, "head")

    odd, mask_first = backward([(0, False, "first")], "backward_0_first")
    other = swap(odd, "ctx", 1)
    *even, mask_second = backward([(0, False, "second")], "backward_0_second")
    even = [even[i] + other[i].astype(f32) for i in range(n // 2)]
    key_grad = even[0]
    sends = [even[i].astype(bf16) for i in range(1, n // 2)]
    keys_t, *sends = lax.optimization_barrier((keys_t, *sends))
    for i in range(1, n // 2):
        key_grad = key_grad + swap(sends[i - 1], "ctx", 2 * i).astype(f32)
    (u_mine,) = call(
        lambda meta_ref, *refs: query_kernel(cfg, refs[:2], *refs[2:]),
        [near(mask_first), near(mask_second), near(keys_t)],
        [jax.ShapeDtypeStruct((rows, depth), f32)],
        [pltpu.VMEM((depth, rows), f32)],
        1,
        "backward_0",
    )

    query_grad, weight_grad = pl.pallas_call(
        functools.partial(finish_kernel, cfg),
        out_shape=[
            jax.ShapeDtypeStruct((rows_here, hh, depth), f32),
            jax.ShapeDtypeStruct((hh, rows_here), f32),
        ],
        in_specs=[vmem] * 3,
        out_specs=[vmem] * 2,
        compiler_params=pltpu.CompilerParams(vmem_limit_bytes=vmem_bytes),
        cost_estimate=pl.CostEstimate(
            flops=8 * rows * depth, bytes_accessed=14 * rows * depth, transcendentals=0
        ),
        name="finish",
    )(u_mine, moving, q_blocks[0])
    return query_grad, key_grad, weight_grad.T


def solution(mesh):
    in_specs = (P("ctx", "head", None), P("ctx", "head"), P("ctx", None), P(None, "ctx"), P(), P())
    out_specs = (P("ctx", "head", None), P(("ctx", "head"), None), P("ctx", "head"))
    return jax.shard_map(
        per_device, mesh=mesh, in_specs=in_specs, out_specs=out_specs, check_vma=False
    )
```

```python
import functools

import jax
import jax.numpy as jnp
from jax import lax
from jax.experimental import pallas as pl
from jax.experimental.pallas import tpu as pltpu
from jax.sharding import PartitionSpec as P

masked_value = -1e30
lanes = 128
stat_rows = 8
vmem_bytes = 6 * 1024 * 1024
contract_last = (((1,), (1,)), ((), ()))


def swap(value, axis, distance):
    size = lax.axis_size(axis)
    return lax.ppermute(value, axis, [(i, i ^ distance) for i in range(size)])


def ring_next(value, axis):
    size = lax.axis_size(axis)
    ring = list(range(0, size, 2)) + list(range(1, size, 2))[::-1]
    return lax.ppermute(value, axis, [(ring[i], ring[(i + 1) % size]) for i in range(size)])


def in_pairs(count, first, step):
    first(0, 0)

    def body(i, _):
        step(0, 2 * i, 2 * i + 1)
        step(1, 2 * i + 1, 2 * i + 2)
        return 0

    lax.fori_loop(0, count // 2 - 1, body, 0)
    step(0, count - 2, count - 1)
    step(1, count - 1, None)


def row_limits(meta_ref, rows_here):
    row = lax.broadcasted_iota(jnp.int32, (rows_here, 1), 0)
    return meta_ref[0] + meta_ref[1] * rows_here + row


def piece_allowed(meta_ref, limit, k, kc, chunk):
    first = (meta_ref[1] ^ k) * kc + meta_ref[2] * chunk
    position = first + lax.broadcasted_iota(jnp.int32, (limit.shape[0], chunk), 1)
    return position <= limit


def forward_kernel(cfg, count, is_first, is_last, meta_ref, *refs):
    order, nh, rows_here, hh, depth, kc, chunk, scale = cfg
    n = len(order)
    rows = rows_here * hh
    refs = list(refs)
    take = lambda count: [refs.pop(0) for _ in range(count)]
    q_refs = take(count)
    if is_first:
        message_refs = take(n)
    else:
        keys_t_ref, before_ref, logits_ref = take(3)
    (score_ref,) = take(1)
    qw_refs = take(count)
    active_refs = [None] * is_first + take(count - is_first)
    if is_first:
        keys_t_ref, keys_ref, logits_ref = take(3)
    if is_last:
        (stats_ref,) = take(1)
    (wb,) = take(1)
    side = min(256, n * chunk)
    tile = min(4 * side, n * chunk)
    tiles = n * chunk // tile
    if is_first:
        for at, k in enumerate(order):
            keys = message_refs[at][:chunk, :]
            keys_ref[at * chunk : (at + 1) * chunk, :depth] = keys
            keys_ref[at * chunk : (at + 1) * chunk, depth:] = jnp.zeros_like(keys)
            keys = keys.astype(jnp.float32)
            keys_t_ref[:, at * chunk : (at + 1) * chunk] = keys.T.astype(jnp.bfloat16)
            for i in range(chunk // lanes):
                first = chunk + (chunk // lanes * (k % 2) + i) * rows_here
                column = at * chunk + i * lanes
                logits_ref[:, column : column + lanes] = message_refs[at][
                    first : first + rows_here, :
                ]

    eye = (
        lax.broadcasted_iota(jnp.int32, (rows_here, lanes), 0)
        == lax.broadcasted_iota(jnp.int32, (rows_here, lanes), 1)
    ).astype(jnp.float32)
    for j, q_ref in enumerate(q_refs):
        slab = q_ref[rows:, :].astype(jnp.float32)
        for head in range(hh):
            picked = jnp.sum(slab[head : head + 1] * eye, axis=1, keepdims=True)
            wb[j, head] = jnp.broadcast_to(picked, (rows_here, lanes))
        for head in range(0, hh, 2):
            at = slice(head * rows_here, (head + 2) * rows_here)
            q = q_ref[at, :].astype(jnp.float32)
            w = wb[j, head : head + 2].reshape(2 * rows_here, lanes) * scale
            qw_refs[j][:, at] = (q * w).T.astype(jnp.bfloat16)

    def step(j, s):
        for first in range(0, tile, side):
            columns = pl.ds(pl.multiple_of(s * tile + first, side), side)
            dots = jnp.dot(
                q_refs[j][:rows, :], keys_t_ref[:, columns], preferred_element_type=jnp.float32
            )
            total = [None] * (rows_here // 16)
            for head in range(hh):
                for t in range(rows_here // 16):
                    row = head * rows_here + t * 16
                    w = wb[j, head, t * 16 : t * 16 + 16, :]
                    w = jnp.concatenate([w] * (side // lanes), axis=1)
                    active = jnp.maximum(dots[row : row + 16, :], 0.0)
                    if active_refs[j] is not None:
                        active_refs[j][row : row + 16, columns] = active.astype(jnp.bfloat16)
                    value = active * w
                    total[t] = value if head == 0 else total[t] + value
            for t, value in enumerate(total):
                at = slice(t * 16, t * 16 + 16)
                value = value * scale
                if j > 0:
                    value = score_ref[at, columns] + value
                elif not is_first:
                    value = before_ref[at, columns] + value
                score_ref[at, columns] = value
        return 0

    for j in range(count):
        lax.fori_loop(0, tiles, lambda s, _, j=j: step(j, s), 0)
    if not is_last:
        return

    limit = row_limits(meta_ref, rows_here)
    lane = lax.broadcasted_iota(jnp.int32, (rows_here, lanes), 1)
    out = jnp.zeros((rows_here, lanes), jnp.float32)

    def piece(i, at):
        if i == 0:
            return score_ref[:, at * chunk : (at + 1) * chunk]
        return logits_ref[:, at * chunk : (at + 1) * chunk].astype(jnp.float32)

    for i in range(2):
        peak = None
        for at, k in enumerate(order):
            allowed = piece_allowed(meta_ref, limit, k, kc, chunk)
            here = jnp.max(jnp.where(allowed, piece(i, at), masked_value), axis=1, keepdims=True)
            peak = here if peak is None else jnp.maximum(peak, here)
        total = None
        for at, k in enumerate(order):
            allowed = piece_allowed(meta_ref, limit, k, kc, chunk)
            here = jnp.where(allowed, jnp.exp(piece(i, at) - peak), 0.0)
            here = jnp.sum(here, axis=1, keepdims=True)
            total = here if total is None else total + here
        out = jnp.where(lane == 2 * i, peak, out)
        out = jnp.where(lane == 2 * i + 1, total, out)
    padded = stats_ref.shape[2]
    if padded > rows_here:
        out = jnp.concatenate([out, jnp.zeros((padded - rows_here, lanes), jnp.float32)], axis=0)
    stats_ref[0] = out.T[:stat_rows]


def score_gradient(cfg, meta_ref, stats, rw_ref, logits_ref, score_ref, cols, grad_ref):
    order, nh, rows_here, hh, depth, kc, chunk, scale = cfg
    for i in range(2):
        peak = functools.reduce(jnp.maximum, [st[2 * i : 2 * i + 1] for st in stats])
        total = functools.reduce(
            jnp.add,
            [st[2 * i + 1 : 2 * i + 2] * jnp.exp(st[2 * i : 2 * i + 1] - peak) for st in stats],
        )
        cols[2 * i : 2 * i + 1, :] = peak
        cols[2 * i + 1 : 2 * i + 2, :] = rw_ref[...] / total
    cols[4:, :] = jnp.zeros((cols.shape[0] - 4, cols.shape[1]), jnp.float32)
    st = cols[...].T[:rows_here]
    limit = row_limits(meta_ref, rows_here)
    for at, k in enumerate(order):
        logits = logits_ref[:, at * chunk : (at + 1) * chunk].astype(jnp.float32)
        score = score_ref[:, at * chunk : (at + 1) * chunk]
        g = jnp.exp(score - st[:, 0:1]) * st[:, 1:2] - jnp.exp(logits - st[:, 2:3]) * st[:, 3:4]
        g = jnp.where(piece_allowed(meta_ref, limit, k, kc, chunk), g, 0.0)
        grad_ref[:, at * chunk : (at + 1) * chunk] = g.astype(jnp.bfloat16)


def backward_kernel(cfg, items, has_before, meta_ref, *refs):
    order, nh, rows_here, hh, depth, kc, chunk, scale = cfg
    n = len(order)
    rows = rows_here * hh
    refs = list(refs)
    take = lambda count: [refs.pop(0) for _ in range(count)]
    is_first = items[0][0] == 1 and items[0][2] is None
    makes_u = any(item[1] for item in items)
    ranges = [item[2] for item in items if item[2] is not None]
    half = ranges[0] if ranges and ranges[0] != "all" else None
    source_refs = take(len(items))
    qw_refs = [take(1)[0] if item[2] is not None else None for item in items]
    (keys_ref,) = take(1)
    if is_first:
        stat_refs = take(nh)
        rw_ref, logits_ref, score_ref = take(3)
    else:
        (grad_ref,) = take(1)
    before_ref = take(1)[0] if has_before else None
    if makes_u:
        (u_ref,) = take(1)
    if ranges:
        kg_refs = take(n // 2 if half == "second" else 1)
    if is_first:
        (grad_ref,) = take(1)
    if half is not None:
        mask_ref, kg_acc = take(2)
    else:
        masks = take(2)
        (u_acc,) = take(1)
    if is_first:
        (cols,) = take(1)
        stats = [ref[0] for ref in stat_refs]
        score_gradient(cfg, meta_ref, stats, rw_ref, logits_ref, score_ref, cols, grad_ref)
    tile = min(512, n * chunk // 4)
    chunks = max(1, min(4, hh))
    heads = hh // chunks
    part = heads * rows_here
    side = tile // 2

    for index, (_, is_u, keys_range) in enumerate(items):
        tiles = n * chunk // tile
        if half is not None:
            tiles = tiles // 2
        offset = tiles if half == "second" else 0
        source_ref, qw_ref = source_refs[index], qw_refs[index]
        is_start = index == 0 or items[index - 1][2] is None

        def tile_at(s, first=0, size=tile, offset=offset):
            return pl.ds(pl.multiple_of((s + offset) * tile + first, size), size)

        def mask_at(buffer, s, at, first=0, size=tile):
            if half is None:
                return masks[buffer].at[at, first : first + size]
            return mask_ref.at[at, pl.ds(pl.multiple_of(s * tile + first, size), size)]

        def mask_part(buffer, s, i, source_ref=source_ref):
            at = slice(i * part, (i + 1) * part)
            if half is None:
                g = grad_ref[:, tile_at(s)]
                value = source_ref[at, tile_at(s)]
            else:
                g = grad_ref[:, tile_at(s)].astype(jnp.float32)
                value = jnp.dot(
                    source_ref[at, :], keys_ref[:, tile_at(s)], preferred_element_type=jnp.float32
                )
            wide = jnp.broadcast_to(g[None], (heads, rows_here, tile)).reshape(part, tile)
            value = jnp.where(value > 0, wide, jnp.zeros_like(wide))
            mask_at(buffer, s, at)[...] = value.astype(jnp.bfloat16)

        def mask(buffer, s):
            for i in range(chunks):
                mask_part(buffer, s, i)

        def step(buffer, s, following):
            for i in range(chunks):
                if following is not None:
                    mask_part(1 - buffer, following, i)
                if is_u:
                    at = slice(i * part, (i + 1) * part)
                    u_acc[at, :] += jnp.dot(
                        mask_at(buffer, s, at)[...],
                        keys_ref[tile_at(s), :],
                        preferred_element_type=jnp.float32,
                    )[:, :depth]
                if keys_range is None or i % (chunks // 2) != chunks // 2 - 1:
                    continue
                first = i // (chunks // 2) * side
                more = jnp.dot(
                    qw_ref[...],
                    mask_at(buffer, s, slice(0, rows), first, side)[...],
                    preferred_element_type=jnp.float32,
                )
                here = tile_at(s, first, side)
                if not is_start:
                    more = kg_refs[0][:, here] + more
                elif before_ref is not None:
                    more = before_ref[:, here] + more
                if half is None:
                    kg_refs[0][:, here] = more
                else:
                    kg_acc[:, pl.ds(pl.multiple_of(s * tile + first, side), side)] = more

        if is_u:
            u_acc[...] = jnp.zeros_like(u_acc)
        in_pairs(tiles, mask, step)
        if is_u:
            u_ref[...] = u_acc[...].astype(u_ref.dtype)

    if half is not None:
        for i in range(n // 2):
            value = kg_acc[:, i * chunk : (i + 1) * chunk].T
            if half == "first":
                kg_refs[0][i] = value.astype(kg_refs[0].dtype)
            else:
                kg_refs[i][...] = value


def query_kernel(cfg, mask_refs, keys_ref, u_ref, u_acc):
    count = mask_refs[0].shape[1]
    tile = min(512, count)
    u_acc[...] = jnp.zeros_like(u_acc)
    for half, mask_ref in enumerate(mask_refs):

        def step(s, _, half=half, mask_ref=mask_ref):
            at = pl.multiple_of(s * tile, tile)
            u_acc[...] += jnp.dot(
                mask_ref[:, pl.ds(at, tile)],
                keys_ref[pl.ds(pl.multiple_of(half * count + at, tile), tile), :],
                preferred_element_type=jnp.float32,
            )[:, : u_acc.shape[1]]
            return 0

        lax.fori_loop(0, count // tile, step, 0)
    u_ref[...] = u_acc[...]


def prepare_kernel(cfg, meta_ref, query_ref, weights_ref, rw_ref, keys_ref, logits_ref, *refs):
    order, nh, rows_here, hh, depth, kc, chunk, scale = cfg
    sends = len(order) // 2
    rows = rows_here * hh
    parts = chunk // lanes
    message_ref, rw_out_ref, key_refs = refs[0], refs[1], refs[2 : 2 + sends]
    wide, sems = refs[-2], refs[-1]
    share = pl.multiple_of(meta_ref[2] * chunk, chunk)
    copies = []

    def copy(source, target):
        copies.append(pltpu.make_async_copy(source, target, sems.at[len(copies)]))
        copies[-1].start()

    for i in reversed(range(sends)):
        copy(keys_ref.at[pl.ds(share, chunk), :], key_refs[i].at[:chunk, :])
        for core in range(2):
            row = pl.multiple_of((meta_ref[1] ^ (2 * i) ^ core) * rows_here, rows_here)
            for part in range(parts):
                first = chunk + (parts * core + part) * rows_here
                copy(
                    logits_ref.at[pl.ds(row, rows_here), pl.ds(share + part * lanes, lanes)],
                    key_refs[i].at[first : first + rows_here, :],
                )
    every = jnp.broadcast_to(rw_ref[...], (8, rw_ref.shape[1]))
    shift = every.shape[1] - meta_ref[1] * rows_here
    here = pltpu.roll(every, shift, 1)[:1, : rw_out_ref.shape[1]]
    rw_out_ref[...] = here * float(kc * len(order)) ** 0.5
    wide[...] = query_ref[...].astype(jnp.float32)
    for head in range(hh):
        at = slice(head * rows_here, (head + 1) * rows_here)
        message_ref[at, :] = wide[:, head, :].astype(jnp.bfloat16)
    message_ref[rows:, :] = jnp.zeros((message_ref.shape[0] - rows, lanes), jnp.bfloat16)
    message_ref[rows : rows + hh, :rows_here] = weights_ref[...]
    for item in copies:
        item.wait()


def add_kernel(u_ref, moving_ref, out_ref):
    out_ref[...] = (u_ref[...] + moving_ref[...].astype(jnp.float32)).astype(out_ref.dtype)


def finish_kernel(cfg, u_ref, moving_ref, q_ref, query_grad_ref, weight_grad_ref):
    order, nh, rows_here, hh, depth, kc, chunk, scale = cfg
    rows = rows_here * hh
    eye = (
        lax.broadcasted_iota(jnp.int32, (rows_here, lanes), 0)
        == lax.broadcasted_iota(jnp.int32, (rows_here, lanes), 1)
    ).astype(jnp.float32)
    lane = lax.broadcasted_iota(jnp.int32, (lanes, lanes), 1)[:rows_here]
    slab = q_ref[rows:, :].astype(jnp.float32)
    out = jnp.zeros((rows_here, lanes), jnp.float32)
    for head in range(hh):
        at = slice(head * rows_here, (head + 1) * rows_here)
        total = u_ref[at, :] + moving_ref[at, :].astype(jnp.float32)
        w = jnp.sum(slab[head : head + 1] * eye, axis=1, keepdims=True) * scale
        query_grad_ref[:, head, :] = total * w
        along = jnp.sum(total * q_ref[at, :].astype(jnp.float32), axis=1, keepdims=True)
        out = jnp.where(lane == head, along * scale, out)
    if rows_here < lanes:
        out = jnp.concatenate([out, jnp.zeros((lanes - rows_here, lanes), jnp.float32)], axis=0)
    weight_grad_ref[...] = out.T[:hh, :rows_here]


def per_device(query, weights, keys, main_logits, row_weight, offset):
    n = lax.axis_size("ctx")
    nh = lax.axis_size("head")
    c = lax.axis_index("ctx")
    h = lax.axis_index("head")
    rows_here, hh, depth = query.shape
    kc = keys.shape[0]
    chunk = kc // nh
    rows = rows_here * hh
    scale = depth ** (-0.5)
    bf16, f32 = jnp.bfloat16, jnp.float32

    order = list(range(1, n, 2)) + list(range(0, n, 2))
    cfg = (order, nh, rows_here, hh, depth, kc, chunk, scale)
    smem = pl.BlockSpec(memory_space=pltpu.SMEM)
    vmem = pl.BlockSpec(memory_space=pltpu.VMEM)
    padded = -(-rows_here // lanes) * lanes
    meta = jnp.concatenate([offset, jnp.stack([c, h]).astype(jnp.int32)])

    far = lambda x: pltpu.with_memory_space_constraint(x, pltpu.HBM)

    slab_rows = -(-hh // 16) * 16
    parts = chunk // lanes
    message, rw, *key_messages = pl.pallas_call(
        functools.partial(prepare_kernel, cfg),
        out_shape=[
            jax.ShapeDtypeStruct((rows + slab_rows, depth), bf16),
            jax.ShapeDtypeStruct((1, padded), f32),
        ]
        + [jax.ShapeDtypeStruct((chunk + 2 * parts * rows_here, depth), bf16)] * (n // 2),
        in_specs=[smem, vmem, vmem, vmem] + [pl.BlockSpec(memory_space=pltpu.HBM)] * 2,
        out_specs=[vmem] * (2 + n // 2),
        scratch_shapes=[
            pltpu.VMEM((rows_here, hh, depth), f32),
            pltpu.SemaphoreType.DMA((n // 2 * (1 + 2 * parts),)),
        ],
        compiler_params=pltpu.CompilerParams(vmem_limit_bytes=vmem_bytes),
        cost_estimate=pl.CostEstimate(
            flops=rows * depth, bytes_accessed=4 * 1024 * 1024, transcendentals=0
        ),
        name="prepare",
    )(meta, far(query), far(weights.T), far(row_weight[None, :]), far(keys), far(main_logits))
    q_blocks = [message, ring_next(message, "head")]

    k_pieces = [None] * n
    k_pieces[0::2] = [key_messages[0]] + [
        swap(key_messages[k // 2], "ctx", k) for k in range(2, n, 2)
    ]
    k_pieces[4], q_blocks[1] = lax.optimization_barrier((k_pieces[4], q_blocks[1]))
    k_pieces[1::2] = [swap(piece, "ctx", 1) for piece in k_pieces[0::2]]
    for j in range(2, nh):
        q_blocks.append(ring_next(q_blocks[-1], "head"))

    total_keys = n * chunk
    macs = rows * total_keys * depth
    tile = 512

    def call(kernel, operands, out_shape, scratch, products, name, aliases={}):
        return pl.pallas_call(
            kernel,
            out_shape=out_shape,
            input_output_aliases=aliases,
            in_specs=[smem] + [vmem] * len(operands),
            out_specs=[vmem] * len(out_shape),
            scratch_shapes=scratch,
            compiler_params=pltpu.CompilerParams(vmem_limit_bytes=vmem_bytes),
            cost_estimate=pl.CostEstimate(
                flops=int(4 * products * macs), bytes_accessed=4 * 1024 * 1024, transcendentals=0
            ),
            name=name,
        )(meta, *operands)

    near = lambda x: pltpu.with_memory_space_constraint(x, pltpu.VMEM)

    score = keys_t = keys_wide = stats = None
    qw, active = [], []
    for js in (range(nh - 1), range(nh - 1, nh)):
        is_first, is_last = js[0] == 0, js[-1] == nh - 1
        operands = [q_blocks[j] for j in js]
        if is_first:
            operands += [k_pieces[k] for k in order]
        else:
            operands += [near(keys_t), near(score), near(logits)]
        out_shape = [pltpu.VMEM((rows_here, total_keys), f32)]
        out_shape += [pltpu.VMEM((depth, rows), bf16)] * len(js)
        kept = len(js) - is_first
        out_shape += [pltpu.VMEM((rows, total_keys), bf16)] * kept
        if is_first:
            out_shape += [pltpu.VMEM((depth, total_keys), bf16)]
            out_shape += [pltpu.VMEM((total_keys, 2 * depth), bf16)]
            out_shape += [pltpu.VMEM((rows_here, total_keys), bf16)]
        if is_last:
            out_shape += [jax.ShapeDtypeStruct((1, stat_rows, padded), f32)]
        scratch = [
            pltpu.VMEM((len(js), hh, rows_here, lanes), f32),
        ]
        kernel = functools.partial(forward_kernel, cfg, len(js), is_first, is_last)
        aliases = {} if is_first else {len(js) + 2: 0}
        outs = call(kernel, operands, out_shape, scratch, len(js), f"forward{js[0]}", aliases)
        score = outs[0]
        qw += outs[1 : 1 + len(js)]
        active += [None] * is_first + list(outs[1 + len(js) : 1 + len(js) + kept])
        if is_first:
            keys_t, keys_wide, logits = outs[-3:]
        stats = outs[-1] if is_last else stats

    all_stats = [stats] + [swap(stats, "head", j) for j in range(1, nh)]

    grad = kg = None

    def backward(items, name):
        nonlocal grad, kg
        is_first = grad is None
        ranges = [item[2] for item in items if item[2] is not None]
        makes_u = any(item[1] for item in items)
        has_before = bool(ranges) and kg is not None
        halved = ranges != [] and ranges[0] != "all"
        operands = [q_blocks[0] if halved else near(active[item[0]]) for item in items]
        operands += [near(qw[item[0]]) for item in items if item[2] is not None]
        operands += [near(keys_t if halved else keys_wide)]
        operands += all_stats + [rw, near(logits), near(score)] if is_first else [near(grad)]
        aliases = {}
        out_shape = [jax.ShapeDtypeStruct((rows, depth), bf16 if is_first else f32)]
        out_shape = out_shape if makes_u else []
        scratch = [pltpu.VMEM((rows, tile), bf16)] * 2 + [pltpu.VMEM((rows, depth), f32)]
        if not halved:
            if ranges:
                if has_before:
                    aliases = {len(operands) + 1: len(out_shape)}
                out_shape += [pltpu.VMEM((depth, total_keys), f32)]
        else:
            if ranges[0] == "first":
                out_shape += [jax.ShapeDtypeStruct((n // 2, chunk, depth), bf16)]
            else:
                out_shape += [jax.ShapeDtypeStruct((chunk, depth), f32)] * (n // 2)
            out_shape += [pltpu.VMEM((rows, total_keys // 2), bf16)]
            scratch = [pltpu.VMEM((depth, total_keys // 2), f32)]
        if has_before:
            operands += [near(kg)]
        if is_first:
            out_shape += [pltpu.VMEM((rows_here, total_keys), bf16)]
            scratch += [pltpu.VMEM((padded, lanes), f32)]
        kernel = functools.partial(backward_kernel, cfg, items, has_before)
        products = 1 if halved else makes_u + len(ranges)
        outs = call(kernel, operands, out_shape, scratch, products, name, aliases)
        if is_first:
            grad = outs[-1]
        if ranges and ranges[0] == "all":
            kg = outs[1 if makes_u else 0]
        return outs

    part = backward([(1, True, None)], "backward_1")[0]
    moving = ring_next(part, "head")
    for j in range(2, nh):
        items = [(j - 1, False, "all"), (j, True, "all" if j == nh - 1 else None)]
        part = backward(items, f"backward_{j}")[0]
        part = pl.pallas_call(
            add_kernel,
            out_shape=jax.ShapeDtypeStruct((rows, depth), bf16),
            in_specs=[vmem] * 2,
            out_specs=vmem,
            compiler_params=pltpu.CompilerParams(vmem_limit_bytes=vmem_bytes),
            cost_estimate=pl.CostEstimate(
                flops=rows * depth, bytes_accessed=8 * rows * depth, transcendentals=0
            ),
            name=f"add_{j}",
        )(part, moving)
        kg, part = lax.optimization_barrier((kg, part))
        moving = ring_next(part, "head")

    odd, mask_first = backward([(0, False, "first")], "backward_0_first")
    other = swap(odd, "ctx", 1)
    *even, mask_second = backward([(0, False, "second")], "backward_0_second")
    even = [even[i] + other[i].astype(f32) for i in range(n // 2)]
    key_grad = even[0]
    sends = [even[i].astype(bf16) for i in range(1, n // 2)]
    keys_wide, *sends = lax.optimization_barrier((keys_wide, *sends))
    for i in range(1, n // 2):
        key_grad = key_grad + swap(sends[i - 1], "ctx", 2 * i).astype(f32)
    (u_mine,) = call(
        lambda meta_ref, *refs: query_kernel(cfg, refs[:2], *refs[2:]),
        [near(mask_first), near(mask_second), near(keys_wide)],
        [jax.ShapeDtypeStruct((rows, depth), f32)],
        [pltpu.VMEM((rows, depth), f32)],
        1,
        "backward_0",
    )

    query_grad, weight_grad = pl.pallas_call(
        functools.partial(finish_kernel, cfg),
        out_shape=[
            jax.ShapeDtypeStruct((rows_here, hh, depth), f32),
            jax.ShapeDtypeStruct((hh, rows_here), f32),
        ],
        in_specs=[vmem] * 3,
        out_specs=[vmem] * 2,
        compiler_params=pltpu.CompilerParams(vmem_limit_bytes=vmem_bytes),
        cost_estimate=pl.CostEstimate(
            flops=8 * rows * depth, bytes_accessed=14 * rows * depth, transcendentals=0
        ),
        name="finish",
    )(u_mine, moving, q_blocks[0])
    return query_grad, key_grad, weight_grad.T


def solution(mesh):
    in_specs = (P("ctx", "head", None), P("ctx", "head"), P("ctx", None), P(None, "ctx"), P(), P())
    out_specs = (P("ctx", "head", None), P(("ctx", "head"), None), P("ctx", "head"))
    return jax.shard_map(
        per_device, mesh=mesh, in_specs=in_specs, out_specs=out_specs, check_vma=False
    )
```

```python
import functools

import jax
import jax.numpy as jnp
from jax import lax
from jax.experimental import pallas as pl
from jax.experimental.pallas import tpu as pltpu
from jax.sharding import PartitionSpec as P

masked_value = -1e30
lanes = 128
stat_rows = 8
vmem_bytes = 6 * 1024 * 1024
contract_last = (((1,), (1,)), ((), ()))


def swap(value, axis, distance):
    size = lax.axis_size(axis)
    return lax.ppermute(value, axis, [(i, i ^ distance) for i in range(size)])


def ring_next(value, axis):
    size = lax.axis_size(axis)
    ring = list(range(0, size, 2)) + list(range(1, size, 2))[::-1]
    return lax.ppermute(value, axis, [(ring[i], ring[(i + 1) % size]) for i in range(size)])


def in_pairs(count, first, step):
    first(0, 0)

    def body(i, _):
        step(0, 2 * i, 2 * i + 1)
        step(1, 2 * i + 1, 2 * i + 2)
        return 0

    lax.fori_loop(0, count // 2 - 1, body, 0)
    step(0, count - 2, count - 1)
    step(1, count - 1, None)


def row_limits(meta_ref, rows_here):
    row = lax.broadcasted_iota(jnp.int32, (rows_here, 1), 0)
    return meta_ref[0] + meta_ref[1] * rows_here + row


def piece_allowed(meta_ref, limit, k, kc, chunk):
    first = (meta_ref[1] ^ k) * kc + meta_ref[2] * chunk
    position = first + lax.broadcasted_iota(jnp.int32, (limit.shape[0], chunk), 1)
    return position <= limit


def spread_weights(cfg, q_ref, wide_ref, qw_ref):
    order, nh, rows_here, hh, depth, kc, chunk, scale = cfg
    rows = rows_here * hh
    eye = (
        lax.broadcasted_iota(jnp.int32, (rows_here, lanes), 0)
        == lax.broadcasted_iota(jnp.int32, (rows_here, lanes), 1)
    ).astype(jnp.float32)
    slab = q_ref[rows:, :].astype(jnp.float32)
    for head in range(hh):
        picked = jnp.sum(slab[head : head + 1] * eye, axis=1, keepdims=True)
        wide_ref[head] = jnp.broadcast_to(picked, (rows_here, lanes))
    for head in range(0, hh, 2):
        at = slice(head * rows_here, (head + 2) * rows_here)
        q = q_ref[at, :].astype(jnp.float32)
        w = wide_ref[head : head + 2].reshape(2 * rows_here, lanes) * scale
        qw_ref[:, at] = (q * w).T.astype(jnp.bfloat16)


def unpack(cfg, message_ref, k, at, keys_ref, keys_t_ref, logits_ref):
    order, nh, rows_here, hh, depth, kc, chunk, scale = cfg
    keys = message_ref[:chunk, :]
    keys_ref[at : at + chunk, :] = keys
    keys_t_ref[:, at : at + chunk] = keys.astype(jnp.float32).T.astype(jnp.bfloat16)
    for i in range(chunk // lanes):
        first = chunk + (chunk // lanes * (k % 2) + i) * rows_here
        column = at + i * lanes
        logits_ref[:, column : column + lanes] = message_ref[first : first + rows_here, :]


def add_scores(cfg, q_ref, wide_ref, keys_t_ref, score_ref, before_ref, start, count, active_ref):
    order, nh, rows_here, hh, depth, kc, chunk, scale = cfg
    rows = rows_here * hh
    side = min(256, count)
    tile = min(4 * side, count)

    def step(s, _):
        for first in range(0, tile, side):
            local = pl.ds(pl.multiple_of(s * tile + first, side), side)
            columns = pl.ds(pl.multiple_of(start + s * tile + first, side), side)
            dots = jnp.dot(
                q_ref[:rows, :], keys_t_ref[:, columns], preferred_element_type=jnp.float32
            )
            total = [None] * (rows_here // 16)
            for head in range(hh):
                for t in range(rows_here // 16):
                    row = head * rows_here + t * 16
                    w = wide_ref[head, t * 16 : t * 16 + 16, :]
                    w = jnp.concatenate([w] * (side // lanes), axis=1)
                    active = jnp.maximum(dots[row : row + 16, :], 0.0)
                    if active_ref is not None:
                        active_ref[row : row + 16, local] = active.astype(jnp.bfloat16)
                    value = active * w
                    total[t] = value if head == 0 else total[t] + value
            for t, value in enumerate(total):
                at = slice(t * 16, t * 16 + 16)
                value = value * scale
                if before_ref is not None:
                    value = before_ref[at, columns] + value
                score_ref[at, columns] = value
        return 0

    lax.fori_loop(0, count // tile, step, 0)


def forward_early_kernel(cfg, pieces, is_first, meta_ref, *refs):
    chunk = cfg[6]
    refs = list(refs)
    take = lambda count: [refs.pop(0) for _ in range(count)]
    q_refs = take(2)
    wide_refs = None if is_first else take(2)
    message_refs = take(len(pieces))
    score_ref, keys_ref, keys_t_ref, logits_ref, active_ref = take(5)
    if is_first:
        qw_refs, wide_refs = take(2), take(2)
        for j in range(2):
            spread_weights(cfg, q_refs[j], wide_refs[j], qw_refs[j])
    for at, k in enumerate(pieces):
        unpack(cfg, message_refs[at], k, at * chunk, keys_ref, keys_t_ref, logits_ref)
    count = len(pieces) * chunk
    add_scores(cfg, q_refs[0], wide_refs[0], keys_t_ref, score_ref, None, 0, count, None)
    add_scores(cfg, q_refs[1], wide_refs[1], keys_t_ref, score_ref, score_ref, 0, count, active_ref)


def forward_middle_kernel(cfg, groups, meta_ref, *refs):
    order, nh, rows_here, hh, depth, kc, chunk, scale = cfg
    refs = list(refs)
    take = lambda count: [refs.pop(0) for _ in range(count)]
    q_refs, wide_refs = take(2), take(2)
    new_q_refs = take(nh - 3)
    parts = [take(4) for _ in groups[:-1]]
    message_refs = take(len(groups[-1]))
    whole = take(4)
    score_ref, keys_ref, keys_t_ref, logits_ref = whole
    (last_active_ref,) = take(1)
    active_refs, qw_refs = take(nh - 3), take(nh - 3)
    (wide,) = take(1)
    start = 0
    for group, part in zip(groups, parts):
        end = start + len(group) * chunk
        score_ref[:, start:end] = part[0][...]
        keys_ref[start:end, :] = part[1][...]
        keys_t_ref[:, start:end] = part[2][...]
        logits_ref[:, start:end] = part[3][...]
        start = end
    for i, k in enumerate(groups[-1]):
        unpack(cfg, message_refs[i], k, start + i * chunk, keys_ref, keys_t_ref, logits_ref)
    count = len(groups[-1]) * chunk
    add_scores(cfg, q_refs[0], wide_refs[0], keys_t_ref, score_ref, None, start, count, None)
    add_scores(
        cfg, q_refs[1], wide_refs[1], keys_t_ref, score_ref, score_ref, start, count, last_active_ref
    )
    for q_ref, active_ref, qw_ref in zip(new_q_refs, active_refs, qw_refs):
        spread_weights(cfg, q_ref, wide, qw_ref)
        every = len(order) * chunk
        add_scores(cfg, q_ref, wide, keys_t_ref, score_ref, score_ref, 0, every, active_ref)


def forward_last_kernel(cfg, meta_ref, *refs):
    order, nh, rows_here, hh, depth, kc, chunk, scale = cfg
    q_ref, keys_t_ref, before_ref, logits_ref, score_ref, active_ref, qw_ref, stats_ref, wide = refs
    spread_weights(cfg, q_ref, wide, qw_ref)
    every = len(order) * chunk
    add_scores(cfg, q_ref, wide, keys_t_ref, score_ref, before_ref, 0, every, active_ref)

    limit = row_limits(meta_ref, rows_here)
    lane = lax.broadcasted_iota(jnp.int32, (rows_here, lanes), 1)
    out = jnp.zeros((rows_here, lanes), jnp.float32)

    def piece(i, at):
        if i == 0:
            return score_ref[:, at * chunk : (at + 1) * chunk]
        return logits_ref[:, at * chunk : (at + 1) * chunk].astype(jnp.float32)

    for i in range(2):
        peak = None
        for at, k in enumerate(order):
            allowed = piece_allowed(meta_ref, limit, k, kc, chunk)
            here = jnp.max(jnp.where(allowed, piece(i, at), masked_value), axis=1, keepdims=True)
            peak = here if peak is None else jnp.maximum(peak, here)
        total = None
        for at, k in enumerate(order):
            allowed = piece_allowed(meta_ref, limit, k, kc, chunk)
            here = jnp.where(allowed, jnp.exp(piece(i, at) - peak), 0.0)
            here = jnp.sum(here, axis=1, keepdims=True)
            total = here if total is None else total + here
        out = jnp.where(lane == 2 * i, peak, out)
        out = jnp.where(lane == 2 * i + 1, total, out)
    padded = stats_ref.shape[2]
    if padded > rows_here:
        out = jnp.concatenate([out, jnp.zeros((padded - rows_here, lanes), jnp.float32)], axis=0)
    stats_ref[0] = out.T[:stat_rows]


def score_gradient(cfg, meta_ref, stats, rw_ref, logits_ref, score_ref, cols, grad_ref):
    order, nh, rows_here, hh, depth, kc, chunk, scale = cfg
    for i in range(2):
        peak = functools.reduce(jnp.maximum, [st[2 * i : 2 * i + 1] for st in stats])
        total = functools.reduce(
            jnp.add,
            [st[2 * i + 1 : 2 * i + 2] * jnp.exp(st[2 * i : 2 * i + 1] - peak) for st in stats],
        )
        cols[2 * i : 2 * i + 1, :] = peak
        cols[2 * i + 1 : 2 * i + 2, :] = rw_ref[...] / total
    cols[4:, :] = jnp.zeros((cols.shape[0] - 4, cols.shape[1]), jnp.float32)
    st = cols[...].T[:rows_here]
    limit = row_limits(meta_ref, rows_here)
    for at, k in enumerate(order):
        logits = logits_ref[:, at * chunk : (at + 1) * chunk].astype(jnp.float32)
        score = score_ref[:, at * chunk : (at + 1) * chunk]
        g = jnp.exp(score - st[:, 0:1]) * st[:, 1:2] - jnp.exp(logits - st[:, 2:3]) * st[:, 3:4]
        g = jnp.where(piece_allowed(meta_ref, limit, k, kc, chunk), g, 0.0)
        grad_ref[:, at * chunk : (at + 1) * chunk] = g.astype(jnp.bfloat16)


def backward_kernel(cfg, items, has_before, meta_ref, *refs):
    order, nh, rows_here, hh, depth, kc, chunk, scale = cfg
    n = len(order)
    rows = rows_here * hh
    refs = list(refs)
    take = lambda count: [refs.pop(0) for _ in range(count)]
    is_first = items[0][0] == 1 and items[0][2] is None
    makes_u = any(item[1] for item in items)
    ranges = [item[2] for item in items if item[2] is not None]
    half = ranges[0] if ranges and ranges[0] != "all" else None
    sources = [take(3 if item[0] == 1 else 1) for item in items]
    qw_refs = [take(1)[0] if item[2] is not None else None for item in items]
    (keys_ref,) = take(1)
    if is_first:
        stat_refs = take(nh)
        rw_ref, logits_ref, score_ref = take(3)
    else:
        (grad_ref,) = take(1)
    before_ref = take(1)[0] if has_before else None
    if makes_u:
        (u_ref,) = take(1)
    if ranges:
        kg_refs = take(n // 2 if half == "second" else 1)
    if is_first:
        (grad_ref,) = take(1)
    if half is not None:
        mask_ref, kg_acc = take(2)
    else:
        masks = take(2)
        (u_acc,) = take(1)
    if is_first:
        (cols,) = take(1)
        stats = [ref[0] for ref in stat_refs]
        score_gradient(cfg, meta_ref, stats, rw_ref, logits_ref, score_ref, cols, grad_ref)
    tile = chunk
    chunks = max(1, min(4, hh))
    heads = hh // chunks
    part = heads * rows_here
    side = tile // 2

    todo = []
    for index, (_, is_u, keys_range) in enumerate(items):
        base = 0
        for ref in sources[index]:
            tiles = n // 2 if half is not None else ref.shape[1] // tile
            todo.append((index, is_u, keys_range, ref, base, tiles))
            base += tiles

    for index, is_u, keys_range, source_ref, base, tiles in todo:
        qw_ref = qw_refs[index]
        is_start = index == 0 or items[index - 1][2] is None

        def tile_at(s, first=0, size=tile, base=base):
            if half is None:
                position = s + base
            else:
                position = meta_ref[3 + (n // 2 if half == "second" else 0) + s]
            return pl.ds(pl.multiple_of(position * tile + first, size), size)

        def local(s, first=0, size=tile):
            return pl.ds(pl.multiple_of(s * tile + first, size), size)

        def mask_at(buffer, s, at, first=0, size=tile):
            if half is None:
                return masks[buffer].at[at, first : first + size]
            return mask_ref.at[at, local(s, first, size)]

        def mask_part(buffer, s, i, source_ref=source_ref):
            at = slice(i * part, (i + 1) * part)
            if half is None:
                g = grad_ref[:, tile_at(s)]
                value = source_ref[at, local(s)]
            else:
                g = grad_ref[:, tile_at(s)].astype(jnp.float32)
                value = jnp.dot(
                    source_ref[at, :], keys_ref[:, tile_at(s)], preferred_element_type=jnp.float32
                )
            wide = jnp.broadcast_to(g[None], (heads, rows_here, tile)).reshape(part, tile)
            value = jnp.where(value > 0, wide, jnp.zeros_like(wide))
            mask_at(buffer, s, at)[...] = value.astype(jnp.bfloat16)

        def mask(buffer, s):
            for i in range(chunks):
                mask_part(buffer, s, i)

        def step(buffer, s, following):
            for i in range(chunks):
                if following is not None:
                    mask_part(1 - buffer, following, i)
                if is_u:
                    at = slice(i * part, (i + 1) * part)
                    u_acc[at, :] += jnp.dot(
                        mask_at(buffer, s, at)[...],
                        keys_ref[tile_at(s), :],
                        preferred_element_type=jnp.float32,
                    )
                if keys_range is None or i % (chunks // 2) != chunks // 2 - 1:
                    continue
                first = i // (chunks // 2) * side
                more = jnp.dot(
                    qw_ref[...],
                    mask_at(buffer, s, slice(0, rows), first, side)[...],
                    preferred_element_type=jnp.float32,
                )
                here = tile_at(s, first, side)
                if not is_start:
                    more = kg_refs[0][:, here] + more
                elif before_ref is not None:
                    more = before_ref[:, here] + more
                if half is None:
                    kg_refs[0][:, here] = more
                else:
                    kg_acc[:, local(s, first, side)] = more

        if is_u and base == 0:
            u_acc[...] = jnp.zeros_like(u_acc)
        in_pairs(tiles, mask, step)
        if is_u and (base + tiles) == n:
            u_ref[...] = u_acc[...].astype(u_ref.dtype)

    if half is not None:
        for i in range(n // 2):
            value = kg_acc[:, i * chunk : (i + 1) * chunk].T
            if half == "first":
                kg_refs[0][i] = value.astype(kg_refs[0].dtype)
            else:
                kg_refs[i][...] = value


def query_kernel(cfg, meta_ref, first_ref, second_ref, keys_ref, u_ref, u_acc):
    chunk, pieces = cfg[6], len(cfg[0]) // 2
    u_acc[...] = jnp.zeros_like(u_acc)
    for half, mask_ref in enumerate((first_ref, second_ref)):

        def step(s, _, half=half, mask_ref=mask_ref):
            position = meta_ref[3 + half * pieces + s]
            u_acc[...] += jnp.dot(
                mask_ref[:, pl.ds(pl.multiple_of(s * chunk, chunk), chunk)],
                keys_ref[pl.ds(pl.multiple_of(position * chunk, chunk), chunk), :],
                preferred_element_type=jnp.float32,
            )
            return 0

        lax.fori_loop(0, pieces, step, 0)
    u_ref[...] = u_acc[...]


def prepare_kernel(cfg, meta_ref, query_ref, weights_ref, rw_ref, keys_ref, logits_ref, *refs):
    order, nh, rows_here, hh, depth, kc, chunk, scale = cfg
    sends = len(order) // 2
    rows = rows_here * hh
    parts = chunk // lanes
    message_ref, rw_out_ref, key_refs = refs[0], refs[1], refs[2 : 2 + sends]
    wide, sems = refs[-2], refs[-1]
    share = pl.multiple_of(meta_ref[2] * chunk, chunk)
    copies = []

    def copy(source, target):
        copies.append(pltpu.make_async_copy(source, target, sems.at[len(copies)]))
        copies[-1].start()

    for i in reversed(range(sends)):
        copy(keys_ref.at[pl.ds(share, chunk), :], key_refs[i].at[:chunk, :])
        for core in range(2):
            row = pl.multiple_of((meta_ref[1] ^ (2 * i) ^ core) * rows_here, rows_here)
            for part in range(parts):
                first = chunk + (parts * core + part) * rows_here
                copy(
                    logits_ref.at[pl.ds(row, rows_here), pl.ds(share + part * lanes, lanes)],
                    key_refs[i].at[first : first + rows_here, :],
                )
    every = jnp.broadcast_to(rw_ref[...], (8, rw_ref.shape[1]))
    shift = every.shape[1] - meta_ref[1] * rows_here
    here = pltpu.roll(every, shift, 1)[:1, : rw_out_ref.shape[1]]
    rw_out_ref[...] = here * float(kc * len(order)) ** 0.5
    wide[...] = query_ref[...].astype(jnp.float32)
    for head in range(hh):
        at = slice(head * rows_here, (head + 1) * rows_here)
        message_ref[at, :] = wide[:, head, :].astype(jnp.bfloat16)
    message_ref[rows:, :] = jnp.zeros((message_ref.shape[0] - rows, lanes), jnp.bfloat16)
    message_ref[rows : rows + hh, :rows_here] = weights_ref[...]
    for item in copies:
        item.wait()


def add_kernel(u_ref, moving_ref, out_ref):
    out_ref[...] = (u_ref[...] + moving_ref[...].astype(jnp.float32)).astype(out_ref.dtype)


def finish_kernel(cfg, u_ref, moving_ref, q_ref, query_grad_ref, weight_grad_ref):
    order, nh, rows_here, hh, depth, kc, chunk, scale = cfg
    rows = rows_here * hh
    eye = (
        lax.broadcasted_iota(jnp.int32, (rows_here, lanes), 0)
        == lax.broadcasted_iota(jnp.int32, (rows_here, lanes), 1)
    ).astype(jnp.float32)
    lane = lax.broadcasted_iota(jnp.int32, (lanes, lanes), 1)[:rows_here]
    slab = q_ref[rows:, :].astype(jnp.float32)
    out = jnp.zeros((rows_here, lanes), jnp.float32)
    for head in range(hh):
        at = slice(head * rows_here, (head + 1) * rows_here)
        total = u_ref[at, :] + moving_ref[at, :].astype(jnp.float32)
        w = jnp.sum(slab[head : head + 1] * eye, axis=1, keepdims=True) * scale
        query_grad_ref[:, head, :] = total * w
        along = jnp.sum(total * q_ref[at, :].astype(jnp.float32), axis=1, keepdims=True)
        out = jnp.where(lane == head, along * scale, out)
    if rows_here < lanes:
        out = jnp.concatenate([out, jnp.zeros((lanes - rows_here, lanes), jnp.float32)], axis=0)
    weight_grad_ref[...] = out.T[:hh, :rows_here]


def per_device(query, weights, keys, main_logits, row_weight, offset):
    n = lax.axis_size("ctx")
    nh = lax.axis_size("head")
    c = lax.axis_index("ctx")
    h = lax.axis_index("head")
    rows_here, hh, depth = query.shape
    kc = keys.shape[0]
    chunk = kc // nh
    rows = rows_here * hh
    scale = depth ** (-0.5)
    bf16, f32 = jnp.bfloat16, jnp.float32

    groups = [
        [1, 0],
        list(range(3, n - 2, 2)) + list(range(2, n - 2, 2)),
        [n - 1, n - 2],
    ]
    order = sum(groups, [])
    cfg = (order, nh, rows_here, hh, depth, kc, chunk, scale)
    smem = pl.BlockSpec(memory_space=pltpu.SMEM)
    vmem = pl.BlockSpec(memory_space=pltpu.VMEM)
    padded = -(-rows_here // lanes) * lanes
    table = [order.index(k) for k in list(range(1, n, 2)) + list(range(0, n, 2))]
    meta = jnp.concatenate(
        [offset, jnp.stack([c, h]).astype(jnp.int32), jnp.array(table, jnp.int32)]
    )

    far = lambda x: pltpu.with_memory_space_constraint(x, pltpu.HBM)

    slab_rows = -(-hh // 16) * 16
    parts = chunk // lanes
    message, rw, *key_messages = pl.pallas_call(
        functools.partial(prepare_kernel, cfg),
        out_shape=[
            jax.ShapeDtypeStruct((rows + slab_rows, depth), bf16),
            jax.ShapeDtypeStruct((1, padded), f32),
        ]
        + [jax.ShapeDtypeStruct((chunk + 2 * parts * rows_here, depth), bf16)] * (n // 2),
        in_specs=[smem, vmem, vmem, vmem] + [pl.BlockSpec(memory_space=pltpu.HBM)] * 2,
        out_specs=[vmem] * (2 + n // 2),
        scratch_shapes=[
            pltpu.VMEM((rows_here, hh, depth), f32),
            pltpu.SemaphoreType.DMA((n // 2 * (1 + 2 * parts),)),
        ],
        compiler_params=pltpu.CompilerParams(vmem_limit_bytes=vmem_bytes),
        cost_estimate=pl.CostEstimate(
            flops=rows * depth, bytes_accessed=4 * 1024 * 1024, transcendentals=0
        ),
        name="prepare",
    )(meta, far(query), far(weights.T), far(row_weight[None, :]), far(keys), far(main_logits))
    q_blocks = [message, ring_next(message, "head")]

    k_pieces = [None] * n
    k_pieces[0::2] = [key_messages[0]] + [
        swap(key_messages[k // 2], "ctx", k) for k in range(2, n, 2)
    ]
    k_pieces[1] = swap(k_pieces[0], "ctx", 1)
    for j in range(2, nh):
        q_blocks.append(ring_next(q_blocks[-1], "head"))

    total_keys = n * chunk
    macs = rows * total_keys * depth
    tile = chunk

    def call(kernel, operands, out_shape, scratch, products, name, aliases={}):
        return pl.pallas_call(
            kernel,
            out_shape=out_shape,
            input_output_aliases=aliases,
            in_specs=[smem] + [vmem] * len(operands),
            out_specs=[vmem] * len(out_shape),
            scratch_shapes=scratch,
            compiler_params=pltpu.CompilerParams(vmem_limit_bytes=vmem_bytes),
            cost_estimate=pl.CostEstimate(
                flops=int(4 * products * macs),
                bytes_accessed=int(4 * products * 2**20),
                transcendentals=0,
            ),
            name=name,
        )(meta, *operands)

    near = lambda x: pltpu.with_memory_space_constraint(x, pltpu.VMEM)

    wide_shape = pltpu.VMEM((hh, rows_here, lanes), f32)
    qw_shape = pltpu.VMEM((depth, rows), bf16)

    def keys_shapes(count):
        return [
            pltpu.VMEM((rows_here, count), f32),
            pltpu.VMEM((count, depth), bf16),
            pltpu.VMEM((depth, count), bf16),
            pltpu.VMEM((rows_here, count), bf16),
        ]

    nears = lambda xs: [near(x) for x in xs]
    early, early_active, qw, wides = [], [], [], []
    for i, group in enumerate(groups[:2]):
        count = len(group) * chunk
        if i == 1:
            far_even = range(2, n - 2, 2)
            wides[0], *came = lax.optimization_barrier((wides[0], *(k_pieces[k] for k in far_even)))
            for k, piece in zip(far_even, came):
                k_pieces[k], k_pieces[k + 1] = piece, swap(piece, "ctx", 1)
        outs = call(
            functools.partial(forward_early_kernel, cfg, group, i == 0),
            q_blocks[:2] + nears(wides) + [k_pieces[k] for k in group],
            keys_shapes(count)
            + [pltpu.VMEM((rows, count), bf16)]
            + ([qw_shape] * 2 + [wide_shape] * 2 if i == 0 else []),
            [],
            0.001,
            f"forward_early_{i}",
        )
        early += outs[:4]
        early_active += [outs[4]]
        if i == 0:
            qw, wides = list(outs[5:7]), list(outs[7:9])
    early[4], came = lax.optimization_barrier((early[4], k_pieces[n - 2]))
    k_pieces[n - 2], k_pieces[n - 1] = came, swap(came, "ctx", 1)
    last = len(groups[2]) * chunk
    outs = call(
        functools.partial(forward_middle_kernel, cfg, groups),
        q_blocks[:2]
        + nears(wides)
        + q_blocks[2 : nh - 1]
        + nears(early)
        + [k_pieces[k] for k in groups[2]],
        keys_shapes(total_keys)
        + [pltpu.VMEM((rows, last), bf16)]
        + [pltpu.VMEM((rows, total_keys), bf16)] * (nh - 3)
        + [qw_shape] * (nh - 3),
        [pltpu.VMEM((hh, rows_here, lanes), f32)],
        nh - 2.5,
        "forward_middle",
    )
    score, keys_all, keys_t, logits = outs[:4]
    active = [None, early_active + [outs[4]]]
    active += [[value] for value in outs[5 : 5 + nh - 3]]
    qw += list(outs[5 + nh - 3 :])
    score, last_active, last_qw, stats = call(
        functools.partial(forward_last_kernel, cfg),
        [q_blocks[nh - 1], near(keys_t), near(score), near(logits)],
        [
            pltpu.VMEM((rows_here, total_keys), f32),
            pltpu.VMEM((rows, total_keys), bf16),
            qw_shape,
            jax.ShapeDtypeStruct((1, stat_rows, padded), f32),
        ],
        [pltpu.VMEM((hh, rows_here, lanes), f32)],
        1,
        "forward_last",
        {3: 0},
    )
    active.append([last_active])
    qw.append(last_qw)

    all_stats = [stats] + [swap(stats, "head", j) for j in range(1, nh)]

    grad = kg = None

    def backward(items, name):
        nonlocal grad, kg
        is_first = grad is None
        ranges = [item[2] for item in items if item[2] is not None]
        makes_u = any(item[1] for item in items)
        has_before = bool(ranges) and kg is not None
        halved = ranges != [] and ranges[0] != "all"
        operands = []
        for item in items:
            operands += [q_blocks[0]] if halved else nears(active[item[0]])
        operands += [near(qw[item[0]]) for item in items if item[2] is not None]
        operands += [near(keys_t if halved else keys_all)]
        operands += all_stats + [rw, near(logits), near(score)] if is_first else [near(grad)]
        aliases = {}
        out_shape = [jax.ShapeDtypeStruct((rows, depth), bf16 if is_first else f32)]
        out_shape = out_shape if makes_u else []
        scratch = [pltpu.VMEM((rows, tile), bf16)] * 2 + [pltpu.VMEM((rows, depth), f32)]
        if not halved:
            if ranges:
                if has_before:
                    aliases = {len(operands) + 1: len(out_shape)}
                out_shape += [pltpu.VMEM((depth, total_keys), f32)]
        else:
            if ranges[0] == "first":
                out_shape += [jax.ShapeDtypeStruct((n // 2, chunk, depth), bf16)]
            else:
                out_shape += [jax.ShapeDtypeStruct((chunk, depth), f32)] * (n // 2)
            out_shape += [pltpu.VMEM((rows, total_keys // 2), bf16)]
            scratch = [pltpu.VMEM((depth, total_keys // 2), f32)]
        if has_before:
            operands += [near(kg)]
        if is_first:
            out_shape += [pltpu.VMEM((rows_here, total_keys), bf16)]
            scratch += [pltpu.VMEM((padded, lanes), f32)]
        kernel = functools.partial(backward_kernel, cfg, items, has_before)
        products = 1 if halved else makes_u + len(ranges)
        outs = call(kernel, operands, out_shape, scratch, products, name, aliases)
        if is_first:
            grad = outs[-1]
        if ranges and ranges[0] == "all":
            kg = outs[1 if makes_u else 0]
        return outs

    part = backward([(1, True, None)], "backward_1")[0]
    moving = ring_next(part, "head")
    for j in range(2, nh):
        items = [(j - 1, False, "all"), (j, True, "all" if j == nh - 1 else None)]
        part = backward(items, f"backward_{j}")[0]
        part = pl.pallas_call(
            add_kernel,
            out_shape=jax.ShapeDtypeStruct((rows, depth), bf16),
            in_specs=[vmem] * 2,
            out_specs=vmem,
            compiler_params=pltpu.CompilerParams(vmem_limit_bytes=vmem_bytes),
            cost_estimate=pl.CostEstimate(
                flops=rows * depth, bytes_accessed=8 * rows * depth, transcendentals=0
            ),
            name=f"add_{j}",
        )(part, moving)
        kg, part = lax.optimization_barrier((kg, part))
        moving = ring_next(part, "head")

    odd, mask_first = backward([(0, False, "first")], "backward_0_first")
    other = swap(odd, "ctx", 1)
    *even, mask_second = backward([(0, False, "second")], "backward_0_second")
    even = [even[i] + other[i].astype(f32) for i in range(n // 2)]
    key_grad = even[0]
    sends = [even[i].astype(bf16) for i in range(1, n // 2)]
    keys_all, *sends = lax.optimization_barrier((keys_all, *sends))
    for i in range(1, n // 2):
        key_grad = key_grad + swap(sends[i - 1], "ctx", 2 * i).astype(f32)
    (u_mine,) = call(
        functools.partial(query_kernel, cfg),
        [near(mask_first), near(mask_second), near(keys_all)],
        [jax.ShapeDtypeStruct((rows, depth), f32)],
        [pltpu.VMEM((rows, depth), f32)],
        1,
        "backward_0",
    )

    query_grad, weight_grad = pl.pallas_call(
        functools.partial(finish_kernel, cfg),
        out_shape=[
            jax.ShapeDtypeStruct((rows_here, hh, depth), f32),
            jax.ShapeDtypeStruct((hh, rows_here), f32),
        ],
        in_specs=[vmem] * 3,
        out_specs=[vmem] * 2,
        compiler_params=pltpu.CompilerParams(vmem_limit_bytes=vmem_bytes),
        cost_estimate=pl.CostEstimate(
            flops=8 * rows * depth, bytes_accessed=14 * rows * depth, transcendentals=0
        ),
        name="finish",
    )(u_mine, moving, q_blocks[0])
    return query_grad, key_grad, weight_grad.T


def solution(mesh):
    in_specs = (P("ctx", "head", None), P("ctx", "head"), P("ctx", None), P(None, "ctx"), P(), P())
    out_specs = (P("ctx", "head", None), P(("ctx", "head"), None), P("ctx", "head"))
    return jax.shard_map(
        per_device, mesh=mesh, in_specs=in_specs, out_specs=out_specs, check_vma=False
    )
```

```python
import functools

import jax
import jax.numpy as jnp
from jax import lax
from jax.experimental import pallas as pl
from jax.experimental.pallas import tpu as pltpu
from jax.sharding import PartitionSpec as P

masked_value = -1e30
lanes = 128
stat_rows = 8
vmem_bytes = 6 * 1024 * 1024
contract_last = (((1,), (1,)), ((), ()))


def swap(value, axis, distance):
    size = lax.axis_size(axis)
    return lax.ppermute(value, axis, [(i, i ^ distance) for i in range(size)])


def ring_next(value, axis, hop=1):
    size = lax.axis_size(axis)
    ring = list(range(0, size, 2)) + list(range(1, size, 2))[::-1]
    return lax.ppermute(value, axis, [(ring[i], ring[(i + hop) % size]) for i in range(size)])


def in_pairs(count, first, step):
    first(0, 0)

    def body(i, _):
        step(0, 2 * i, 2 * i + 1)
        step(1, 2 * i + 1, 2 * i + 2)
        return 0

    lax.fori_loop(0, count // 2 - 1, body, 0)
    step(0, count - 2, count - 1)
    step(1, count - 1, None)


def row_limits(meta_ref, rows_here):
    row = lax.broadcasted_iota(jnp.int32, (rows_here, 1), 0)
    return meta_ref[0] + meta_ref[1] * rows_here + row


def piece_allowed(meta_ref, limit, k, kc, chunk):
    first = (meta_ref[1] ^ k) * kc + meta_ref[2] * chunk
    position = first + lax.broadcasted_iota(jnp.int32, (limit.shape[0], chunk), 1)
    return position <= limit


def spread_weights(cfg, q_ref, wide_ref, qw_ref):
    order, nh, rows_here, hh, depth, kc, chunk, scale = cfg
    rows = rows_here * hh
    eye = (
        lax.broadcasted_iota(jnp.int32, (rows_here, lanes), 0)
        == lax.broadcasted_iota(jnp.int32, (rows_here, lanes), 1)
    ).astype(jnp.float32)
    slab = q_ref[rows:, :].astype(jnp.float32)
    for head in range(hh):
        picked = jnp.sum(slab[head : head + 1] * eye, axis=1, keepdims=True)
        wide_ref[head] = jnp.broadcast_to(picked, (rows_here, lanes))
    for head in range(0, hh, 2):
        at = slice(head * rows_here, (head + 2) * rows_here)
        q = q_ref[at, :].astype(jnp.float32)
        w = wide_ref[head : head + 2].reshape(2 * rows_here, lanes) * scale
        qw_ref[:, at] = (q * w).T.astype(jnp.bfloat16)


def unpack(cfg, message_ref, k, at, keys_ref, keys_t_ref, logits_ref):
    order, nh, rows_here, hh, depth, kc, chunk, scale = cfg
    keys = message_ref[:chunk, :]
    keys_ref[at : at + chunk, :] = keys
    keys_t_ref[:, at : at + chunk] = keys.astype(jnp.float32).T.astype(jnp.bfloat16)
    for i in range(chunk // lanes):
        first = chunk + (chunk // lanes * (k % 2) + i) * rows_here
        column = at + i * lanes
        logits_ref[:, column : column + lanes] = message_ref[first : first + rows_here, :]


def add_scores(cfg, q_ref, wide_ref, keys_t_ref, score_ref, before_ref, start, count, active_ref):
    order, nh, rows_here, hh, depth, kc, chunk, scale = cfg
    rows = rows_here * hh
    side = min(256, count)
    tile = next(size for size in (4 * side, 2 * side, side) if count % size == 0)

    def step(s, _):
        for first in range(0, tile, side):
            local = pl.ds(pl.multiple_of(s * tile + first, side), side)
            columns = pl.ds(pl.multiple_of(start + s * tile + first, side), side)
            dots = jnp.dot(
                q_ref[:rows, :], keys_t_ref[:, columns], preferred_element_type=jnp.float32
            )
            total = [None] * (rows_here // 16)
            for head in range(hh):
                for t in range(rows_here // 16):
                    row = head * rows_here + t * 16
                    w = wide_ref[head, t * 16 : t * 16 + 16, :]
                    w = jnp.concatenate([w] * (side // lanes), axis=1)
                    active = jnp.maximum(dots[row : row + 16, :], 0.0)
                    if active_ref is not None:
                        active_ref[row : row + 16, local] = active.astype(jnp.bfloat16)
                    value = active * w
                    total[t] = value if head == 0 else total[t] + value
            for t, value in enumerate(total):
                at = slice(t * 16, t * 16 + 16)
                value = value * scale
                if before_ref is not None:
                    value = before_ref[at, columns] + value
                score_ref[at, columns] = value
        return 0

    lax.fori_loop(0, count // tile, step, 0)


def forward_early_kernel(cfg, done, pieces, meta_ref, *refs):
    chunk = cfg[6]
    refs = list(refs)
    take = lambda count: [refs.pop(0) for _ in range(count)]
    q_refs = take(2 if done else 1)
    start, count = len(done) * chunk, len(pieces) * chunk
    if done:
        (own_wide_ref,) = take(1)
        part = take(4)
    message_refs = take(len(pieces))
    score_ref, keys_ref, keys_t_ref, logits_ref = take(4)
    active_ref = take(1)[0] if done else None
    qw_ref, wide_ref = take(2)
    spread_weights(cfg, q_refs[-1], wide_ref, qw_ref)
    if done:
        score_ref[:, :start] = part[0][...]
        keys_ref[:start, :] = part[1][...]
        keys_t_ref[:, :start] = part[2][...]
        logits_ref[:, :start] = part[3][...]
    else:
        own_wide_ref = wide_ref
    for i, k in enumerate(pieces):
        unpack(cfg, message_refs[i], k, start + i * chunk, keys_ref, keys_t_ref, logits_ref)
    add_scores(cfg, q_refs[0], own_wide_ref, keys_t_ref, score_ref, None, start, count, None)
    if done:
        count = start + count
        add_scores(cfg, q_refs[1], wide_ref, keys_t_ref, score_ref, score_ref, 0, count, active_ref)


def forward_middle_kernel(cfg, groups, meta_ref, *refs):
    order, nh, rows_here, hh, depth, kc, chunk, scale = cfg
    refs = list(refs)
    take = lambda count: [refs.pop(0) for _ in range(count)]
    q_refs, wide_refs = take(2), take(2)
    new_q_refs = take(nh - 3)
    parts = [take(4) for _ in groups[:-1]]
    message_refs = take(len(groups[-1]))
    whole = take(4)
    score_ref, keys_ref, keys_t_ref, logits_ref = whole
    (last_active_ref,) = take(1)
    active_refs, qw_refs = take(nh - 3), take(nh - 3)
    (wide,) = take(1)
    start = 0
    for group, part in zip(groups, parts):
        end = start + len(group) * chunk
        score_ref[:, start:end] = part[0][...]
        keys_ref[start:end, :] = part[1][...]
        keys_t_ref[:, start:end] = part[2][...]
        logits_ref[:, start:end] = part[3][...]
        start = end
    for i, k in enumerate(groups[-1]):
        unpack(cfg, message_refs[i], k, start + i * chunk, keys_ref, keys_t_ref, logits_ref)
    count = len(groups[-1]) * chunk
    add_scores(cfg, q_refs[0], wide_refs[0], keys_t_ref, score_ref, None, start, count, None)
    add_scores(
        cfg, q_refs[1], wide_refs[1], keys_t_ref, score_ref, score_ref, start, count, last_active_ref
    )
    for q_ref, active_ref, qw_ref in zip(new_q_refs, active_refs, qw_refs):
        spread_weights(cfg, q_ref, wide, qw_ref)
        every = len(order) * chunk
        add_scores(cfg, q_ref, wide, keys_t_ref, score_ref, score_ref, 0, every, active_ref)


def forward_last_kernel(cfg, meta_ref, *refs):
    order, nh, rows_here, hh, depth, kc, chunk, scale = cfg
    q_ref, keys_t_ref, before_ref, logits_ref, score_ref, active_ref, qw_ref, stats_ref, wide = refs
    spread_weights(cfg, q_ref, wide, qw_ref)
    every = len(order) * chunk
    add_scores(cfg, q_ref, wide, keys_t_ref, score_ref, before_ref, 0, every, active_ref)

    limit = row_limits(meta_ref, rows_here)
    lane = lax.broadcasted_iota(jnp.int32, (rows_here, lanes), 1)
    out = jnp.zeros((rows_here, lanes), jnp.float32)

    def piece(i, at):
        if i == 0:
            return score_ref[:, at * chunk : (at + 1) * chunk]
        return logits_ref[:, at * chunk : (at + 1) * chunk].astype(jnp.float32)

    for i in range(2):
        peak = None
        for at, k in enumerate(order):
            allowed = piece_allowed(meta_ref, limit, k, kc, chunk)
            here = jnp.max(jnp.where(allowed, piece(i, at), masked_value), axis=1, keepdims=True)
            peak = here if peak is None else jnp.maximum(peak, here)
        total = None
        for at, k in enumerate(order):
            allowed = piece_allowed(meta_ref, limit, k, kc, chunk)
            here = jnp.where(allowed, jnp.exp(piece(i, at) - peak), 0.0)
            here = jnp.sum(here, axis=1, keepdims=True)
            total = here if total is None else total + here
        out = jnp.where(lane == 2 * i, peak, out)
        out = jnp.where(lane == 2 * i + 1, total, out)
    padded = stats_ref.shape[2]
    if padded > rows_here:
        out = jnp.concatenate([out, jnp.zeros((padded - rows_here, lanes), jnp.float32)], axis=0)
    stats_ref[0] = out.T[:stat_rows]


def score_gradient(cfg, meta_ref, stats, rw_ref, logits_ref, score_ref, cols, grad_ref):
    order, nh, rows_here, hh, depth, kc, chunk, scale = cfg
    for i in range(2):
        peak = functools.reduce(jnp.maximum, [st[2 * i : 2 * i + 1] for st in stats])
        total = functools.reduce(
            jnp.add,
            [st[2 * i + 1 : 2 * i + 2] * jnp.exp(st[2 * i : 2 * i + 1] - peak) for st in stats],
        )
        cols[2 * i : 2 * i + 1, :] = peak
        cols[2 * i + 1 : 2 * i + 2, :] = rw_ref[...] / total
    cols[4:, :] = jnp.zeros((cols.shape[0] - 4, cols.shape[1]), jnp.float32)
    st = cols[...].T[:rows_here]
    limit = row_limits(meta_ref, rows_here)
    for at, k in enumerate(order):
        logits = logits_ref[:, at * chunk : (at + 1) * chunk].astype(jnp.float32)
        score = score_ref[:, at * chunk : (at + 1) * chunk]
        g = jnp.exp(score - st[:, 0:1]) * st[:, 1:2] - jnp.exp(logits - st[:, 2:3]) * st[:, 3:4]
        g = jnp.where(piece_allowed(meta_ref, limit, k, kc, chunk), g, 0.0)
        grad_ref[:, at * chunk : (at + 1) * chunk] = g.astype(jnp.bfloat16)


def backward_kernel(cfg, items, has_before, meta_ref, *refs):
    order, nh, rows_here, hh, depth, kc, chunk, scale = cfg
    n = len(order)
    rows = rows_here * hh
    refs = list(refs)
    take = lambda count: [refs.pop(0) for _ in range(count)]
    is_first = items[0][0] == 1 and items[0][2] is None
    makes_u = any(item[1] for item in items)
    ranges = [item[2] for item in items if item[2] is not None]
    half = ranges[0] if ranges and ranges[0] != "all" else None
    sources = [take(2 if item[0] == 1 else 1) for item in items]
    qw_refs = [take(1)[0] if item[2] is not None else None for item in items]
    (keys_ref,) = take(1)
    if is_first:
        stat_refs = take(nh)
        rw_ref, logits_ref, score_ref = take(3)
    else:
        (grad_ref,) = take(1)
    before_ref = take(1)[0] if has_before else None
    if makes_u:
        (u_ref,) = take(1)
    if ranges:
        kg_refs = take(n // 2 if half == "second" else 1)
    if is_first:
        (grad_ref,) = take(1)
    if half is not None:
        mask_ref, kg_acc = take(2)
    else:
        masks = take(2)
        (u_acc,) = take(1)
    if is_first:
        (cols,) = take(1)
        stats = [ref[0] for ref in stat_refs]
        score_gradient(cfg, meta_ref, stats, rw_ref, logits_ref, score_ref, cols, grad_ref)
    tile = chunk
    chunks = max(1, min(4, hh))
    heads = hh // chunks
    part = heads * rows_here
    side = tile // 2

    todo = []
    for index, (_, is_u, keys_range) in enumerate(items):
        base = 0
        for ref in sources[index]:
            tiles = n // 2 if half is not None else ref.shape[1] // tile
            todo.append((index, is_u, keys_range, ref, base, tiles))
            base += tiles

    for index, is_u, keys_range, source_ref, base, tiles in todo:
        qw_ref = qw_refs[index]
        is_start = index == 0 or items[index - 1][2] is None

        def tile_at(s, first=0, size=tile, base=base):
            if half is None:
                position = s + base
            else:
                position = meta_ref[3 + (n // 2 if half == "second" else 0) + s]
            return pl.ds(pl.multiple_of(position * tile + first, size), size)

        def local(s, first=0, size=tile):
            return pl.ds(pl.multiple_of(s * tile + first, size), size)

        def mask_at(buffer, s, at, first=0, size=tile):
            if half is None:
                return masks[buffer].at[at, first : first + size]
            return mask_ref.at[at, local(s, first, size)]

        def mask_part(buffer, s, i, source_ref=source_ref):
            at = slice(i * part, (i + 1) * part)
            if half is None:
                g = grad_ref[:, tile_at(s)]
                value = source_ref[at, local(s)]
            else:
                g = grad_ref[:, tile_at(s)].astype(jnp.float32)
                value = jnp.dot(
                    source_ref[at, :], keys_ref[:, tile_at(s)], preferred_element_type=jnp.float32
                )
            wide = jnp.broadcast_to(g[None], (heads, rows_here, tile)).reshape(part, tile)
            value = jnp.where(value > 0, wide, jnp.zeros_like(wide))
            mask_at(buffer, s, at)[...] = value.astype(jnp.bfloat16)

        def mask(buffer, s):
            for i in range(chunks):
                mask_part(buffer, s, i)

        def step(buffer, s, following):
            for i in range(chunks):
                if following is not None:
                    mask_part(1 - buffer, following, i)
                if is_u:
                    at = slice(i * part, (i + 1) * part)
                    u_acc[at, :] += jnp.dot(
                        mask_at(buffer, s, at)[...],
                        keys_ref[tile_at(s), :],
                        preferred_element_type=jnp.float32,
                    )
                if keys_range is None or i % (chunks // 2) != chunks // 2 - 1:
                    continue
                first = i // (chunks // 2) * side
                more = jnp.dot(
                    qw_ref[...],
                    mask_at(buffer, s, slice(0, rows), first, side)[...],
                    preferred_element_type=jnp.float32,
                )
                here = tile_at(s, first, side)
                if not is_start:
                    more = kg_refs[0][:, here] + more
                elif before_ref is not None:
                    more = before_ref[:, here] + more
                if half is None:
                    kg_refs[0][:, here] = more
                else:
                    kg_acc[:, local(s, first, side)] = more

        if is_u and base == 0:
            u_acc[...] = jnp.zeros_like(u_acc)
        in_pairs(tiles, mask, step)
        if is_u and (base + tiles) == n:
            u_ref[...] = u_acc[...].astype(u_ref.dtype)

    if half is not None:
        for i in range(n // 2):
            value = kg_acc[:, i * chunk : (i + 1) * chunk].T
            if half == "first":
                kg_refs[0][i] = value.astype(kg_refs[0].dtype)
            else:
                kg_refs[i][...] = value


def query_kernel(cfg, meta_ref, first_ref, second_ref, keys_ref, u_ref, u_acc):
    chunk, pieces = cfg[6], len(cfg[0]) // 2
    u_acc[...] = jnp.zeros_like(u_acc)
    for half, mask_ref in enumerate((first_ref, second_ref)):

        def step(s, _, half=half, mask_ref=mask_ref):
            position = meta_ref[3 + half * pieces + s]
            u_acc[...] += jnp.dot(
                mask_ref[:, pl.ds(pl.multiple_of(s * chunk, chunk), chunk)],
                keys_ref[pl.ds(pl.multiple_of(position * chunk, chunk), chunk), :],
                preferred_element_type=jnp.float32,
            )
            return 0

        lax.fori_loop(0, pieces, step, 0)
    u_ref[...] = u_acc[...]


def prepare_kernel(cfg, meta_ref, query_ref, weights_ref, rw_ref, keys_ref, logits_ref, *refs):
    order, nh, rows_here, hh, depth, kc, chunk, scale = cfg
    sends = len(order) // 2
    rows = rows_here * hh
    parts = chunk // lanes
    message_ref, rw_out_ref, key_refs = refs[0], refs[1], refs[2 : 2 + sends]
    wide, sems = refs[-2], refs[-1]
    share = pl.multiple_of(meta_ref[2] * chunk, chunk)
    copies = []

    def copy(source, target):
        copies.append(pltpu.make_async_copy(source, target, sems.at[len(copies)]))
        copies[-1].start()

    for i in reversed(range(sends)):
        copy(keys_ref.at[pl.ds(share, chunk), :], key_refs[i].at[:chunk, :])
        for core in range(2):
            row = pl.multiple_of((meta_ref[1] ^ (2 * i) ^ core) * rows_here, rows_here)
            for part in range(parts):
                first = chunk + (parts * core + part) * rows_here
                copy(
                    logits_ref.at[pl.ds(row, rows_here), pl.ds(share + part * lanes, lanes)],
                    key_refs[i].at[first : first + rows_here, :],
                )
    every = jnp.broadcast_to(rw_ref[...], (8, rw_ref.shape[1]))
    shift = every.shape[1] - meta_ref[1] * rows_here
    here = pltpu.roll(every, shift, 1)[:1, : rw_out_ref.shape[1]]
    rw_out_ref[...] = here * float(kc * len(order)) ** 0.5
    wide[...] = query_ref[...].astype(jnp.float32)
    for head in range(hh):
        at = slice(head * rows_here, (head + 1) * rows_here)
        message_ref[at, :] = wide[:, head, :].astype(jnp.bfloat16)
    message_ref[rows:, :] = jnp.zeros((message_ref.shape[0] - rows, lanes), jnp.bfloat16)
    message_ref[rows : rows + hh, :rows_here] = weights_ref[...]
    for item in copies:
        item.wait()


def add_kernel(u_ref, moving_ref, out_ref):
    out_ref[...] = (u_ref[...] + moving_ref[...].astype(jnp.float32)).astype(out_ref.dtype)


def finish_kernel(cfg, u_ref, moving_ref, q_ref, query_grad_ref, weight_grad_ref):
    order, nh, rows_here, hh, depth, kc, chunk, scale = cfg
    rows = rows_here * hh
    eye = (
        lax.broadcasted_iota(jnp.int32, (rows_here, lanes), 0)
        == lax.broadcasted_iota(jnp.int32, (rows_here, lanes), 1)
    ).astype(jnp.float32)
    lane = lax.broadcasted_iota(jnp.int32, (lanes, lanes), 1)[:rows_here]
    slab = q_ref[rows:, :].astype(jnp.float32)
    out = jnp.zeros((rows_here, lanes), jnp.float32)
    for head in range(hh):
        at = slice(head * rows_here, (head + 1) * rows_here)
        total = u_ref[at, :] + moving_ref[at, :].astype(jnp.float32)
        w = jnp.sum(slab[head : head + 1] * eye, axis=1, keepdims=True) * scale
        query_grad_ref[:, head, :] = total * w
        along = jnp.sum(total * q_ref[at, :].astype(jnp.float32), axis=1, keepdims=True)
        out = jnp.where(lane == head, along * scale, out)
    if rows_here < lanes:
        out = jnp.concatenate([out, jnp.zeros((lanes - rows_here, lanes), jnp.float32)], axis=0)
    weight_grad_ref[...] = out.T[:hh, :rows_here]


def per_device(query, weights, keys, main_logits, row_weight, offset):
    n = lax.axis_size("ctx")
    nh = lax.axis_size("head")
    c = lax.axis_index("ctx")
    h = lax.axis_index("head")
    rows_here, hh, depth = query.shape
    kc = keys.shape[0]
    chunk = kc // nh
    rows = rows_here * hh
    scale = depth ** (-0.5)
    bf16, f32 = jnp.bfloat16, jnp.float32

    groups = [
        [1, 0],
        list(range(3, n - 2, 2)) + list(range(2, n - 2, 2)),
        [n - 1, n - 2],
    ]
    order = sum(groups, [])
    cfg = (order, nh, rows_here, hh, depth, kc, chunk, scale)
    smem = pl.BlockSpec(memory_space=pltpu.SMEM)
    vmem = pl.BlockSpec(memory_space=pltpu.VMEM)
    padded = -(-rows_here // lanes) * lanes
    table = [order.index(k) for k in list(range(1, n, 2)) + list(range(0, n, 2))]
    meta = jnp.concatenate(
        [offset, jnp.stack([c, h]).astype(jnp.int32), jnp.array(table, jnp.int32)]
    )

    far = lambda x: pltpu.with_memory_space_constraint(x, pltpu.HBM)

    slab_rows = -(-hh // 16) * 16
    parts = chunk // lanes
    message, rw, *key_messages = pl.pallas_call(
        functools.partial(prepare_kernel, cfg),
        out_shape=[
            jax.ShapeDtypeStruct((rows + slab_rows, depth), bf16),
            jax.ShapeDtypeStruct((1, padded), f32),
        ]
        + [jax.ShapeDtypeStruct((chunk + 2 * parts * rows_here, depth), bf16)] * (n // 2),
        in_specs=[smem, vmem, vmem, vmem] + [pl.BlockSpec(memory_space=pltpu.HBM)] * 2,
        out_specs=[vmem] * (2 + n // 2),
        scratch_shapes=[
            pltpu.VMEM((rows_here, hh, depth), f32),
            pltpu.SemaphoreType.DMA((n // 2 * (1 + 2 * parts),)),
        ],
        compiler_params=pltpu.CompilerParams(vmem_limit_bytes=vmem_bytes),
        cost_estimate=pl.CostEstimate(
            flops=rows * depth, bytes_accessed=4 * 1024 * 1024, transcendentals=0
        ),
        name="prepare",
    )(meta, far(query), far(weights.T), far(row_weight[None, :]), far(keys), far(main_logits))
    q_blocks = [message] * nh
    for hop in range(1, nh // 2 + 1):
        q_blocks[hop] = ring_next(q_blocks[hop - 1], "head")
        if nh - hop > hop:
            q_blocks[nh - hop] = ring_next(q_blocks[(nh - hop + 1) % nh], "head", -1)
    arrival = [1]
    for hop in range(1, nh // 2 + 1):
        arrival += [j for j in sorted({hop, nh - hop}) if j not in arrival]

    k_pieces = [None] * n
    k_pieces[0::2] = [key_messages[0]] + [
        swap(key_messages[k // 2], "ctx", k) for k in range(2, n, 2)
    ]
    k_pieces[1] = swap(k_pieces[0], "ctx", 1)
    total_keys = n * chunk
    macs = rows * total_keys * depth
    tile = chunk

    def call(kernel, operands, out_shape, scratch, products, name, aliases={}):
        return pl.pallas_call(
            kernel,
            out_shape=out_shape,
            input_output_aliases=aliases,
            in_specs=[smem] + [vmem] * len(operands),
            out_specs=[vmem] * len(out_shape),
            scratch_shapes=scratch,
            compiler_params=pltpu.CompilerParams(vmem_limit_bytes=vmem_bytes),
            cost_estimate=pl.CostEstimate(
                flops=int(4 * products * macs),
                bytes_accessed=int(4 * products * 2**20),
                transcendentals=0,
            ),
            name=name,
        )(meta, *operands)

    near = lambda x: pltpu.with_memory_space_constraint(x, pltpu.VMEM)

    wide_shape = pltpu.VMEM((hh, rows_here, lanes), f32)
    qw_shape = pltpu.VMEM((depth, rows), bf16)

    def keys_shapes(count):
        return [
            pltpu.VMEM((rows_here, count), f32),
            pltpu.VMEM((count, depth), bf16),
            pltpu.VMEM((depth, count), bf16),
            pltpu.VMEM((rows_here, count), bf16),
        ]

    nears = lambda xs: [near(x) for x in xs]
    early, qw, wides = [], [], []
    for i, group in enumerate(groups[:2]):
        if i == 1:
            far_even = range(2, n - 2, 2)
            wides[0], *came = lax.optimization_barrier((wides[0], *(k_pieces[k] for k in far_even)))
            for k, piece in zip(far_even, came):
                k_pieces[k], k_pieces[k + 1] = piece, swap(piece, "ctx", 1)
        count = (len(group) + i * len(groups[0])) * chunk
        outs = call(
            functools.partial(forward_early_kernel, cfg, groups[0] if i == 1 else [], group),
            q_blocks[: i + 1] + nears(wides) + nears(early) + [k_pieces[k] for k in group],
            keys_shapes(count) + [pltpu.VMEM((rows, count), bf16)] * i + [qw_shape, wide_shape],
            [],
            0.001,
            f"forward_early_{i}",
        )
        early = list(outs[:4])
        qw.append(outs[-2])
        wides.append(outs[-1])
    early_active = outs[4]
    early[0], came = lax.optimization_barrier((early[0], k_pieces[n - 2]))
    k_pieces[n - 2], k_pieces[n - 1] = came, swap(came, "ctx", 1)
    last = len(groups[2]) * chunk
    outs = call(
        functools.partial(forward_middle_kernel, cfg, [groups[0] + groups[1], groups[2]]),
        q_blocks[:2]
        + nears(wides)
        + [q_blocks[j] for j in arrival[1:-1]]
        + nears(early)
        + [k_pieces[k] for k in groups[2]],
        keys_shapes(total_keys)
        + [pltpu.VMEM((rows, last), bf16)]
        + [pltpu.VMEM((rows, total_keys), bf16)] * (nh - 3)
        + [qw_shape] * (nh - 3),
        [pltpu.VMEM((hh, rows_here, lanes), f32)],
        nh - 2.5,
        "forward_middle",
    )
    score, keys_all, keys_t, logits = outs[:4]
    active = {1: [early_active, outs[4]]}
    qw = dict(enumerate(qw))
    for i, j in enumerate(arrival[1:-1]):
        active[j], qw[j] = [outs[5 + i]], outs[5 + nh - 3 + i]
    score, last_active, last_qw, stats = call(
        functools.partial(forward_last_kernel, cfg),
        [q_blocks[arrival[-1]], near(keys_t), near(score), near(logits)],
        [
            pltpu.VMEM((rows_here, total_keys), f32),
            pltpu.VMEM((rows, total_keys), bf16),
            qw_shape,
            jax.ShapeDtypeStruct((1, stat_rows, padded), f32),
        ],
        [pltpu.VMEM((hh, rows_here, lanes), f32)],
        1,
        "forward_last",
        {3: 0},
    )
    active[arrival[-1]], qw[arrival[-1]] = [last_active], last_qw

    all_stats = [stats] + [swap(stats, "head", j) for j in range(1, nh)]

    grad = kg = None

    def backward(items, name):
        nonlocal grad, kg
        is_first = grad is None
        ranges = [item[2] for item in items if item[2] is not None]
        makes_u = any(item[1] for item in items)
        has_before = bool(ranges) and kg is not None
        halved = ranges != [] and ranges[0] != "all"
        operands = []
        for item in items:
            operands += [q_blocks[0]] if halved else nears(active[item[0]])
        operands += [near(qw[item[0]]) for item in items if item[2] is not None]
        operands += [near(keys_t if halved else keys_all)]
        operands += all_stats + [rw, near(logits), near(score)] if is_first else [near(grad)]
        aliases = {}
        out_shape = [jax.ShapeDtypeStruct((rows, depth), bf16 if is_first else f32)]
        out_shape = out_shape if makes_u else []
        scratch = [pltpu.VMEM((rows, tile), bf16)] * 2 + [pltpu.VMEM((rows, depth), f32)]
        if not halved:
            if ranges:
                if has_before:
                    aliases = {len(operands) + 1: len(out_shape)}
                out_shape += [pltpu.VMEM((depth, total_keys), f32)]
        else:
            if ranges[0] == "first":
                out_shape += [jax.ShapeDtypeStruct((n // 2, chunk, depth), bf16)]
            else:
                out_shape += [jax.ShapeDtypeStruct((chunk, depth), f32)] * (n // 2)
            out_shape += [pltpu.VMEM((rows, total_keys // 2), bf16)]
            scratch = [pltpu.VMEM((depth, total_keys // 2), f32)]
        if has_before:
            operands += [near(kg)]
        if is_first:
            out_shape += [pltpu.VMEM((rows_here, total_keys), bf16)]
            scratch += [pltpu.VMEM((padded, lanes), f32)]
        kernel = functools.partial(backward_kernel, cfg, items, has_before)
        products = 1 if halved else makes_u + len(ranges)
        outs = call(kernel, operands, out_shape, scratch, products, name, aliases)
        if is_first:
            grad = outs[-1]
        if ranges and ranges[0] == "all":
            kg = outs[1 if makes_u else 0]
        return outs

    part = backward([(1, True, None)], "backward_1")[0]
    moving = ring_next(part, "head")
    for j in range(2, nh):
        items = [(j - 1, False, "all"), (j, True, "all" if j == nh - 1 else None)]
        part = backward(items, f"backward_{j}")[0]
        part = pl.pallas_call(
            add_kernel,
            out_shape=jax.ShapeDtypeStruct((rows, depth), bf16),
            in_specs=[vmem] * 2,
            out_specs=vmem,
            compiler_params=pltpu.CompilerParams(vmem_limit_bytes=vmem_bytes),
            cost_estimate=pl.CostEstimate(
                flops=rows * depth, bytes_accessed=8 * rows * depth, transcendentals=0
            ),
            name=f"add_{j}",
        )(part, moving)
        kg, part = lax.optimization_barrier((kg, part))
        moving = ring_next(part, "head")

    odd, mask_first = backward([(0, False, "first")], "backward_0_first")
    other = swap(odd, "ctx", 1)
    *even, mask_second = backward([(0, False, "second")], "backward_0_second")
    even = [even[i] + other[i].astype(f32) for i in range(n // 2)]
    key_grad = even[0]
    sends = [even[i].astype(bf16) for i in range(1, n // 2)]
    keys_all, *sends = lax.optimization_barrier((keys_all, *sends))
    for i in range(1, n // 2):
        key_grad = key_grad + swap(sends[i - 1], "ctx", 2 * i).astype(f32)
    (u_mine,) = call(
        functools.partial(query_kernel, cfg),
        [near(mask_first), near(mask_second), near(keys_all)],
        [jax.ShapeDtypeStruct((rows, depth), f32)],
        [pltpu.VMEM((rows, depth), f32)],
        1,
        "backward_0",
    )

    query_grad, weight_grad = pl.pallas_call(
        functools.partial(finish_kernel, cfg),
        out_shape=[
            jax.ShapeDtypeStruct((rows_here, hh, depth), f32),
            jax.ShapeDtypeStruct((hh, rows_here), f32),
        ],
        in_specs=[vmem] * 3,
        out_specs=[vmem] * 2,
        compiler_params=pltpu.CompilerParams(vmem_limit_bytes=vmem_bytes),
        cost_estimate=pl.CostEstimate(
            flops=8 * rows * depth, bytes_accessed=14 * rows * depth, transcendentals=0
        ),
        name="finish",
    )(u_mine, moving, q_blocks[0])
    return query_grad, key_grad, weight_grad.T


def solution(mesh):
    in_specs = (P("ctx", "head", None), P("ctx", "head"), P("ctx", None), P(None, "ctx"), P(), P())
    out_specs = (P("ctx", "head", None), P(("ctx", "head"), None), P("ctx", "head"))
    return jax.shard_map(
        per_device, mesh=mesh, in_specs=in_specs, out_specs=out_specs, check_vma=False
    )
```

```python
import functools

import jax
import jax.numpy as jnp
from jax import lax
from jax.experimental import pallas as pl
from jax.experimental.pallas import tpu as pltpu
from jax.sharding import PartitionSpec as P

masked_value = -1e30
lanes = 128
stat_rows = 8
vmem_bytes = 6 * 1024 * 1024
contract_last = (((1,), (1,)), ((), ()))


def swap(value, axis, distance):
    size = lax.axis_size(axis)
    return lax.ppermute(value, axis, [(i, i ^ distance) for i in range(size)])


def ring_next(value, axis, hop=1):
    size = lax.axis_size(axis)
    ring = list(range(0, size, 2)) + list(range(1, size, 2))[::-1]
    return lax.ppermute(value, axis, [(ring[i], ring[(i + hop) % size]) for i in range(size)])


def in_pairs(count, first, step):
    first(0, 0)

    def body(i, _):
        step(0, 2 * i, 2 * i + 1)
        step(1, 2 * i + 1, 2 * i + 2)
        return 0

    lax.fori_loop(0, count // 2 - 1, body, 0)
    step(0, count - 2, count - 1)
    step(1, count - 1, None)


def row_limits(meta_ref, rows_here):
    row = lax.broadcasted_iota(jnp.int32, (rows_here, 1), 0)
    return meta_ref[0] + meta_ref[1] * rows_here + row


def piece_allowed(meta_ref, limit, k, kc, chunk):
    first = (meta_ref[1] ^ k) * kc + meta_ref[2] * chunk
    position = first + lax.broadcasted_iota(jnp.int32, (limit.shape[0], chunk), 1)
    return position <= limit


def spread_weights(cfg, q_ref, wide_ref, qw_ref):
    order, nh, rows_here, hh, depth, kc, chunk, scale = cfg
    rows = rows_here * hh
    eye = (
        lax.broadcasted_iota(jnp.int32, (rows_here, lanes), 0)
        == lax.broadcasted_iota(jnp.int32, (rows_here, lanes), 1)
    ).astype(jnp.float32)
    slab = q_ref[rows:, :].astype(jnp.float32)
    for head in range(hh):
        picked = jnp.sum(slab[head : head + 1] * eye, axis=1, keepdims=True)
        wide_ref[head] = jnp.broadcast_to(picked, (rows_here, lanes))
    for head in range(0, hh, 2):
        at = slice(head * rows_here, (head + 2) * rows_here)
        q = q_ref[at, :].astype(jnp.float32)
        w = wide_ref[head : head + 2].reshape(2 * rows_here, lanes) * scale
        qw_ref[:, at] = (q * w).T.astype(jnp.bfloat16)


def unpack(cfg, message_ref, k, at, keys_ref, keys_t_ref, logits_ref):
    order, nh, rows_here, hh, depth, kc, chunk, scale = cfg
    keys = message_ref[:chunk, :]
    keys_ref[at : at + chunk, :] = keys
    keys_t_ref[:, at : at + chunk] = keys.astype(jnp.float32).T.astype(jnp.bfloat16)
    for i in range(chunk // lanes):
        first = chunk + (chunk // lanes * (k % 2) + i) * rows_here
        column = at + i * lanes
        logits_ref[:, column : column + lanes] = message_ref[first : first + rows_here, :]


def add_scores(cfg, q_ref, wide_ref, keys_t_ref, score_ref, before_ref, start, count, active_ref):
    order, nh, rows_here, hh, depth, kc, chunk, scale = cfg
    rows = rows_here * hh
    side = min(256, count)
    tile = next(size for size in (4 * side, 2 * side, side) if count % size == 0)

    def step(s, _):
        for first in range(0, tile, side):
            local = pl.ds(pl.multiple_of(s * tile + first, side), side)
            columns = pl.ds(pl.multiple_of(start + s * tile + first, side), side)
            dots = jnp.dot(
                q_ref[:rows, :], keys_t_ref[:, columns], preferred_element_type=jnp.float32
            )
            total = [None] * (rows_here // 16)
            for head in range(hh):
                for t in range(rows_here // 16):
                    row = head * rows_here + t * 16
                    w = wide_ref[head, t * 16 : t * 16 + 16, :]
                    w = jnp.concatenate([w] * (side // lanes), axis=1)
                    active = jnp.maximum(dots[row : row + 16, :], 0.0)
                    if active_ref is not None:
                        active_ref[row : row + 16, local] = active.astype(jnp.bfloat16)
                    value = active * w
                    total[t] = value if head == 0 else total[t] + value
            for t, value in enumerate(total):
                at = slice(t * 16, t * 16 + 16)
                value = value * scale
                if before_ref is not None:
                    value = before_ref[at, columns] + value
                score_ref[at, columns] = value
        return 0

    lax.fori_loop(0, count // tile, step, 0)


def forward_early_kernel(cfg, done, pieces, meta_ref, *refs):
    chunk = cfg[6]
    refs = list(refs)
    take = lambda count: [refs.pop(0) for _ in range(count)]
    q_refs = take(2 if done else 1)
    start, count = len(done) * chunk, len(pieces) * chunk
    if done:
        (own_wide_ref,) = take(1)
        part = take(4)
    message_refs = take(len(pieces))
    score_ref, keys_ref, keys_t_ref, logits_ref = take(4)
    active_ref = take(1)[0] if done else None
    qw_ref, wide_ref = take(2)
    spread_weights(cfg, q_refs[-1], wide_ref, qw_ref)
    if done:
        score_ref[:, :start] = part[0][...]
        keys_ref[:start, :] = part[1][...]
        keys_t_ref[:, :start] = part[2][...]
        logits_ref[:, :start] = part[3][...]
    else:
        own_wide_ref = wide_ref
    for i, k in enumerate(pieces):
        unpack(cfg, message_refs[i], k, start + i * chunk, keys_ref, keys_t_ref, logits_ref)
    add_scores(cfg, q_refs[0], own_wide_ref, keys_t_ref, score_ref, None, start, count, None)
    if done:
        count = start + count
        add_scores(cfg, q_refs[1], wide_ref, keys_t_ref, score_ref, score_ref, 0, count, active_ref)


def forward_middle_kernel(cfg, groups, meta_ref, *refs):
    order, nh, rows_here, hh, depth, kc, chunk, scale = cfg
    refs = list(refs)
    take = lambda count: [refs.pop(0) for _ in range(count)]
    q_refs, wide_refs = take(2), take(2)
    new_q_refs = take(nh - 3)
    parts = [take(4) for _ in groups[:-1]]
    message_refs = take(len(groups[-1]))
    whole = take(4)
    score_ref, keys_ref, keys_t_ref, logits_ref = whole
    (last_active_ref,) = take(1)
    active_refs, qw_refs = take(nh - 3), take(nh - 3)
    (wide,) = take(1)
    start = 0
    for group, part in zip(groups, parts):
        end = start + len(group) * chunk
        score_ref[:, start:end] = part[0][...]
        keys_ref[start:end, :] = part[1][...]
        keys_t_ref[:, start:end] = part[2][...]
        logits_ref[:, start:end] = part[3][...]
        start = end
    for i, k in enumerate(groups[-1]):
        unpack(cfg, message_refs[i], k, start + i * chunk, keys_ref, keys_t_ref, logits_ref)
    count = len(groups[-1]) * chunk
    add_scores(cfg, q_refs[0], wide_refs[0], keys_t_ref, score_ref, None, start, count, None)
    add_scores(
        cfg, q_refs[1], wide_refs[1], keys_t_ref, score_ref, score_ref, start, count, last_active_ref
    )
    for q_ref, active_ref, qw_ref in zip(new_q_refs, active_refs, qw_refs):
        spread_weights(cfg, q_ref, wide, qw_ref)
        every = len(order) * chunk
        add_scores(cfg, q_ref, wide, keys_t_ref, score_ref, score_ref, 0, every, active_ref)


def forward_last_kernel(cfg, meta_ref, *refs):
    order, nh, rows_here, hh, depth, kc, chunk, scale = cfg
    q_ref, keys_t_ref, before_ref, logits_ref, score_ref, active_ref, qw_ref, stats_ref, wide = refs
    spread_weights(cfg, q_ref, wide, qw_ref)
    every = len(order) * chunk
    add_scores(cfg, q_ref, wide, keys_t_ref, score_ref, before_ref, 0, every, active_ref)

    limit = row_limits(meta_ref, rows_here)
    lane = lax.broadcasted_iota(jnp.int32, (rows_here, lanes), 1)
    out = jnp.zeros((rows_here, lanes), jnp.float32)

    def piece(i, at):
        if i == 0:
            return score_ref[:, at * chunk : (at + 1) * chunk]
        return logits_ref[:, at * chunk : (at + 1) * chunk].astype(jnp.float32)

    for i in range(2):
        peak = None
        for at, k in enumerate(order):
            allowed = piece_allowed(meta_ref, limit, k, kc, chunk)
            here = jnp.max(jnp.where(allowed, piece(i, at), masked_value), axis=1, keepdims=True)
            peak = here if peak is None else jnp.maximum(peak, here)
        total = None
        for at, k in enumerate(order):
            allowed = piece_allowed(meta_ref, limit, k, kc, chunk)
            here = jnp.where(allowed, jnp.exp(piece(i, at) - peak), 0.0)
            here = jnp.sum(here, axis=1, keepdims=True)
            total = here if total is None else total + here
        out = jnp.where(lane == 2 * i, peak, out)
        out = jnp.where(lane == 2 * i + 1, total, out)
    padded = stats_ref.shape[2]
    if padded > rows_here:
        out = jnp.concatenate([out, jnp.zeros((padded - rows_here, lanes), jnp.float32)], axis=0)
    stats_ref[0] = out.T[:stat_rows]


def score_gradient(cfg, meta_ref, stats, rw_ref, logits_ref, score_ref, cols, grad_ref):
    order, nh, rows_here, hh, depth, kc, chunk, scale = cfg
    for i in range(2):
        peak = functools.reduce(jnp.maximum, [st[2 * i : 2 * i + 1] for st in stats])
        total = functools.reduce(
            jnp.add,
            [st[2 * i + 1 : 2 * i + 2] * jnp.exp(st[2 * i : 2 * i + 1] - peak) for st in stats],
        )
        cols[2 * i : 2 * i + 1, :] = peak
        cols[2 * i + 1 : 2 * i + 2, :] = rw_ref[...] / total
    cols[4:, :] = jnp.zeros((cols.shape[0] - 4, cols.shape[1]), jnp.float32)
    st = cols[...].T[:rows_here]
    limit = row_limits(meta_ref, rows_here)
    for at, k in enumerate(order):
        logits = logits_ref[:, at * chunk : (at + 1) * chunk].astype(jnp.float32)
        score = score_ref[:, at * chunk : (at + 1) * chunk]
        g = jnp.exp(score - st[:, 0:1]) * st[:, 1:2] - jnp.exp(logits - st[:, 2:3]) * st[:, 3:4]
        g = jnp.where(piece_allowed(meta_ref, limit, k, kc, chunk), g, 0.0)
        grad_ref[:, at * chunk : (at + 1) * chunk] = g.astype(jnp.bfloat16)


def backward_kernel(cfg, items, has_before, meta_ref, *refs):
    order, nh, rows_here, hh, depth, kc, chunk, scale = cfg
    n = len(order)
    rows = rows_here * hh
    refs = list(refs)
    take = lambda count: [refs.pop(0) for _ in range(count)]
    is_first = items[0][0] == 1 and items[0][2] is None
    makes_u = any(item[1] for item in items)
    ranges = [item[2] for item in items if item[2] is not None]
    half = ranges[0] if ranges and ranges[0] != "all" else None
    sources = [take(2 if item[0] == 1 else 1) for item in items]
    qw_refs = [take(1)[0] if item[2] is not None else None for item in items]
    (keys_ref,) = take(1)
    if is_first:
        stat_refs = take(nh)
        rw_ref, logits_ref, score_ref = take(3)
    else:
        (grad_ref,) = take(1)
    before_ref = take(1)[0] if has_before else None
    if makes_u:
        (u_ref,) = take(1)
    if ranges:
        kg_refs = take(n // 2 if half == "second" else 1)
    if is_first:
        (grad_ref,) = take(1)
    if half is not None:
        mask_ref, kg_acc = take(2)
    else:
        masks = take(2)
        (u_acc,) = take(1)
    if is_first:
        (cols,) = take(1)
        stats = [ref[0] for ref in stat_refs]
        score_gradient(cfg, meta_ref, stats, rw_ref, logits_ref, score_ref, cols, grad_ref)
    tile = chunk
    chunks = max(1, min(4, hh))
    heads = hh // chunks
    part = heads * rows_here
    side = tile // 2

    todo = []
    for index, (_, is_u, keys_range) in enumerate(items):
        base = 0
        for ref in sources[index]:
            tiles = n // 2 if half is not None else ref.shape[1] // tile
            todo.append((index, is_u, keys_range, ref, base, tiles))
            base += tiles

    for index, is_u, keys_range, source_ref, base, tiles in todo:
        qw_ref = qw_refs[index]
        is_start = index == 0 or items[index - 1][2] is None

        def tile_at(s, first=0, size=tile, base=base):
            if half is None:
                position = s + base
            else:
                position = meta_ref[3 + (n // 2 if half == "second" else 0) + s]
            return pl.ds(pl.multiple_of(position * tile + first, size), size)

        def local(s, first=0, size=tile):
            return pl.ds(pl.multiple_of(s * tile + first, size), size)

        def mask_at(buffer, s, at, first=0, size=tile):
            if half is None:
                return masks[buffer].at[at, first : first + size]
            return mask_ref.at[at, local(s, first, size)]

        def mask_part(buffer, s, i, source_ref=source_ref):
            at = slice(i * part, (i + 1) * part)
            g = grad_ref[:, tile_at(s)]
            value = source_ref[at, local(s)]
            wide = jnp.broadcast_to(g[None], (heads, rows_here, tile)).reshape(part, tile)
            value = jnp.where(value > 0, wide, jnp.zeros_like(wide))
            mask_at(buffer, s, at)[...] = value.astype(jnp.bfloat16)

        def mask(buffer, s):
            for i in range(chunks):
                mask_part(buffer, s, i)

        def step(buffer, s, following):
            for i in range(chunks):
                if following is not None:
                    mask_part(1 - buffer, following, i)
                if is_u:
                    at = slice(i * part, (i + 1) * part)
                    u_acc[at, :] += jnp.dot(
                        mask_at(buffer, s, at)[...],
                        keys_ref[tile_at(s), :],
                        preferred_element_type=jnp.float32,
                    )
                if keys_range is None or i % (chunks // 2) != chunks // 2 - 1:
                    continue
                first = i // (chunks // 2) * side
                more = jnp.dot(
                    qw_ref[...],
                    mask_at(buffer, s, slice(0, rows), first, side)[...],
                    preferred_element_type=jnp.float32,
                )
                here = tile_at(s, first, side)
                if not is_start:
                    more = kg_refs[0][:, here] + more
                elif before_ref is not None:
                    more = before_ref[:, here] + more
                if half is None:
                    kg_refs[0][:, here] = more
                else:
                    kg_acc[:, local(s, first, side)] = more

        if is_u and base == 0:
            u_acc[...] = jnp.zeros_like(u_acc)
        in_pairs(tiles, mask, step)
        if is_u and (base + tiles) == n:
            u_ref[...] = u_acc[...].astype(u_ref.dtype)

    if half is not None:
        for i in range(n // 2):
            value = kg_acc[:, i * chunk : (i + 1) * chunk].T
            if half == "first":
                kg_refs[0][i] = value.astype(kg_refs[0].dtype)
            else:
                kg_refs[i][...] = value


def own_active_kernel(cfg, meta_ref, q_ref, keys_t_ref, first_ref, second_ref):
    order, nh, rows_here, hh, depth, kc, chunk, scale = cfg
    pieces = len(order) // 2
    side = min(256, chunk)
    for half, active_ref in enumerate((first_ref, second_ref)):

        def step(s, _, half=half, active_ref=active_ref):
            position = meta_ref[3 + half * pieces + s]
            for first in range(0, chunk, side):
                columns = pl.ds(pl.multiple_of(position * chunk + first, side), side)
                local = pl.ds(pl.multiple_of(s * chunk + first, side), side)
                dots = jnp.dot(
                    q_ref[: rows_here * hh, :],
                    keys_t_ref[:, columns],
                    preferred_element_type=jnp.float32,
                )
                active_ref[:, local] = jnp.maximum(dots, 0.0).astype(jnp.bfloat16)
            return 0

        lax.fori_loop(0, pieces, step, 0)


def query_kernel(cfg, meta_ref, first_ref, second_ref, keys_ref, u_ref, u_acc):
    chunk, pieces = cfg[6], len(cfg[0]) // 2
    u_acc[...] = jnp.zeros_like(u_acc)
    for half, mask_ref in enumerate((first_ref, second_ref)):

        def step(s, _, half=half, mask_ref=mask_ref):
            position = meta_ref[3 + half * pieces + s]
            u_acc[...] += jnp.dot(
                mask_ref[:, pl.ds(pl.multiple_of(s * chunk, chunk), chunk)],
                keys_ref[pl.ds(pl.multiple_of(position * chunk, chunk), chunk), :],
                preferred_element_type=jnp.float32,
            )
            return 0

        lax.fori_loop(0, pieces, step, 0)
    u_ref[...] = u_acc[...]


def prepare_kernel(cfg, query_ref, weights_ref, rw_ref, keys_ref, logits_ref, *refs):
    order, nh, rows_here, hh, depth, kc, chunk, scale = cfg
    sends = len(order) // 2
    rows = rows_here * hh
    parts = chunk // lanes
    message_ref, rw_out_ref, key_refs = refs[0], refs[1], refs[2 : 2 + sends]
    wide, sems = refs[-2], refs[-1]
    share = pl.multiple_of(lax.axis_index("head") * chunk, chunk)
    copies = []

    def copy(source, target):
        copies.append(pltpu.make_async_copy(source, target, sems.at[len(copies)]))
        copies[-1].start()

    for i in reversed(range(sends)):
        copy(keys_ref.at[pl.ds(share, chunk), :], key_refs[i].at[:chunk, :])
        for core in range(2):
            row = pl.multiple_of((lax.axis_index("ctx") ^ (2 * i) ^ core) * rows_here, rows_here)
            for part in range(parts):
                first = chunk + (parts * core + part) * rows_here
                copy(
                    logits_ref.at[pl.ds(row, rows_here), pl.ds(share + part * lanes, lanes)],
                    key_refs[i].at[first : first + rows_here, :],
                )
    every = jnp.broadcast_to(rw_ref[...], (8, rw_ref.shape[1]))
    shift = every.shape[1] - lax.axis_index("ctx") * rows_here
    here = pltpu.roll(every, shift, 1)[:1, : rw_out_ref.shape[1]]
    rw_out_ref[...] = here * float(kc * len(order)) ** 0.5
    wide[...] = query_ref[...].astype(jnp.float32)
    for head in range(hh):
        at = slice(head * rows_here, (head + 1) * rows_here)
        message_ref[at, :] = wide[:, head, :].astype(jnp.bfloat16)
    message_ref[rows:, :] = jnp.zeros((message_ref.shape[0] - rows, lanes), jnp.bfloat16)
    message_ref[rows : rows + hh, :rows_here] = weights_ref[...]
    for item in copies:
        item.wait()


def add_kernel(u_ref, moving_ref, out_ref):
    out_ref[...] = (u_ref[...] + moving_ref[...].astype(jnp.float32)).astype(out_ref.dtype)


def finish_kernel(cfg, u_ref, moving_ref, q_ref, query_grad_ref, weight_grad_ref):
    order, nh, rows_here, hh, depth, kc, chunk, scale = cfg
    rows = rows_here * hh
    eye = (
        lax.broadcasted_iota(jnp.int32, (rows_here, lanes), 0)
        == lax.broadcasted_iota(jnp.int32, (rows_here, lanes), 1)
    ).astype(jnp.float32)
    lane = lax.broadcasted_iota(jnp.int32, (lanes, lanes), 1)[:rows_here]
    slab = q_ref[rows:, :].astype(jnp.float32)
    out = jnp.zeros((rows_here, lanes), jnp.float32)
    for head in range(hh):
        at = slice(head * rows_here, (head + 1) * rows_here)
        total = u_ref[at, :] + moving_ref[at, :].astype(jnp.float32)
        w = jnp.sum(slab[head : head + 1] * eye, axis=1, keepdims=True) * scale
        query_grad_ref[:, head, :] = total * w
        along = jnp.sum(total * q_ref[at, :].astype(jnp.float32), axis=1, keepdims=True)
        out = jnp.where(lane == head, along * scale, out)
    if rows_here < lanes:
        out = jnp.concatenate([out, jnp.zeros((lanes - rows_here, lanes), jnp.float32)], axis=0)
    weight_grad_ref[...] = out.T[:hh, :rows_here]


def per_device(query, weights, keys, main_logits, row_weight, offset):
    n = lax.axis_size("ctx")
    nh = lax.axis_size("head")
    c = lax.axis_index("ctx")
    h = lax.axis_index("head")
    rows_here, hh, depth = query.shape
    kc = keys.shape[0]
    chunk = kc // nh
    rows = rows_here * hh
    scale = depth ** (-0.5)
    bf16, f32 = jnp.bfloat16, jnp.float32

    groups = [
        [1, 0],
        list(range(3, n - 2, 2)) + list(range(2, n - 2, 2)),
        [n - 1, n - 2],
    ]
    order = sum(groups, [])
    cfg = (order, nh, rows_here, hh, depth, kc, chunk, scale)
    smem = pl.BlockSpec(memory_space=pltpu.SMEM)
    vmem = pl.BlockSpec(memory_space=pltpu.VMEM)
    padded = -(-rows_here // lanes) * lanes
    table = [order.index(k) for k in list(range(1, n, 2)) + list(range(0, n, 2))]
    meta = jnp.concatenate(
        [offset, jnp.stack([c, h]).astype(jnp.int32), jnp.array(table, jnp.int32)]
    )

    far = lambda x: pltpu.with_memory_space_constraint(x, pltpu.HBM)

    slab_rows = -(-hh // 16) * 16
    parts = chunk // lanes
    message, rw, *key_messages = pl.pallas_call(
        functools.partial(prepare_kernel, cfg),
        out_shape=[
            jax.ShapeDtypeStruct((rows + slab_rows, depth), bf16),
            jax.ShapeDtypeStruct((1, padded), f32),
        ]
        + [jax.ShapeDtypeStruct((chunk + 2 * parts * rows_here, depth), bf16)] * (n // 2),
        in_specs=[vmem, vmem, vmem] + [pl.BlockSpec(memory_space=pltpu.HBM)] * 2,
        out_specs=[vmem] * (2 + n // 2),
        scratch_shapes=[
            pltpu.VMEM((rows_here, hh, depth), f32),
            pltpu.SemaphoreType.DMA((n // 2 * (1 + 2 * parts),)),
        ],
        compiler_params=pltpu.CompilerParams(vmem_limit_bytes=vmem_bytes),
        cost_estimate=pl.CostEstimate(
            flops=rows * depth, bytes_accessed=4 * 1024 * 1024, transcendentals=0
        ),
        name="prepare",
    )(far(query), far(weights.T), far(row_weight[None, :]), far(keys), far(main_logits))
    q_blocks = [message] * nh
    for hop in range(1, nh // 2 + 1):
        q_blocks[hop] = ring_next(q_blocks[hop - 1], "head")
        if nh - hop > hop:
            q_blocks[nh - hop] = ring_next(q_blocks[(nh - hop + 1) % nh], "head", -1)
    arrival = [1]
    for hop in range(1, nh // 2 + 1):
        arrival += [j for j in sorted({hop, nh - hop}) if j not in arrival]

    k_pieces = [None] * n
    k_pieces[0::2] = [key_messages[0]] + [
        swap(key_messages[k // 2], "ctx", k) for k in range(2, n, 2)
    ]
    k_pieces[1] = swap(k_pieces[0], "ctx", 1)
    total_keys = n * chunk
    macs = rows * total_keys * depth
    tile = chunk

    def call(kernel, operands, out_shape, scratch, products, name, aliases={}):
        return pl.pallas_call(
            kernel,
            out_shape=out_shape,
            input_output_aliases=aliases,
            in_specs=[smem] + [vmem] * len(operands),
            out_specs=[vmem] * len(out_shape),
            scratch_shapes=scratch,
            compiler_params=pltpu.CompilerParams(vmem_limit_bytes=vmem_bytes),
            cost_estimate=pl.CostEstimate(
                flops=int(4 * products * macs),
                bytes_accessed=int(4 * products * 2**20),
                transcendentals=0,
            ),
            name=name,
        )(meta, *operands)

    near = lambda x: pltpu.with_memory_space_constraint(x, pltpu.VMEM)

    wide_shape = pltpu.VMEM((hh, rows_here, lanes), f32)
    qw_shape = pltpu.VMEM((depth, rows), bf16)

    def keys_shapes(count):
        return [
            pltpu.VMEM((rows_here, count), f32),
            pltpu.VMEM((count, depth), bf16),
            pltpu.VMEM((depth, count), bf16),
            pltpu.VMEM((rows_here, count), bf16),
        ]

    nears = lambda xs: [near(x) for x in xs]
    early, qw, wides = [], [], []
    for i, group in enumerate(groups[:2]):
        if i == 1:
            far_even = range(2, n - 2, 2)
            wides[0], *came = lax.optimization_barrier((wides[0], *(k_pieces[k] for k in far_even)))
            for k, piece in zip(far_even, came):
                k_pieces[k], k_pieces[k + 1] = piece, swap(piece, "ctx", 1)
        count = (len(group) + i * len(groups[0])) * chunk
        outs = call(
            functools.partial(forward_early_kernel, cfg, groups[0] if i == 1 else [], group),
            q_blocks[: i + 1] + nears(wides) + nears(early) + [k_pieces[k] for k in group],
            keys_shapes(count) + [pltpu.VMEM((rows, count), bf16)] * i + [qw_shape, wide_shape],
            [],
            0.001,
            f"forward_early_{i}",
        )
        early = list(outs[:4])
        qw.append(outs[-2])
        wides.append(outs[-1])
    early_active = outs[4]
    early[0], came = lax.optimization_barrier((early[0], k_pieces[n - 2]))
    k_pieces[n - 2], k_pieces[n - 1] = came, swap(came, "ctx", 1)
    last = len(groups[2]) * chunk
    outs = call(
        functools.partial(forward_middle_kernel, cfg, [groups[0] + groups[1], groups[2]]),
        q_blocks[:2]
        + nears(wides)
        + [q_blocks[j] for j in arrival[1:-1]]
        + nears(early)
        + [k_pieces[k] for k in groups[2]],
        keys_shapes(total_keys)
        + [pltpu.VMEM((rows, last), bf16)]
        + [pltpu.VMEM((rows, total_keys), bf16)] * (nh - 3)
        + [qw_shape] * (nh - 3),
        [pltpu.VMEM((hh, rows_here, lanes), f32)],
        nh - 2.5,
        "forward_middle",
    )
    score, keys_all, keys_t, logits = outs[:4]
    active = {1: [early_active, outs[4]]}
    qw = dict(enumerate(qw))
    for i, j in enumerate(arrival[1:-1]):
        active[j], qw[j] = [outs[5 + i]], outs[5 + nh - 3 + i]
    score, last_active, last_qw, stats = call(
        functools.partial(forward_last_kernel, cfg),
        [q_blocks[arrival[-1]], near(keys_t), near(score), near(logits)],
        [
            pltpu.VMEM((rows_here, total_keys), f32),
            pltpu.VMEM((rows, total_keys), bf16),
            qw_shape,
            jax.ShapeDtypeStruct((1, stat_rows, padded), f32),
        ],
        [pltpu.VMEM((hh, rows_here, lanes), f32)],
        1,
        "forward_last",
        {3: 0},
    )
    active[arrival[-1]], qw[arrival[-1]] = [last_active], last_qw

    all_stats = [stats] + [swap(stats, "head", j) for j in range(1, nh)]

    q_own, _ = lax.optimization_barrier((q_blocks[0], stats))
    outs = call(
        functools.partial(own_active_kernel, cfg),
        [q_own, near(keys_t)],
        [pltpu.VMEM((rows, total_keys // 2), bf16)] * 2,
        [],
        1,
        "own_active",
    )
    rw, *outs = lax.optimization_barrier((rw, *outs))
    own_active = {"first": outs[:1], "second": outs[1:]}

    grad = kg = None

    def backward(items, name):
        nonlocal grad, kg
        is_first = grad is None
        ranges = [item[2] for item in items if item[2] is not None]
        makes_u = any(item[1] for item in items)
        has_before = bool(ranges) and kg is not None
        halved = ranges != [] and ranges[0] != "all"
        operands = []
        for item in items:
            operands += nears(own_active[ranges[0]] if halved else active[item[0]])
        operands += [near(qw[item[0]]) for item in items if item[2] is not None]
        operands += [near(keys_all)]
        operands += all_stats + [rw, near(logits), near(score)] if is_first else [near(grad)]
        aliases = {}
        out_shape = [jax.ShapeDtypeStruct((rows, depth), bf16 if is_first else f32)]
        out_shape = out_shape if makes_u else []
        scratch = [pltpu.VMEM((rows, tile), bf16)] * 2 + [pltpu.VMEM((rows, depth), f32)]
        if not halved:
            if ranges:
                if has_before:
                    aliases = {len(operands) + 1: len(out_shape)}
                out_shape += [pltpu.VMEM((depth, total_keys), f32)]
        else:
            if ranges[0] == "first":
                out_shape += [jax.ShapeDtypeStruct((n // 2, chunk, depth), bf16)]
            else:
                out_shape += [jax.ShapeDtypeStruct((chunk, depth), f32)] * (n // 2)
            out_shape += [pltpu.VMEM((rows, total_keys // 2), bf16)]
            scratch = [pltpu.VMEM((depth, total_keys // 2), f32)]
        if has_before:
            operands += [near(kg)]
        if is_first:
            out_shape += [pltpu.VMEM((rows_here, total_keys), bf16)]
            scratch += [pltpu.VMEM((padded, lanes), f32)]
        kernel = functools.partial(backward_kernel, cfg, items, has_before)
        products = 1 if halved else makes_u + len(ranges)
        outs = call(kernel, operands, out_shape, scratch, products, name, aliases)
        if is_first:
            grad = outs[-1]
        if ranges and ranges[0] == "all":
            kg = outs[1 if makes_u else 0]
        return outs

    part = backward([(1, True, None)], "backward_1")[0]
    moving = ring_next(part, "head")
    for j in range(2, nh):
        items = [(j - 1, False, "all"), (j, True, "all" if j == nh - 1 else None)]
        part = backward(items, f"backward_{j}")[0]
        part = pl.pallas_call(
            add_kernel,
            out_shape=jax.ShapeDtypeStruct((rows, depth), bf16),
            in_specs=[vmem] * 2,
            out_specs=vmem,
            compiler_params=pltpu.CompilerParams(vmem_limit_bytes=vmem_bytes),
            cost_estimate=pl.CostEstimate(
                flops=rows * depth, bytes_accessed=8 * rows * depth, transcendentals=0
            ),
            name=f"add_{j}",
        )(part, moving)
        kg, part = lax.optimization_barrier((kg, part))
        moving = ring_next(part, "head")

    odd, mask_first = backward([(0, False, "first")], "backward_0_first")
    other = swap(odd, "ctx", 1)
    *even, mask_second = backward([(0, False, "second")], "backward_0_second")
    even = [even[i] + other[i].astype(f32) for i in range(n // 2)]
    key_grad = even[0]
    sends = [even[i].astype(bf16) for i in range(1, n // 2)]
    keys_all, *sends = lax.optimization_barrier((keys_all, *sends))
    for i in range(1, n // 2):
        key_grad = key_grad + swap(sends[i - 1], "ctx", 2 * i).astype(f32)
    (u_mine,) = call(
        functools.partial(query_kernel, cfg),
        [near(mask_first), near(mask_second), near(keys_all)],
        [jax.ShapeDtypeStruct((rows, depth), f32)],
        [pltpu.VMEM((rows, depth), f32)],
        1,
        "backward_0",
    )

    query_grad, weight_grad = pl.pallas_call(
        functools.partial(finish_kernel, cfg),
        out_shape=[
            jax.ShapeDtypeStruct((rows_here, hh, depth), f32),
            jax.ShapeDtypeStruct((hh, rows_here), f32),
        ],
        in_specs=[vmem] * 3,
        out_specs=[vmem] * 2,
        compiler_params=pltpu.CompilerParams(vmem_limit_bytes=vmem_bytes),
        cost_estimate=pl.CostEstimate(
            flops=8 * rows * depth, bytes_accessed=14 * rows * depth, transcendentals=0
        ),
        name="finish",
    )(u_mine, moving, q_blocks[0])
    return query_grad, key_grad, weight_grad.T


def solution(mesh):
    in_specs = (P("ctx", "head", None), P("ctx", "head"), P("ctx", None), P(None, "ctx"), P(), P())
    out_specs = (P("ctx", "head", None), P(("ctx", "head"), None), P("ctx", "head"))
    return jax.shard_map(
        per_device, mesh=mesh, in_specs=in_specs, out_specs=out_specs, check_vma=False
    )
```

```python
import functools

import jax
import jax.numpy as jnp
from jax import lax
from jax.experimental import pallas as pl
from jax.experimental.pallas import tpu as pltpu
from jax.sharding import PartitionSpec as P

masked_value = -1e30
lanes = 128
stat_rows = 8
vmem_bytes = 6 * 1024 * 1024
contract_last = (((1,), (1,)), ((), ()))


def swap(value, axis, distance):
    size = lax.axis_size(axis)
    return lax.ppermute(value, axis, [(i, i ^ distance) for i in range(size)])


def ring_next(value, axis, hop=1):
    size = lax.axis_size(axis)
    ring = list(range(0, size, 2)) + list(range(1, size, 2))[::-1]
    return lax.ppermute(value, axis, [(ring[i], ring[(i + hop) % size]) for i in range(size)])


def in_pairs(count, first, step):
    first(0, 0)
    if count <= 8:
        for i in range(count):
            step(i % 2, i, i + 1 if i + 1 < count else None)
        return

    def body(i, _):
        step(0, 2 * i, 2 * i + 1)
        step(1, 2 * i + 1, 2 * i + 2)
        return 0

    lax.fori_loop(0, count // 2 - 1, body, 0)
    step(0, count - 2, count - 1)
    step(1, count - 1, None)


def row_limits(meta_ref, rows_here):
    row = lax.broadcasted_iota(jnp.int32, (rows_here, 1), 0)
    return meta_ref[0] + meta_ref[1] * rows_here + row


def piece_allowed(meta_ref, limit, k, kc, chunk):
    first = (meta_ref[1] ^ k) * kc + meta_ref[2] * chunk
    position = first + lax.broadcasted_iota(jnp.int32, (limit.shape[0], chunk), 1)
    return position <= limit


def spread_weights(cfg, q_ref, wide_ref, qw_ref):
    order, nh, rows_here, hh, depth, kc, chunk, scale = cfg
    rows = rows_here * hh
    eye = (
        lax.broadcasted_iota(jnp.int32, (rows_here, lanes), 0)
        == lax.broadcasted_iota(jnp.int32, (rows_here, lanes), 1)
    ).astype(jnp.float32)
    slab = q_ref[rows:, :].astype(jnp.float32)
    for head in range(hh):
        picked = jnp.sum(slab[head : head + 1] * eye, axis=1, keepdims=True)
        wide_ref[head] = jnp.broadcast_to(picked, (rows_here, lanes))
    for head in range(0, hh, 2):
        at = slice(head * rows_here, (head + 2) * rows_here)
        q = q_ref[at, :].astype(jnp.float32)
        w = wide_ref[head : head + 2].reshape(2 * rows_here, lanes) * scale
        qw_ref[:, at] = (q * w).T.astype(jnp.bfloat16)


def unpack(cfg, message_ref, k, at, keys_ref, keys_t_ref, logits_ref):
    order, nh, rows_here, hh, depth, kc, chunk, scale = cfg
    keys = message_ref[:chunk, :]
    keys_ref[at : at + chunk, :] = keys
    keys_t_ref[:, at : at + chunk] = keys.astype(jnp.float32).T.astype(jnp.bfloat16)
    for i in range(chunk // lanes):
        first = chunk + (chunk // lanes * (k % 2) + i) * rows_here
        column = at + i * lanes
        logits_ref[:, column : column + lanes] = message_ref[first : first + rows_here, :]


def add_scores(cfg, q_ref, wide_ref, keys_t_ref, score_ref, before_ref, start, count, active_ref):
    order, nh, rows_here, hh, depth, kc, chunk, scale = cfg
    rows = rows_here * hh
    side = min(256, count)
    tile = next(size * side for size in (8, 6, 4, 2, 1) if count % (size * side) == 0)

    def step(s, _):
        for first in range(0, tile, side):
            local = pl.ds(pl.multiple_of(s * tile + first, side), side)
            columns = pl.ds(pl.multiple_of(start + s * tile + first, side), side)
            dots = jnp.dot(
                q_ref[:rows, :], keys_t_ref[:, columns], preferred_element_type=jnp.float32
            )
            total = [None] * (rows_here // 16)
            for head in range(hh):
                for t in range(rows_here // 16):
                    row = head * rows_here + t * 16
                    w = wide_ref[head, t * 16 : t * 16 + 16, :]
                    w = jnp.concatenate([w] * (side // lanes), axis=1)
                    active = jnp.maximum(dots[row : row + 16, :], 0.0)
                    if active_ref is not None:
                        active_ref[row : row + 16, local] = active.astype(jnp.bfloat16)
                    value = active * w
                    total[t] = value if head == 0 else total[t] + value
            for t, value in enumerate(total):
                at = slice(t * 16, t * 16 + 16)
                value = value * scale
                if before_ref is not None:
                    value = before_ref[at, columns] + value
                score_ref[at, columns] = value
        return 0

    lax.fori_loop(0, count // tile, step, 0)


def forward_early_kernel(cfg, done, pieces, meta_ref, *refs):
    chunk = cfg[6]
    refs = list(refs)
    take = lambda count: [refs.pop(0) for _ in range(count)]
    q_refs = take(2 if done else 1)
    start, count = len(done) * chunk, len(pieces) * chunk
    if done:
        (own_wide_ref,) = take(1)
        part = take(4)
    message_refs = take(len(pieces))
    score_ref, keys_ref, keys_t_ref, logits_ref = take(4)
    active_ref = take(1)[0] if done else None
    qw_ref, wide_ref = take(2)
    spread_weights(cfg, q_refs[-1], wide_ref, qw_ref)
    if done:
        score_ref[:, :start] = part[0][...]
        keys_ref[:start, :] = part[1][...]
        keys_t_ref[:, :start] = part[2][...]
        logits_ref[:, :start] = part[3][...]
    else:
        own_wide_ref = wide_ref
    for i, k in enumerate(pieces):
        unpack(cfg, message_refs[i], k, start + i * chunk, keys_ref, keys_t_ref, logits_ref)
    add_scores(cfg, q_refs[0], own_wide_ref, keys_t_ref, score_ref, None, start, count, None)
    if done:
        count = start + count
        add_scores(cfg, q_refs[1], wide_ref, keys_t_ref, score_ref, score_ref, 0, count, active_ref)


def forward_middle_kernel(cfg, groups, meta_ref, *refs):
    order, nh, rows_here, hh, depth, kc, chunk, scale = cfg
    refs = list(refs)
    take = lambda count: [refs.pop(0) for _ in range(count)]
    q_refs, wide_refs = take(2), take(2)
    new_q_refs = take(nh - 3)
    parts = [take(4) for _ in groups[:-1]]
    message_refs = take(len(groups[-1]))
    whole = take(4)
    score_ref, keys_ref, keys_t_ref, logits_ref = whole
    (last_active_ref,) = take(1)
    active_refs, qw_refs = take(nh - 3), take(nh - 3)
    (wide,) = take(1)
    start = 0
    for group, part in zip(groups, parts):
        end = start + len(group) * chunk
        score_ref[:, start:end] = part[0][...]
        keys_ref[start:end, :] = part[1][...]
        keys_t_ref[:, start:end] = part[2][...]
        logits_ref[:, start:end] = part[3][...]
        start = end
    for i, k in enumerate(groups[-1]):
        unpack(cfg, message_refs[i], k, start + i * chunk, keys_ref, keys_t_ref, logits_ref)
    count = len(groups[-1]) * chunk
    add_scores(cfg, q_refs[0], wide_refs[0], keys_t_ref, score_ref, None, start, count, None)
    add_scores(
        cfg, q_refs[1], wide_refs[1], keys_t_ref, score_ref, score_ref, start, count, last_active_ref
    )
    for q_ref, active_ref, qw_ref in zip(new_q_refs, active_refs, qw_refs):
        spread_weights(cfg, q_ref, wide, qw_ref)
        every = len(order) * chunk
        add_scores(cfg, q_ref, wide, keys_t_ref, score_ref, score_ref, 0, every, active_ref)


def forward_last_kernel(cfg, meta_ref, *refs):
    order, nh, rows_here, hh, depth, kc, chunk, scale = cfg
    q_ref, keys_t_ref, before_ref, logits_ref, score_ref, active_ref, qw_ref, stats_ref, wide = refs
    spread_weights(cfg, q_ref, wide, qw_ref)
    every = len(order) * chunk
    add_scores(cfg, q_ref, wide, keys_t_ref, score_ref, before_ref, 0, every, active_ref)

    limit = row_limits(meta_ref, rows_here)
    lane = lax.broadcasted_iota(jnp.int32, (rows_here, lanes), 1)
    out = jnp.zeros((rows_here, lanes), jnp.float32)

    def piece(i, at):
        if i == 0:
            return score_ref[:, at * chunk : (at + 1) * chunk]
        return logits_ref[:, at * chunk : (at + 1) * chunk].astype(jnp.float32)

    for i in range(2):
        peak = None
        for at, k in enumerate(order):
            allowed = piece_allowed(meta_ref, limit, k, kc, chunk)
            here = jnp.max(jnp.where(allowed, piece(i, at), masked_value), axis=1, keepdims=True)
            peak = here if peak is None else jnp.maximum(peak, here)
        total = None
        for at, k in enumerate(order):
            allowed = piece_allowed(meta_ref, limit, k, kc, chunk)
            here = jnp.where(allowed, jnp.exp(piece(i, at) - peak), 0.0)
            here = jnp.sum(here, axis=1, keepdims=True)
            total = here if total is None else total + here
        out = jnp.where(lane == 2 * i, peak, out)
        out = jnp.where(lane == 2 * i + 1, total, out)
    padded = stats_ref.shape[2]
    if padded > rows_here:
        out = jnp.concatenate([out, jnp.zeros((padded - rows_here, lanes), jnp.float32)], axis=0)
    stats_ref[0] = out.T[:stat_rows]


def score_gradient(cfg, meta_ref, stats, rw_ref, logits_ref, score_ref, cols, grad_ref):
    order, nh, rows_here, hh, depth, kc, chunk, scale = cfg
    for i in range(2):
        peak = functools.reduce(jnp.maximum, [st[2 * i : 2 * i + 1] for st in stats])
        total = functools.reduce(
            jnp.add,
            [st[2 * i + 1 : 2 * i + 2] * jnp.exp(st[2 * i : 2 * i + 1] - peak) for st in stats],
        )
        cols[2 * i : 2 * i + 1, :] = peak
        cols[2 * i + 1 : 2 * i + 2, :] = rw_ref[...] / total
    cols[4:, :] = jnp.zeros((cols.shape[0] - 4, cols.shape[1]), jnp.float32)
    st = cols[...].T[:rows_here]
    limit = row_limits(meta_ref, rows_here)
    for at, k in enumerate(order):
        logits = logits_ref[:, at * chunk : (at + 1) * chunk].astype(jnp.float32)
        score = score_ref[:, at * chunk : (at + 1) * chunk]
        g = jnp.exp(score - st[:, 0:1]) * st[:, 1:2] - jnp.exp(logits - st[:, 2:3]) * st[:, 3:4]
        g = jnp.where(piece_allowed(meta_ref, limit, k, kc, chunk), g, 0.0)
        grad_ref[:, at * chunk : (at + 1) * chunk] = g.astype(jnp.bfloat16)


def backward_kernel(cfg, items, has_before, meta_ref, *refs):
    order, nh, rows_here, hh, depth, kc, chunk, scale = cfg
    n = len(order)
    rows = rows_here * hh
    refs = list(refs)
    take = lambda count: [refs.pop(0) for _ in range(count)]
    is_first = items[0][0] == 1 and items[0][2] is None
    makes_u = any(item[1] for item in items)
    ranges = [item[2] for item in items if item[2] is not None]
    half = ranges[0] if ranges and ranges[0] != "all" else None
    sources = [take(2 if item[0] == 1 else 1) for item in items]
    qw_refs = [take(1)[0] if item[2] is not None else None for item in items]
    (keys_ref,) = take(1)
    if is_first:
        stat_refs = take(nh)
        rw_ref, logits_ref, score_ref = take(3)
    else:
        (grad_ref,) = take(1)
    before_ref = take(1)[0] if has_before else None
    if makes_u:
        (u_ref,) = take(1)
    if ranges:
        kg_refs = take(n // 2 if half == "second" else 1)
    if is_first:
        (grad_ref,) = take(1)
    if half is not None:
        mask_ref, kg_acc = take(2)
    else:
        masks = take(2)
        (u_acc,) = take(1)
    if is_first:
        (cols,) = take(1)
        stats = [ref[0] for ref in stat_refs]
        score_gradient(cfg, meta_ref, stats, rw_ref, logits_ref, score_ref, cols, grad_ref)
    tile = chunk
    chunks = max(1, min(4, hh))
    heads = hh // chunks
    part = heads * rows_here
    side = tile // 2

    todo = []
    for index, (_, is_u, keys_range) in enumerate(items):
        base = 0
        for ref in sources[index]:
            tiles = n // 2 if half is not None else ref.shape[1] // tile
            todo.append((index, is_u, keys_range, ref, base, tiles))
            base += tiles

    for index, is_u, keys_range, source_ref, base, tiles in todo:
        qw_ref = qw_refs[index]
        is_start = index == 0 or items[index - 1][2] is None

        def tile_at(s, first=0, size=tile, base=base):
            if half is None:
                position = s + base
            else:
                position = meta_ref[3 + (n // 2 if half == "second" else 0) + s]
            return pl.ds(pl.multiple_of(position * tile + first, size), size)

        def local(s, first=0, size=tile):
            return pl.ds(pl.multiple_of(s * tile + first, size), size)

        def mask_at(buffer, s, at, first=0, size=tile):
            if half is None:
                return masks[buffer].at[at, first : first + size]
            return mask_ref.at[at, local(s, first, size)]

        def mask_part(buffer, s, i, source_ref=source_ref):
            at = slice(i * part, (i + 1) * part)
            g = grad_ref[:, tile_at(s)]
            value = source_ref[at, local(s)]
            wide = jnp.broadcast_to(g[None], (heads, rows_here, tile)).reshape(part, tile)
            value = jnp.where(value > 0, wide, jnp.zeros_like(wide))
            mask_at(buffer, s, at)[...] = value.astype(jnp.bfloat16)

        def mask(buffer, s):
            for i in range(chunks):
                mask_part(buffer, s, i)

        def step(buffer, s, following):
            for i in range(chunks):
                if following is not None:
                    mask_part(1 - buffer, following, i)
                if is_u:
                    at = slice(i * part, (i + 1) * part)
                    u_acc[at, :] += jnp.dot(
                        mask_at(buffer, s, at)[...],
                        keys_ref[tile_at(s), :],
                        preferred_element_type=jnp.float32,
                    )
                if keys_range is None or i % (chunks // 2) != chunks // 2 - 1:
                    continue
                first = i // (chunks // 2) * side
                more = jnp.dot(
                    qw_ref[...],
                    mask_at(buffer, s, slice(0, rows), first, side)[...],
                    preferred_element_type=jnp.float32,
                )
                here = tile_at(s, first, side)
                if not is_start:
                    more = kg_refs[0][:, here] + more
                elif before_ref is not None:
                    more = before_ref[:, here] + more
                if half is None:
                    kg_refs[0][:, here] = more
                else:
                    kg_acc[:, local(s, first, side)] = more

        if is_u and base == 0:
            u_acc[...] = jnp.zeros_like(u_acc)
        in_pairs(tiles, mask, step)
        if is_u and (base + tiles) == n:
            u_ref[...] = u_acc[...].astype(u_ref.dtype)

    if half is not None:
        for i in range(n // 2):
            value = kg_acc[:, i * chunk : (i + 1) * chunk].T
            if half == "first":
                kg_refs[0][i] = value.astype(kg_refs[0].dtype)
            else:
                kg_refs[i][...] = value


def own_active_kernel(cfg, meta_ref, q_ref, keys_t_ref, first_ref, second_ref):
    order, nh, rows_here, hh, depth, kc, chunk, scale = cfg
    side = min(256, chunk)
    for half, active_ref in enumerate((first_ref, second_ref)):
        for s, k in enumerate(range(1 - half, len(order), 2)):
            for first in range(0, chunk, side):
                column = order.index(k) * chunk + first
                dots = jnp.dot(
                    q_ref[: rows_here * hh, :],
                    keys_t_ref[:, column : column + side],
                    preferred_element_type=jnp.float32,
                )
                active = jnp.maximum(dots, 0.0).astype(jnp.bfloat16)
                active_ref[:, s * chunk + first : s * chunk + first + side] = active


def query_kernel(cfg, meta_ref, first_ref, second_ref, keys_ref, u_ref, u_acc):
    order, chunk = cfg[0], cfg[6]
    for half, mask_ref in enumerate((first_ref, second_ref)):
        for s, k in enumerate(range(1 - half, len(order), 2)):
            position = order.index(k)
            more = jnp.dot(
                mask_ref[:, s * chunk : (s + 1) * chunk],
                keys_ref[position * chunk : (position + 1) * chunk, :],
                preferred_element_type=jnp.float32,
            )
            if half == 0 and s == 0:
                u_acc[...] = more
            else:
                u_acc[...] += more
    u_ref[...] = u_acc[...]


def prepare_kernel(cfg, query_ref, weights_ref, rw_ref, keys_ref, logits_ref, *refs):
    order, nh, rows_here, hh, depth, kc, chunk, scale = cfg
    sends = len(order) // 2
    rows = rows_here * hh
    parts = chunk // lanes
    message_ref, rw_out_ref, key_refs = refs[0], refs[1], refs[2 : 2 + sends]
    wide, sems = refs[-2], refs[-1]
    share = pl.multiple_of(lax.axis_index("head") * chunk, chunk)
    copies = []

    def copy(source, target):
        copies.append(pltpu.make_async_copy(source, target, sems.at[len(copies)]))
        copies[-1].start()

    for i in reversed(range(sends)):
        copy(keys_ref.at[pl.ds(share, chunk), :], key_refs[i].at[:chunk, :])
        for core in range(2):
            row = pl.multiple_of((lax.axis_index("ctx") ^ (2 * i) ^ core) * rows_here, rows_here)
            for part in range(parts):
                first = chunk + (parts * core + part) * rows_here
                copy(
                    logits_ref.at[pl.ds(row, rows_here), pl.ds(share + part * lanes, lanes)],
                    key_refs[i].at[first : first + rows_here, :],
                )
    every = jnp.broadcast_to(rw_ref[...], (8, rw_ref.shape[1]))
    shift = every.shape[1] - lax.axis_index("ctx") * rows_here
    here = pltpu.roll(every, shift, 1)[:1, : rw_out_ref.shape[1]]
    rw_out_ref[...] = here * float(kc * len(order)) ** 0.5
    wide[...] = query_ref[...].astype(jnp.float32)
    for head in range(hh):
        at = slice(head * rows_here, (head + 1) * rows_here)
        message_ref[at, :] = wide[:, head, :].astype(jnp.bfloat16)
    message_ref[rows:, :] = jnp.zeros((message_ref.shape[0] - rows, lanes), jnp.bfloat16)
    message_ref[rows : rows + hh, :rows_here] = weights_ref[...]
    for item in copies:
        item.wait()


def add_kernel(u_ref, moving_ref, out_ref):
    out_ref[...] = (u_ref[...] + moving_ref[...].astype(jnp.float32)).astype(out_ref.dtype)


def finish_kernel(cfg, u_ref, moving_ref, q_ref, query_grad_ref, weight_grad_ref):
    order, nh, rows_here, hh, depth, kc, chunk, scale = cfg
    rows = rows_here * hh
    eye = (
        lax.broadcasted_iota(jnp.int32, (rows_here, lanes), 0)
        == lax.broadcasted_iota(jnp.int32, (rows_here, lanes), 1)
    ).astype(jnp.float32)
    lane = lax.broadcasted_iota(jnp.int32, (lanes, lanes), 1)[:rows_here]
    slab = q_ref[rows:, :].astype(jnp.float32)
    out = jnp.zeros((rows_here, lanes), jnp.float32)
    for head in range(hh):
        at = slice(head * rows_here, (head + 1) * rows_here)
        total = u_ref[at, :] + moving_ref[at, :].astype(jnp.float32)
        w = jnp.sum(slab[head : head + 1] * eye, axis=1, keepdims=True) * scale
        query_grad_ref[:, head, :] = total * w
        along = jnp.sum(total * q_ref[at, :].astype(jnp.float32), axis=1, keepdims=True)
        out = jnp.where(lane == head, along * scale, out)
    if rows_here < lanes:
        out = jnp.concatenate([out, jnp.zeros((lanes - rows_here, lanes), jnp.float32)], axis=0)
    weight_grad_ref[...] = out.T[:hh, :rows_here]


def per_device(query, weights, keys, main_logits, row_weight, offset):
    n = lax.axis_size("ctx")
    nh = lax.axis_size("head")
    c = lax.axis_index("ctx")
    h = lax.axis_index("head")
    rows_here, hh, depth = query.shape
    kc = keys.shape[0]
    chunk = kc // nh
    rows = rows_here * hh
    scale = depth ** (-0.5)
    bf16, f32 = jnp.bfloat16, jnp.float32

    groups = [
        [1, 0],
        list(range(3, n - 2, 2)) + list(range(2, n - 2, 2)),
        [n - 1, n - 2],
    ]
    order = sum(groups, [])
    cfg = (order, nh, rows_here, hh, depth, kc, chunk, scale)
    smem = pl.BlockSpec(memory_space=pltpu.SMEM)
    vmem = pl.BlockSpec(memory_space=pltpu.VMEM)
    padded = -(-rows_here // lanes) * lanes
    table = [order.index(k) for k in list(range(1, n, 2)) + list(range(0, n, 2))]
    meta = jnp.concatenate(
        [offset, jnp.stack([c, h]).astype(jnp.int32), jnp.array(table, jnp.int32)]
    )

    far = lambda x: pltpu.with_memory_space_constraint(x, pltpu.HBM)

    slab_rows = -(-hh // 16) * 16
    parts = chunk // lanes
    message, rw, *key_messages = pl.pallas_call(
        functools.partial(prepare_kernel, cfg),
        out_shape=[
            jax.ShapeDtypeStruct((rows + slab_rows, depth), bf16),
            jax.ShapeDtypeStruct((1, padded), f32),
        ]
        + [jax.ShapeDtypeStruct((chunk + 2 * parts * rows_here, depth), bf16)] * (n // 2),
        in_specs=[vmem, vmem, vmem] + [pl.BlockSpec(memory_space=pltpu.HBM)] * 2,
        out_specs=[vmem] * (2 + n // 2),
        scratch_shapes=[
            pltpu.VMEM((rows_here, hh, depth), f32),
            pltpu.SemaphoreType.DMA((n // 2 * (1 + 2 * parts),)),
        ],
        compiler_params=pltpu.CompilerParams(vmem_limit_bytes=vmem_bytes),
        cost_estimate=pl.CostEstimate(
            flops=rows * depth, bytes_accessed=4 * 1024 * 1024, transcendentals=0
        ),
        name="prepare",
    )(far(query), far(weights.T), far(row_weight[None, :]), far(keys), far(main_logits))
    q_blocks = [message] * nh
    for hop in range(1, nh // 2 + 1):
        q_blocks[hop] = ring_next(q_blocks[hop - 1], "head")
        if nh - hop > hop:
            q_blocks[nh - hop] = ring_next(q_blocks[(nh - hop + 1) % nh], "head", -1)
    arrival = [1]
    for hop in range(1, nh // 2 + 1):
        arrival += [j for j in sorted({hop, nh - hop}) if j not in arrival]

    k_pieces = [None] * n
    k_pieces[0::2] = [key_messages[0]] + [
        swap(key_messages[k // 2], "ctx", k) for k in range(2, n, 2)
    ]
    k_pieces[1] = swap(k_pieces[0], "ctx", 1)
    total_keys = n * chunk
    macs = rows * total_keys * depth
    tile = chunk

    def call(kernel, operands, out_shape, scratch, products, name, aliases={}):
        return pl.pallas_call(
            kernel,
            out_shape=out_shape,
            input_output_aliases=aliases,
            in_specs=[smem] + [vmem] * len(operands),
            out_specs=[vmem] * len(out_shape),
            scratch_shapes=scratch,
            compiler_params=pltpu.CompilerParams(vmem_limit_bytes=vmem_bytes),
            cost_estimate=pl.CostEstimate(
                flops=int(4 * products * macs),
                bytes_accessed=int(4 * products * 2**20),
                transcendentals=0,
            ),
            name=name,
        )(meta, *operands)

    near = lambda x: pltpu.with_memory_space_constraint(x, pltpu.VMEM)

    wide_shape = pltpu.VMEM((hh, rows_here, lanes), f32)
    qw_shape = pltpu.VMEM((depth, rows), bf16)

    def keys_shapes(count):
        return [
            pltpu.VMEM((rows_here, count), f32),
            pltpu.VMEM((count, depth), bf16),
            pltpu.VMEM((depth, count), bf16),
            pltpu.VMEM((rows_here, count), bf16),
        ]

    nears = lambda xs: [near(x) for x in xs]
    early, qw, wides = [], [], []
    for i, group in enumerate(groups[:2]):
        if i == 1:
            far_even = range(2, n - 2, 2)
            wides[0], *came = lax.optimization_barrier((wides[0], *(k_pieces[k] for k in far_even)))
            for k, piece in zip(far_even, came):
                k_pieces[k], k_pieces[k + 1] = piece, swap(piece, "ctx", 1)
        count = (len(group) + i * len(groups[0])) * chunk
        outs = call(
            functools.partial(forward_early_kernel, cfg, groups[0] if i == 1 else [], group),
            q_blocks[: i + 1] + nears(wides) + nears(early) + [k_pieces[k] for k in group],
            keys_shapes(count) + [pltpu.VMEM((rows, count), bf16)] * i + [qw_shape, wide_shape],
            [],
            0.001,
            f"forward_early_{i}",
        )
        early = list(outs[:4])
        qw.append(outs[-2])
        wides.append(outs[-1])
    early_active = outs[4]
    early[0], came = lax.optimization_barrier((early[0], k_pieces[n - 2]))
    k_pieces[n - 2], k_pieces[n - 1] = came, swap(came, "ctx", 1)
    last = len(groups[2]) * chunk
    outs = call(
        functools.partial(forward_middle_kernel, cfg, [groups[0] + groups[1], groups[2]]),
        q_blocks[:2]
        + nears(wides)
        + [q_blocks[j] for j in arrival[1:-1]]
        + nears(early)
        + [k_pieces[k] for k in groups[2]],
        keys_shapes(total_keys)
        + [pltpu.VMEM((rows, last), bf16)]
        + [pltpu.VMEM((rows, total_keys), bf16)] * (nh - 3)
        + [qw_shape] * (nh - 3),
        [pltpu.VMEM((hh, rows_here, lanes), f32)],
        nh - 2.5,
        "forward_middle",
    )
    score, keys_all, keys_t, logits = outs[:4]
    active = {1: [early_active, outs[4]]}
    qw = dict(enumerate(qw))
    for i, j in enumerate(arrival[1:-1]):
        active[j], qw[j] = [outs[5 + i]], outs[5 + nh - 3 + i]
    score, last_active, last_qw, stats = call(
        functools.partial(forward_last_kernel, cfg),
        [q_blocks[arrival[-1]], near(keys_t), near(score), near(logits)],
        [
            pltpu.VMEM((rows_here, total_keys), f32),
            pltpu.VMEM((rows, total_keys), bf16),
            qw_shape,
            jax.ShapeDtypeStruct((1, stat_rows, padded), f32),
        ],
        [pltpu.VMEM((hh, rows_here, lanes), f32)],
        1,
        "forward_last",
        {3: 0},
    )
    active[arrival[-1]], qw[arrival[-1]] = [last_active], last_qw

    all_stats = [stats] + [swap(stats, "head", j) for j in range(1, nh)]

    q_own, _ = lax.optimization_barrier((q_blocks[0], stats))
    outs = call(
        functools.partial(own_active_kernel, cfg),
        [q_own, near(keys_t)],
        [pltpu.VMEM((rows, total_keys // 2), bf16)] * 2,
        [],
        1,
        "own_active",
    )
    rw, *outs = lax.optimization_barrier((rw, *outs))
    own_active = {"first": outs[:1], "second": outs[1:]}

    grad = kg = None

    def backward(items, name):
        nonlocal grad, kg
        is_first = grad is None
        ranges = [item[2] for item in items if item[2] is not None]
        makes_u = any(item[1] for item in items)
        has_before = bool(ranges) and kg is not None
        halved = ranges != [] and ranges[0] != "all"
        operands = []
        for item in items:
            operands += nears(own_active[ranges[0]] if halved else active[item[0]])
        operands += [near(qw[item[0]]) for item in items if item[2] is not None]
        operands += [near(keys_all)]
        operands += all_stats + [rw, near(logits), near(score)] if is_first else [near(grad)]
        aliases = {}
        out_shape = [jax.ShapeDtypeStruct((rows, depth), bf16 if is_first else f32)]
        out_shape = out_shape if makes_u else []
        scratch = [pltpu.VMEM((rows, tile), bf16)] * 2 + [pltpu.VMEM((rows, depth), f32)]
        if not halved:
            if ranges:
                if has_before:
                    aliases = {len(operands) + 1: len(out_shape)}
                out_shape += [pltpu.VMEM((depth, total_keys), f32)]
        else:
            if ranges[0] == "first":
                out_shape += [jax.ShapeDtypeStruct((n // 2, chunk, depth), bf16)]
            else:
                out_shape += [jax.ShapeDtypeStruct((chunk, depth), f32)] * (n // 2)
            out_shape += [pltpu.VMEM((rows, total_keys // 2), bf16)]
            scratch = [pltpu.VMEM((depth, total_keys // 2), f32)]
        if has_before:
            operands += [near(kg)]
        if is_first:
            out_shape += [pltpu.VMEM((rows_here, total_keys), bf16)]
            scratch += [pltpu.VMEM((padded, lanes), f32)]
        kernel = functools.partial(backward_kernel, cfg, items, has_before)
        products = 1 if halved else makes_u + len(ranges)
        outs = call(kernel, operands, out_shape, scratch, products, name, aliases)
        if is_first:
            grad = outs[-1]
        if ranges and ranges[0] == "all":
            kg = outs[1 if makes_u else 0]
        return outs

    part = backward([(1, True, None)], "backward_1")[0]
    moving = ring_next(part, "head")
    for j in range(2, nh):
        items = [(j - 1, False, "all"), (j, True, "all" if j == nh - 1 else None)]
        part = backward(items, f"backward_{j}")[0]
        part = pl.pallas_call(
            add_kernel,
            out_shape=jax.ShapeDtypeStruct((rows, depth), bf16),
            in_specs=[vmem] * 2,
            out_specs=vmem,
            compiler_params=pltpu.CompilerParams(vmem_limit_bytes=vmem_bytes),
            cost_estimate=pl.CostEstimate(
                flops=rows * depth, bytes_accessed=8 * rows * depth, transcendentals=0
            ),
            name=f"add_{j}",
        )(part, moving)
        kg, part = lax.optimization_barrier((kg, part))
        moving = ring_next(part, "head")

    odd, mask_first = backward([(0, False, "first")], "backward_0_first")
    other = swap(odd, "ctx", 1)
    *even, mask_second = backward([(0, False, "second")], "backward_0_second")
    even = [even[i] + other[i].astype(f32) for i in range(n // 2)]
    key_grad = even[0]
    sends = [even[i].astype(bf16) for i in range(1, n // 2)]
    keys_all, *sends = lax.optimization_barrier((keys_all, *sends))
    for i in range(1, n // 2):
        key_grad = key_grad + swap(sends[i - 1], "ctx", 2 * i).astype(f32)
    (u_mine,) = call(
        functools.partial(query_kernel, cfg),
        [near(mask_first), near(mask_second), near(keys_all)],
        [jax.ShapeDtypeStruct((rows, depth), f32)],
        [pltpu.VMEM((rows, depth), f32)],
        1,
        "backward_0",
    )

    query_grad, weight_grad = pl.pallas_call(
        functools.partial(finish_kernel, cfg),
        out_shape=[
            jax.ShapeDtypeStruct((rows_here, hh, depth), f32),
            jax.ShapeDtypeStruct((hh, rows_here), f32),
        ],
        in_specs=[vmem] * 3,
        out_specs=[vmem] * 2,
        compiler_params=pltpu.CompilerParams(vmem_limit_bytes=vmem_bytes),
        cost_estimate=pl.CostEstimate(
            flops=8 * rows * depth, bytes_accessed=14 * rows * depth, transcendentals=0
        ),
        name="finish",
    )(u_mine, moving, q_blocks[0])
    return query_grad, key_grad, weight_grad.T


def solution(mesh):
    in_specs = (P("ctx", "head", None), P("ctx", "head"), P("ctx", None), P(None, "ctx"), P(), P())
    out_specs = (P("ctx", "head", None), P(("ctx", "head"), None), P("ctx", "head"))
    return jax.shard_map(
        per_device, mesh=mesh, in_specs=in_specs, out_specs=out_specs, check_vma=False
    )
```

```python
import functools

import jax
import jax.numpy as jnp
from jax import lax
from jax.experimental import pallas as pl
from jax.experimental.pallas import tpu as pltpu
from jax.sharding import PartitionSpec as P

masked_value = -1e30
lanes = 128
stat_rows = 8
vmem_bytes = 6 * 1024 * 1024
contract_last = (((1,), (1,)), ((), ()))


def swap(value, axis, distance):
    size = lax.axis_size(axis)
    return lax.ppermute(value, axis, [(i, i ^ distance) for i in range(size)])


def ring_next(value, axis, hop=1):
    size = lax.axis_size(axis)
    ring = list(range(0, size, 2)) + list(range(1, size, 2))[::-1]
    return lax.ppermute(value, axis, [(ring[i], ring[(i + hop) % size]) for i in range(size)])


def in_pairs(count, first, step):
    first(0, 0)
    if count <= 8:
        for i in range(count):
            step(i % 2, i, i + 1 if i + 1 < count else None)
        return

    def body(i, _):
        step(0, 2 * i, 2 * i + 1)
        step(1, 2 * i + 1, 2 * i + 2)
        return 0

    lax.fori_loop(0, count // 2 - 1, body, 0)
    step(0, count - 2, count - 1)
    step(1, count - 1, None)


def row_limits(meta_ref, rows_here):
    row = lax.broadcasted_iota(jnp.int32, (rows_here, 1), 0)
    return meta_ref[0] + meta_ref[1] * rows_here + row


def piece_allowed(meta_ref, limit, k, kc, chunk):
    first = (meta_ref[1] ^ k) * kc + meta_ref[2] * chunk
    position = first + lax.broadcasted_iota(jnp.int32, (limit.shape[0], chunk), 1)
    return position <= limit


def spread_weights(cfg, q_ref, wide_ref, qw_ref):
    order, nh, rows_here, hh, depth, kc, chunk, scale = cfg
    rows = rows_here * hh
    eye = (
        lax.broadcasted_iota(jnp.int32, (rows_here, lanes), 0)
        == lax.broadcasted_iota(jnp.int32, (rows_here, lanes), 1)
    ).astype(jnp.float32)
    slab = q_ref[rows:, :].astype(jnp.float32)
    for head in range(hh):
        picked = jnp.sum(slab[head : head + 1] * eye, axis=1, keepdims=True)
        wide_ref[head] = jnp.broadcast_to(picked, (rows_here, lanes))
    for head in range(0, hh, 2):
        at = slice(head * rows_here, (head + 2) * rows_here)
        q = q_ref[at, :].astype(jnp.float32)
        w = wide_ref[head : head + 2].reshape(2 * rows_here, lanes) * scale
        qw_ref[:, at] = (q * w).T.astype(jnp.bfloat16)


def unpack(cfg, message_ref, k, at, keys_ref, keys_t_ref, logits_ref):
    order, nh, rows_here, hh, depth, kc, chunk, scale = cfg
    keys = message_ref[:chunk, :]
    keys_ref[at : at + chunk, :] = keys
    keys_t_ref[:, at : at + chunk] = keys.astype(jnp.float32).T.astype(jnp.bfloat16)
    for i in range(chunk // lanes):
        first = chunk + (chunk // lanes * (k % 2) + i) * rows_here
        column = at + i * lanes
        logits_ref[:, column : column + lanes] = message_ref[first : first + rows_here, :]


def add_scores(cfg, q_ref, wide_ref, keys_t_ref, score_ref, before_ref, start, count, active_ref):
    order, nh, rows_here, hh, depth, kc, chunk, scale = cfg
    rows = rows_here * hh
    side = min(256, count)
    tile = next(size * side for size in (16, 12, 8, 6, 4, 2, 1) if count % (size * side) == 0)

    def step(s, _):
        for first in range(0, tile, side):
            local = pl.ds(pl.multiple_of(s * tile + first, side), side)
            columns = pl.ds(pl.multiple_of(start + s * tile + first, side), side)
            dots = jnp.dot(
                q_ref[:rows, :], keys_t_ref[:, columns], preferred_element_type=jnp.float32
            )
            total = [None] * (rows_here // 16)
            for head in range(hh):
                for t in range(rows_here // 16):
                    row = head * rows_here + t * 16
                    w = wide_ref[head, t * 16 : t * 16 + 16, :]
                    w = jnp.concatenate([w] * (side // lanes), axis=1)
                    active = jnp.maximum(dots[row : row + 16, :], 0.0)
                    if active_ref is not None:
                        active_ref[row : row + 16, local] = active.astype(jnp.bfloat16)
                    value = active * w
                    total[t] = value if head == 0 else total[t] + value
            for t, value in enumerate(total):
                at = slice(t * 16, t * 16 + 16)
                value = value * scale
                if before_ref is not None:
                    value = before_ref[at, columns] + value
                score_ref[at, columns] = value
        return 0

    lax.fori_loop(0, count // tile, step, 0)


def forward_early_kernel(cfg, done, pieces, meta_ref, *refs):
    chunk = cfg[6]
    refs = list(refs)
    take = lambda count: [refs.pop(0) for _ in range(count)]
    q_refs = take(2 if done else 1)
    start, count = len(done) * chunk, len(pieces) * chunk
    if done:
        (own_wide_ref,) = take(1)
        part = take(4)
    message_refs = take(len(pieces))
    score_ref, keys_ref, keys_t_ref, logits_ref = take(4)
    active_ref = take(1)[0] if done else None
    qw_ref, wide_ref = take(2)
    spread_weights(cfg, q_refs[-1], wide_ref, qw_ref)
    if done:
        score_ref[:, :start] = part[0][...]
        keys_ref[:start, :] = part[1][...]
        keys_t_ref[:, :start] = part[2][...]
        logits_ref[:, :start] = part[3][...]
    else:
        own_wide_ref = wide_ref
    for i, k in enumerate(pieces):
        unpack(cfg, message_refs[i], k, start + i * chunk, keys_ref, keys_t_ref, logits_ref)
    add_scores(cfg, q_refs[0], own_wide_ref, keys_t_ref, score_ref, None, start, count, None)
    if done:
        count = start + count
        add_scores(cfg, q_refs[1], wide_ref, keys_t_ref, score_ref, score_ref, 0, count, active_ref)


def forward_middle_kernel(cfg, groups, meta_ref, *refs):
    order, nh, rows_here, hh, depth, kc, chunk, scale = cfg
    refs = list(refs)
    take = lambda count: [refs.pop(0) for _ in range(count)]
    q_refs, wide_refs = take(2), take(2)
    new_q_refs = take(nh - 3)
    parts = [take(4) for _ in groups[:-1]]
    message_refs = take(len(groups[-1]))
    whole = take(4)
    score_ref, keys_ref, keys_t_ref, logits_ref = whole
    (last_active_ref,) = take(1)
    active_refs, qw_refs = take(nh - 3), take(nh - 3)
    (wide,) = take(1)
    start = 0
    for group, part in zip(groups, parts):
        end = start + len(group) * chunk
        score_ref[:, start:end] = part[0][...]
        keys_ref[start:end, :] = part[1][...]
        keys_t_ref[:, start:end] = part[2][...]
        logits_ref[:, start:end] = part[3][...]
        start = end
    for i, k in enumerate(groups[-1]):
        unpack(cfg, message_refs[i], k, start + i * chunk, keys_ref, keys_t_ref, logits_ref)
    count = len(groups[-1]) * chunk
    add_scores(cfg, q_refs[0], wide_refs[0], keys_t_ref, score_ref, None, start, count, None)
    add_scores(
        cfg, q_refs[1], wide_refs[1], keys_t_ref, score_ref, score_ref, start, count, last_active_ref
    )
    for q_ref, active_ref, qw_ref in zip(new_q_refs, active_refs, qw_refs):
        spread_weights(cfg, q_ref, wide, qw_ref)
        every = len(order) * chunk
        add_scores(cfg, q_ref, wide, keys_t_ref, score_ref, score_ref, 0, every, active_ref)


def forward_last_kernel(cfg, meta_ref, *refs):
    order, nh, rows_here, hh, depth, kc, chunk, scale = cfg
    q_ref, keys_t_ref, before_ref, logits_ref, score_ref, active_ref, qw_ref, stats_ref, wide = refs
    spread_weights(cfg, q_ref, wide, qw_ref)
    every = len(order) * chunk
    add_scores(cfg, q_ref, wide, keys_t_ref, score_ref, before_ref, 0, every, active_ref)

    limit = row_limits(meta_ref, rows_here)
    lane = lax.broadcasted_iota(jnp.int32, (rows_here, lanes), 1)
    out = jnp.zeros((rows_here, lanes), jnp.float32)

    def piece(i, at):
        if i == 0:
            return score_ref[:, at * chunk : (at + 1) * chunk]
        return logits_ref[:, at * chunk : (at + 1) * chunk].astype(jnp.float32)

    for i in range(2):
        peak = None
        for at, k in enumerate(order):
            allowed = piece_allowed(meta_ref, limit, k, kc, chunk)
            here = jnp.max(jnp.where(allowed, piece(i, at), masked_value), axis=1, keepdims=True)
            peak = here if peak is None else jnp.maximum(peak, here)
        total = None
        for at, k in enumerate(order):
            allowed = piece_allowed(meta_ref, limit, k, kc, chunk)
            here = jnp.where(allowed, jnp.exp(piece(i, at) - peak), 0.0)
            here = jnp.sum(here, axis=1, keepdims=True)
            total = here if total is None else total + here
        out = jnp.where(lane == 2 * i, peak, out)
        out = jnp.where(lane == 2 * i + 1, total, out)
    padded = stats_ref.shape[2]
    if padded > rows_here:
        out = jnp.concatenate([out, jnp.zeros((padded - rows_here, lanes), jnp.float32)], axis=0)
    stats_ref[0] = out.T[:stat_rows]


def score_gradient(cfg, meta_ref, stats, rw_ref, logits_ref, score_ref, cols, grad_ref):
    order, nh, rows_here, hh, depth, kc, chunk, scale = cfg
    for i in range(2):
        peak = functools.reduce(jnp.maximum, [st[2 * i : 2 * i + 1] for st in stats])
        total = functools.reduce(
            jnp.add,
            [st[2 * i + 1 : 2 * i + 2] * jnp.exp(st[2 * i : 2 * i + 1] - peak) for st in stats],
        )
        cols[2 * i : 2 * i + 1, :] = peak
        cols[2 * i + 1 : 2 * i + 2, :] = rw_ref[...] / total
    cols[4:, :] = jnp.zeros((cols.shape[0] - 4, cols.shape[1]), jnp.float32)
    st = cols[...].T[:rows_here]
    limit = row_limits(meta_ref, rows_here)
    for at, k in enumerate(order):
        logits = logits_ref[:, at * chunk : (at + 1) * chunk].astype(jnp.float32)
        score = score_ref[:, at * chunk : (at + 1) * chunk]
        g = jnp.exp(score - st[:, 0:1]) * st[:, 1:2] - jnp.exp(logits - st[:, 2:3]) * st[:, 3:4]
        g = jnp.where(piece_allowed(meta_ref, limit, k, kc, chunk), g, 0.0)
        grad_ref[:, at * chunk : (at + 1) * chunk] = g.astype(jnp.bfloat16)


def backward_kernel(cfg, items, has_before, meta_ref, *refs):
    order, nh, rows_here, hh, depth, kc, chunk, scale = cfg
    n = len(order)
    rows = rows_here * hh
    refs = list(refs)
    take = lambda count: [refs.pop(0) for _ in range(count)]
    is_first = items[0][0] == 1 and items[0][2] is None
    makes_u = any(item[1] for item in items)
    ranges = [item[2] for item in items if item[2] is not None]
    half = ranges[0] if ranges and ranges[0] != "all" else None
    sources = [take(2 if item[0] == 1 else 1) for item in items]
    qw_refs = [take(1)[0] if item[2] is not None else None for item in items]
    (keys_ref,) = take(1)
    if is_first:
        stat_refs = take(nh)
        rw_ref, logits_ref, score_ref = take(3)
    else:
        (grad_ref,) = take(1)
    before_ref = take(1)[0] if has_before else None
    if makes_u:
        (u_ref,) = take(1)
    if ranges:
        kg_refs = take(n // 2 if half == "second" else 1)
    if is_first:
        (grad_ref,) = take(1)
    if half is not None:
        mask_ref, kg_acc = take(2)
    else:
        masks = take(2)
        (u_acc,) = take(1)
    if is_first:
        (cols,) = take(1)
        stats = [ref[0] for ref in stat_refs]
        score_gradient(cfg, meta_ref, stats, rw_ref, logits_ref, score_ref, cols, grad_ref)
    tile = chunk
    chunks = max(1, min(4, hh))
    heads = hh // chunks
    part = heads * rows_here
    side = tile // 2

    todo = []
    for index, (_, is_u, keys_range) in enumerate(items):
        base = 0
        for ref in sources[index]:
            tiles = n // 2 if half is not None else ref.shape[1] // tile
            todo.append((index, is_u, keys_range, ref, base, tiles))
            base += tiles

    for index, is_u, keys_range, source_ref, base, tiles in todo:
        qw_ref = qw_refs[index]
        is_start = index == 0 or items[index - 1][2] is None

        def tile_at(s, first=0, size=tile, base=base):
            if half is None:
                position = s + base
            else:
                position = meta_ref[3 + (n // 2 if half == "second" else 0) + s]
            return pl.ds(pl.multiple_of(position * tile + first, size), size)

        def local(s, first=0, size=tile):
            return pl.ds(pl.multiple_of(s * tile + first, size), size)

        def mask_at(buffer, s, at, first=0, size=tile):
            if half is None:
                return masks[buffer].at[at, first : first + size]
            return mask_ref.at[at, local(s, first, size)]

        def mask_part(buffer, s, i, source_ref=source_ref):
            at = slice(i * part, (i + 1) * part)
            g = grad_ref[:, tile_at(s)]
            value = source_ref[at, local(s)]
            wide = jnp.broadcast_to(g[None], (heads, rows_here, tile)).reshape(part, tile)
            value = jnp.where(value > 0, wide, jnp.zeros_like(wide))
            mask_at(buffer, s, at)[...] = value.astype(jnp.bfloat16)

        def mask(buffer, s):
            for i in range(chunks):
                mask_part(buffer, s, i)

        def step(buffer, s, following):
            for i in range(chunks):
                if following is not None:
                    mask_part(1 - buffer, following, i)
                if is_u:
                    at = slice(i * part, (i + 1) * part)
                    u_acc[at, :] += jnp.dot(
                        mask_at(buffer, s, at)[...],
                        keys_ref[tile_at(s), :],
                        preferred_element_type=jnp.float32,
                    )
                if keys_range is None or i % (chunks // 2) != chunks // 2 - 1:
                    continue
                first = i // (chunks // 2) * side
                more = jnp.dot(
                    qw_ref[...],
                    mask_at(buffer, s, slice(0, rows), first, side)[...],
                    preferred_element_type=jnp.float32,
                )
                here = tile_at(s, first, side)
                if not is_start:
                    more = kg_refs[0][:, here] + more
                elif before_ref is not None:
                    more = before_ref[:, here] + more
                if half is None:
                    kg_refs[0][:, here] = more
                else:
                    kg_acc[:, local(s, first, side)] = more

        if is_u and base == 0:
            u_acc[...] = jnp.zeros_like(u_acc)
        in_pairs(tiles, mask, step)
        if is_u and (base + tiles) == n:
            u_ref[...] = u_acc[...].astype(u_ref.dtype)

    if half is not None:
        for i in range(n // 2):
            value = kg_acc[:, i * chunk : (i + 1) * chunk].T
            if half == "first":
                kg_refs[0][i] = value.astype(kg_refs[0].dtype)
            else:
                kg_refs[i][...] = value


def own_active_kernel(cfg, meta_ref, q_ref, keys_t_ref, first_ref, second_ref):
    order, nh, rows_here, hh, depth, kc, chunk, scale = cfg
    side = min(256, chunk)
    for half, active_ref in enumerate((first_ref, second_ref)):
        for s, k in enumerate(range(1 - half, len(order), 2)):
            for first in range(0, chunk, side):
                column = order.index(k) * chunk + first
                dots = jnp.dot(
                    q_ref[: rows_here * hh, :],
                    keys_t_ref[:, column : column + side],
                    preferred_element_type=jnp.float32,
                )
                active = jnp.maximum(dots, 0.0).astype(jnp.bfloat16)
                active_ref[:, s * chunk + first : s * chunk + first + side] = active


def query_kernel(cfg, meta_ref, first_ref, second_ref, keys_ref, u_ref, u_acc):
    order, chunk = cfg[0], cfg[6]
    for half, mask_ref in enumerate((first_ref, second_ref)):
        for s, k in enumerate(range(1 - half, len(order), 2)):
            position = order.index(k)
            more = jnp.dot(
                mask_ref[:, s * chunk : (s + 1) * chunk],
                keys_ref[position * chunk : (position + 1) * chunk, :],
                preferred_element_type=jnp.float32,
            )
            if half == 0 and s == 0:
                u_acc[...] = more
            else:
                u_acc[...] += more
    u_ref[...] = u_acc[...]


def prepare_kernel(cfg, query_ref, weights_ref, rw_ref, keys_ref, logits_ref, *refs):
    order, nh, rows_here, hh, depth, kc, chunk, scale = cfg
    sends = len(order) // 2
    rows = rows_here * hh
    parts = chunk // lanes
    message_ref, rw_out_ref, key_refs = refs[0], refs[1], refs[2 : 2 + sends]
    query_here, weights_here, rw_here, wide, sems = refs[-5:]
    share = pl.multiple_of(lax.axis_index("head") * chunk, chunk)
    copies = []

    def copy(source, target):
        copies.append(pltpu.make_async_copy(source, target, sems.at[len(copies)]))
        copies[-1].start()

    copy(query_ref, query_here)
    copy(rw_ref, rw_here)
    copy(weights_ref, weights_here)
    for i in reversed(range(sends)):
        copy(keys_ref.at[pl.ds(share, chunk), :], key_refs[i].at[:chunk, :])
        for core in range(2):
            row = pl.multiple_of((lax.axis_index("ctx") ^ (2 * i) ^ core) * rows_here, rows_here)
            for part in range(parts):
                first = chunk + (parts * core + part) * rows_here
                copy(
                    logits_ref.at[pl.ds(row, rows_here), pl.ds(share + part * lanes, lanes)],
                    key_refs[i].at[first : first + rows_here, :],
                )
    for item in copies[:3]:
        item.wait()
    every = jnp.broadcast_to(rw_here[...], (8, rw_here.shape[1]))
    shift = every.shape[1] - lax.axis_index("ctx") * rows_here
    here = pltpu.roll(every, shift, 1)[:1, : rw_out_ref.shape[1]]
    rw_out_ref[...] = here * float(kc * len(order)) ** 0.5
    wide[...] = query_here[...].astype(jnp.float32)
    for head in range(hh):
        at = slice(head * rows_here, (head + 1) * rows_here)
        message_ref[at, :] = wide[:, head, :].astype(jnp.bfloat16)
    message_ref[rows:, :] = jnp.zeros((message_ref.shape[0] - rows, lanes), jnp.bfloat16)
    message_ref[rows : rows + hh, :rows_here] = weights_here[...]
    for item in copies[3:]:
        item.wait()


def add_kernel(u_ref, moving_ref, out_ref):
    out_ref[...] = (u_ref[...] + moving_ref[...].astype(jnp.float32)).astype(out_ref.dtype)


def finish_kernel(cfg, u_ref, moving_ref, q_ref, query_grad_ref, weight_grad_ref):
    order, nh, rows_here, hh, depth, kc, chunk, scale = cfg
    rows = rows_here * hh
    eye = (
        lax.broadcasted_iota(jnp.int32, (rows_here, lanes), 0)
        == lax.broadcasted_iota(jnp.int32, (rows_here, lanes), 1)
    ).astype(jnp.float32)
    lane = lax.broadcasted_iota(jnp.int32, (lanes, lanes), 1)[:rows_here]
    slab = q_ref[rows:, :].astype(jnp.float32)
    out = jnp.zeros((rows_here, lanes), jnp.float32)
    for head in range(hh):
        at = slice(head * rows_here, (head + 1) * rows_here)
        total = u_ref[at, :] + moving_ref[at, :].astype(jnp.float32)
        w = jnp.sum(slab[head : head + 1] * eye, axis=1, keepdims=True) * scale
        query_grad_ref[:, head, :] = total * w
        along = jnp.sum(total * q_ref[at, :].astype(jnp.float32), axis=1, keepdims=True)
        out = jnp.where(lane == head, along * scale, out)
    if rows_here < lanes:
        out = jnp.concatenate([out, jnp.zeros((lanes - rows_here, lanes), jnp.float32)], axis=0)
    weight_grad_ref[...] = out.T[:hh, :rows_here]


def per_device(query, weights, keys, main_logits, row_weight, offset):
    n = lax.axis_size("ctx")
    nh = lax.axis_size("head")
    c = lax.axis_index("ctx")
    h = lax.axis_index("head")
    rows_here, hh, depth = query.shape
    kc = keys.shape[0]
    chunk = kc // nh
    rows = rows_here * hh
    scale = depth ** (-0.5)
    bf16, f32 = jnp.bfloat16, jnp.float32

    groups = [
        [1, 0],
        list(range(3, n - 2, 2)) + list(range(2, n - 2, 2)),
        [n - 1, n - 2],
    ]
    order = sum(groups, [])
    cfg = (order, nh, rows_here, hh, depth, kc, chunk, scale)
    smem = pl.BlockSpec(memory_space=pltpu.SMEM)
    vmem = pl.BlockSpec(memory_space=pltpu.VMEM)
    padded = -(-rows_here // lanes) * lanes
    table = [order.index(k) for k in list(range(1, n, 2)) + list(range(0, n, 2))]
    meta = jnp.concatenate(
        [offset, jnp.stack([c, h]).astype(jnp.int32), jnp.array(table, jnp.int32)]
    )

    far = lambda x: pltpu.with_memory_space_constraint(x, pltpu.HBM)

    slab_rows = -(-hh // 16) * 16
    parts = chunk // lanes
    message, rw, *key_messages = pl.pallas_call(
        functools.partial(prepare_kernel, cfg),
        out_shape=[
            jax.ShapeDtypeStruct((rows + slab_rows, depth), bf16),
            jax.ShapeDtypeStruct((1, padded), f32),
        ]
        + [jax.ShapeDtypeStruct((chunk + 2 * parts * rows_here, depth), bf16)] * (n // 2),
        in_specs=[pl.BlockSpec(memory_space=pltpu.HBM)] * 5,
        out_specs=[vmem] * (2 + n // 2),
        scratch_shapes=[
            pltpu.VMEM((rows_here, hh, depth), bf16),
            pltpu.VMEM((hh, rows_here), bf16),
            pltpu.VMEM((1, rows_here * n), f32),
            pltpu.VMEM((rows_here, hh, depth), f32),
            pltpu.SemaphoreType.DMA((3 + n // 2 * (1 + 2 * parts),)),
        ],
        compiler_params=pltpu.CompilerParams(vmem_limit_bytes=vmem_bytes),
        cost_estimate=pl.CostEstimate(
            flops=rows * depth, bytes_accessed=4 * 1024 * 1024, transcendentals=0
        ),
        name="prepare",
    )(far(query), far(weights.T), far(row_weight[None, :]), far(keys), far(main_logits))
    q_blocks = [message] * nh
    for hop in range(1, nh // 2 + 1):
        q_blocks[hop] = ring_next(q_blocks[hop - 1], "head")
        if nh - hop > hop:
            q_blocks[nh - hop] = ring_next(q_blocks[(nh - hop + 1) % nh], "head", -1)
    arrival = [1]
    for hop in range(1, nh // 2 + 1):
        arrival += [j for j in sorted({hop, nh - hop}) if j not in arrival]

    k_pieces = [None] * n
    k_pieces[0::2] = [key_messages[0]] + [
        swap(key_messages[k // 2], "ctx", k) for k in range(2, n, 2)
    ]
    k_pieces[1] = swap(k_pieces[0], "ctx", 1)
    total_keys = n * chunk
    macs = rows * total_keys * depth
    tile = chunk

    def call(kernel, operands, out_shape, scratch, products, name, aliases={}):
        return pl.pallas_call(
            kernel,
            out_shape=out_shape,
            input_output_aliases=aliases,
            in_specs=[smem] + [vmem] * len(operands),
            out_specs=[vmem] * len(out_shape),
            scratch_shapes=scratch,
            compiler_params=pltpu.CompilerParams(vmem_limit_bytes=vmem_bytes),
            cost_estimate=pl.CostEstimate(
                flops=int(4 * products * macs),
                bytes_accessed=int(4 * products * 2**20),
                transcendentals=0,
            ),
            name=name,
        )(meta, *operands)

    near = lambda x: pltpu.with_memory_space_constraint(x, pltpu.VMEM)

    wide_shape = pltpu.VMEM((hh, rows_here, lanes), f32)
    qw_shape = pltpu.VMEM((depth, rows), bf16)

    def keys_shapes(count):
        return [
            pltpu.VMEM((rows_here, count), f32),
            pltpu.VMEM((count, depth), bf16),
            pltpu.VMEM((depth, count), bf16),
            pltpu.VMEM((rows_here, count), bf16),
        ]

    nears = lambda xs: [near(x) for x in xs]
    early, qw, wides = [], [], []
    for i, group in enumerate(groups[:2]):
        if i == 1:
            far_even = range(2, n - 2, 2)
            wides[0], *came = lax.optimization_barrier((wides[0], *(k_pieces[k] for k in far_even)))
            for k, piece in zip(far_even, came):
                k_pieces[k], k_pieces[k + 1] = piece, swap(piece, "ctx", 1)
        count = (len(group) + i * len(groups[0])) * chunk
        outs = call(
            functools.partial(forward_early_kernel, cfg, groups[0] if i == 1 else [], group),
            q_blocks[: i + 1] + nears(wides) + nears(early) + [k_pieces[k] for k in group],
            keys_shapes(count) + [pltpu.VMEM((rows, count), bf16)] * i + [qw_shape, wide_shape],
            [],
            0.001,
            f"forward_early_{i}",
        )
        early = list(outs[:4])
        qw.append(outs[-2])
        wides.append(outs[-1])
    early_active = outs[4]
    early[0], came = lax.optimization_barrier((early[0], k_pieces[n - 2]))
    k_pieces[n - 2], k_pieces[n - 1] = came, swap(came, "ctx", 1)
    last = len(groups[2]) * chunk
    outs = call(
        functools.partial(forward_middle_kernel, cfg, [groups[0] + groups[1], groups[2]]),
        q_blocks[:2]
        + nears(wides)
        + [q_blocks[j] for j in arrival[1:-1]]
        + nears(early)
        + [k_pieces[k] for k in groups[2]],
        keys_shapes(total_keys)
        + [pltpu.VMEM((rows, last), bf16)]
        + [pltpu.VMEM((rows, total_keys), bf16)] * (nh - 3)
        + [qw_shape] * (nh - 3),
        [pltpu.VMEM((hh, rows_here, lanes), f32)],
        nh - 2.5,
        "forward_middle",
    )
    score, keys_all, keys_t, logits = outs[:4]
    active = {1: [early_active, outs[4]]}
    qw = dict(enumerate(qw))
    for i, j in enumerate(arrival[1:-1]):
        active[j], qw[j] = [outs[5 + i]], outs[5 + nh - 3 + i]
    score, last_active, last_qw, stats = call(
        functools.partial(forward_last_kernel, cfg),
        [q_blocks[arrival[-1]], near(keys_t), near(score), near(logits)],
        [
            pltpu.VMEM((rows_here, total_keys), f32),
            pltpu.VMEM((rows, total_keys), bf16),
            qw_shape,
            jax.ShapeDtypeStruct((1, stat_rows, padded), f32),
        ],
        [pltpu.VMEM((hh, rows_here, lanes), f32)],
        1,
        "forward_last",
        {3: 0},
    )
    active[arrival[-1]], qw[arrival[-1]] = [last_active], last_qw

    all_stats = [stats] + [swap(stats, "head", j) for j in range(1, nh)]

    q_own, _ = lax.optimization_barrier((q_blocks[0], stats))
    outs = call(
        functools.partial(own_active_kernel, cfg),
        [q_own, near(keys_t)],
        [pltpu.VMEM((rows, total_keys // 2), bf16)] * 2,
        [],
        1,
        "own_active",
    )
    rw, *outs = lax.optimization_barrier((rw, *outs))
    own_active = {"first": outs[:1], "second": outs[1:]}

    grad = kg = None

    def backward(items, name):
        nonlocal grad, kg
        is_first = grad is None
        ranges = [item[2] for item in items if item[2] is not None]
        makes_u = any(item[1] for item in items)
        has_before = bool(ranges) and kg is not None
        halved = ranges != [] and ranges[0] != "all"
        operands = []
        for item in items:
            operands += nears(own_active[ranges[0]] if halved else active[item[0]])
        operands += [near(qw[item[0]]) for item in items if item[2] is not None]
        operands += [near(keys_all)]
        operands += all_stats + [rw, near(logits), near(score)] if is_first else [near(grad)]
        aliases = {}
        out_shape = [jax.ShapeDtypeStruct((rows, depth), bf16 if is_first else f32)]
        out_shape = out_shape if makes_u else []
        scratch = [pltpu.VMEM((rows, tile), bf16)] * 2 + [pltpu.VMEM((rows, depth), f32)]
        if not halved:
            if ranges:
                if has_before:
                    aliases = {len(operands) + 1: len(out_shape)}
                out_shape += [pltpu.VMEM((depth, total_keys), f32)]
        else:
            if ranges[0] == "first":
                out_shape += [jax.ShapeDtypeStruct((n // 2, chunk, depth), bf16)]
            else:
                out_shape += [jax.ShapeDtypeStruct((chunk, depth), f32)] * (n // 2)
            out_shape += [pltpu.VMEM((rows, total_keys // 2), bf16)]
            scratch = [pltpu.VMEM((depth, total_keys // 2), f32)]
        if has_before:
            operands += [near(kg)]
        if is_first:
            out_shape += [pltpu.VMEM((rows_here, total_keys), bf16)]
            scratch += [pltpu.VMEM((padded, lanes), f32)]
        kernel = functools.partial(backward_kernel, cfg, items, has_before)
        products = 1 if halved else makes_u + len(ranges)
        outs = call(kernel, operands, out_shape, scratch, products, name, aliases)
        if is_first:
            grad = outs[-1]
        if ranges and ranges[0] == "all":
            kg = outs[1 if makes_u else 0]
        return outs

    part = backward([(1, True, None)], "backward_1")[0]
    moving = ring_next(part, "head")
    for j in range(2, nh):
        items = [(j - 1, False, "all"), (j, True, "all" if j == nh - 1 else None)]
        part = backward(items, f"backward_{j}")[0]
        part = pl.pallas_call(
            add_kernel,
            out_shape=jax.ShapeDtypeStruct((rows, depth), bf16),
            in_specs=[vmem] * 2,
            out_specs=vmem,
            compiler_params=pltpu.CompilerParams(vmem_limit_bytes=vmem_bytes),
            cost_estimate=pl.CostEstimate(
                flops=rows * depth, bytes_accessed=8 * rows * depth, transcendentals=0
            ),
            name=f"add_{j}",
        )(part, moving)
        kg, part = lax.optimization_barrier((kg, part))
        moving = ring_next(part, "head")

    odd, mask_first = backward([(0, False, "first")], "backward_0_first")
    other = swap(odd, "ctx", 1)
    *even, mask_second = backward([(0, False, "second")], "backward_0_second")
    even = [even[i] + other[i].astype(f32) for i in range(n // 2)]
    key_grad = even[0]
    sends = [even[i].astype(bf16) for i in range(1, n // 2)]
    keys_all, *sends = lax.optimization_barrier((keys_all, *sends))
    for i in range(1, n // 2):
        key_grad = key_grad + swap(sends[i - 1], "ctx", 2 * i).astype(f32)
    (u_mine,) = call(
        functools.partial(query_kernel, cfg),
        [near(mask_first), near(mask_second), near(keys_all)],
        [jax.ShapeDtypeStruct((rows, depth), f32)],
        [pltpu.VMEM((rows, depth), f32)],
        1,
        "backward_0",
    )

    query_grad, weight_grad = pl.pallas_call(
        functools.partial(finish_kernel, cfg),
        out_shape=[
            jax.ShapeDtypeStruct((rows_here, hh, depth), f32),
            jax.ShapeDtypeStruct((hh, rows_here), f32),
        ],
        in_specs=[vmem] * 3,
        out_specs=[vmem] * 2,
        compiler_params=pltpu.CompilerParams(vmem_limit_bytes=vmem_bytes),
        cost_estimate=pl.CostEstimate(
            flops=8 * rows * depth, bytes_accessed=14 * rows * depth, transcendentals=0
        ),
        name="finish",
    )(u_mine, moving, q_blocks[0])
    return query_grad, key_grad, weight_grad.T


def solution(mesh):
    in_specs = (P("ctx", "head", None), P("ctx", "head"), P("ctx", None), P(None, "ctx"), P(), P())
    out_specs = (P("ctx", "head", None), P(("ctx", "head"), None), P("ctx", "head"))
    return jax.shard_map(
        per_device, mesh=mesh, in_specs=in_specs, out_specs=out_specs, check_vma=False
    )
```

```python
import functools

import jax
import jax.numpy as jnp
from jax import lax
from jax.experimental import pallas as pl
from jax.experimental.pallas import tpu as pltpu
from jax.sharding import PartitionSpec as P

masked_value = -1e30
lanes = 128
stat_rows = 8
vmem_bytes = 6 * 1024 * 1024
contract_last = (((1,), (1,)), ((), ()))


def swap(value, axis, distance):
    size = lax.axis_size(axis)
    return lax.ppermute(value, axis, [(i, i ^ distance) for i in range(size)])


def ring_next(value, axis, hop=1):
    size = lax.axis_size(axis)
    ring = list(range(0, size, 2)) + list(range(1, size, 2))[::-1]
    return lax.ppermute(value, axis, [(ring[i], ring[(i + hop) % size]) for i in range(size)])


def in_pairs(count, first, step):
    first(0, 0)
    if count <= 8:
        for i in range(count):
            step(i % 2, i, i + 1 if i + 1 < count else None)
        return

    def body(i, _):
        step(0, 2 * i, 2 * i + 1)
        step(1, 2 * i + 1, 2 * i + 2)
        return 0

    lax.fori_loop(0, count // 2 - 1, body, 0)
    step(0, count - 2, count - 1)
    step(1, count - 1, None)


def row_limits(meta_ref, rows_here):
    row = lax.broadcasted_iota(jnp.int32, (rows_here, 1), 0)
    return meta_ref[0] + meta_ref[1] * rows_here + row


def piece_allowed(meta_ref, limit, k, kc, chunk):
    first = (meta_ref[1] ^ k) * kc + meta_ref[2] * chunk
    position = first + lax.broadcasted_iota(jnp.int32, (limit.shape[0], chunk), 1)
    return position <= limit


def spread_weights(cfg, q_ref, wide_ref, qw_ref):
    order, nh, rows_here, hh, depth, kc, chunk, scale = cfg
    rows = rows_here * hh
    eye = (
        lax.broadcasted_iota(jnp.int32, (rows_here, lanes), 0)
        == lax.broadcasted_iota(jnp.int32, (rows_here, lanes), 1)
    ).astype(jnp.float32)
    slab = q_ref[rows:, :].astype(jnp.float32)
    for head in range(hh):
        picked = jnp.sum(slab[head : head + 1] * eye, axis=1, keepdims=True)
        wide_ref[head] = jnp.broadcast_to(picked, (rows_here, lanes))
    for head in range(0, hh, 2):
        at = slice(head * rows_here, (head + 2) * rows_here)
        q = q_ref[at, :].astype(jnp.float32)
        w = wide_ref[head : head + 2].reshape(2 * rows_here, lanes) * scale
        qw_ref[:, at] = (q * w).T.astype(jnp.bfloat16)


def unpack(cfg, message_ref, k, at, keys_ref, keys_t_ref, logits_ref):
    order, nh, rows_here, hh, depth, kc, chunk, scale = cfg
    keys = message_ref[:chunk, :]
    keys_ref[at : at + chunk, :] = keys
    keys_t_ref[:, at : at + chunk] = keys.astype(jnp.float32).T.astype(jnp.bfloat16)
    for i in range(chunk // lanes):
        first = chunk + (chunk // lanes * (k % 2) + i) * rows_here
        column = at + i * lanes
        logits_ref[:, column : column + lanes] = message_ref[first : first + rows_here, :]


def add_scores(cfg, q_ref, wide_ref, keys_t_ref, score_ref, before_ref, start, count, active_ref):
    order, nh, rows_here, hh, depth, kc, chunk, scale = cfg
    rows = rows_here * hh
    side = min(256, count)
    tile = next(size * side for size in (16, 12, 8, 6, 4, 2, 1) if count % (size * side) == 0)

    def step(s, _):
        for first in range(0, tile, side):
            local = pl.ds(pl.multiple_of(s * tile + first, side), side)
            columns = pl.ds(pl.multiple_of(start + s * tile + first, side), side)
            dots = jnp.dot(
                q_ref[:rows, :], keys_t_ref[:, columns], preferred_element_type=jnp.float32
            )
            total = [None] * (rows_here // 16)
            for head in range(hh):
                for t in range(rows_here // 16):
                    row = head * rows_here + t * 16
                    w = wide_ref[head, t * 16 : t * 16 + 16, :]
                    w = jnp.concatenate([w] * (side // lanes), axis=1)
                    active = jnp.maximum(dots[row : row + 16, :], 0.0)
                    if active_ref is not None:
                        active_ref[row : row + 16, local] = active.astype(jnp.bfloat16)
                    value = active * w
                    total[t] = value if head == 0 else total[t] + value
            for t, value in enumerate(total):
                at = slice(t * 16, t * 16 + 16)
                value = value * scale
                if before_ref is not None:
                    value = before_ref[at, columns] + value
                score_ref[at, columns] = value
        return 0

    lax.fori_loop(0, count // tile, step, 0)


def forward_early_kernel(cfg, done, pieces, meta_ref, *refs):
    chunk = cfg[6]
    refs = list(refs)
    take = lambda count: [refs.pop(0) for _ in range(count)]
    q_refs = take(2 if done else 1)
    start, count = len(done) * chunk, len(pieces) * chunk
    if done:
        (own_wide_ref,) = take(1)
        part = take(4)
    message_refs = take(len(pieces))
    score_ref, keys_ref, keys_t_ref, logits_ref = take(4)
    active_ref = take(1)[0] if done else None
    qw_ref, wide_ref = take(2)
    spread_weights(cfg, q_refs[-1], wide_ref, qw_ref)
    if done:
        score_ref[:, :start] = part[0][...]
        keys_ref[:start, :] = part[1][...]
        keys_t_ref[:, :start] = part[2][...]
        logits_ref[:, :start] = part[3][...]
    else:
        own_wide_ref = wide_ref
    for i, k in enumerate(pieces):
        unpack(cfg, message_refs[i], k, start + i * chunk, keys_ref, keys_t_ref, logits_ref)
    add_scores(cfg, q_refs[0], own_wide_ref, keys_t_ref, score_ref, None, start, count, None)
    if done:
        count = start + count
        add_scores(cfg, q_refs[1], wide_ref, keys_t_ref, score_ref, score_ref, 0, count, active_ref)


def forward_middle_kernel(cfg, groups, meta_ref, *refs):
    order, nh, rows_here, hh, depth, kc, chunk, scale = cfg
    refs = list(refs)
    take = lambda count: [refs.pop(0) for _ in range(count)]
    q_refs, wide_refs = take(2), take(2)
    new_q_refs = take(nh - 3)
    parts = [take(4) for _ in groups[:-1]]
    message_refs = take(len(groups[-1]))
    whole = take(4)
    score_ref, keys_ref, keys_t_ref, logits_ref = whole
    (last_active_ref,) = take(1)
    active_refs, qw_refs = take(nh - 3), take(nh - 3)
    (wide,) = take(1)
    start = 0
    for group, part in zip(groups, parts):
        end = start + len(group) * chunk
        score_ref[:, start:end] = part[0][...]
        keys_ref[start:end, :] = part[1][...]
        keys_t_ref[:, start:end] = part[2][...]
        logits_ref[:, start:end] = part[3][...]
        start = end
    for i, k in enumerate(groups[-1]):
        unpack(cfg, message_refs[i], k, start + i * chunk, keys_ref, keys_t_ref, logits_ref)
    count = len(groups[-1]) * chunk
    add_scores(cfg, q_refs[0], wide_refs[0], keys_t_ref, score_ref, None, start, count, None)
    add_scores(
        cfg, q_refs[1], wide_refs[1], keys_t_ref, score_ref, score_ref, start, count, last_active_ref
    )
    for q_ref, active_ref, qw_ref in zip(new_q_refs, active_refs, qw_refs):
        spread_weights(cfg, q_ref, wide, qw_ref)
        every = len(order) * chunk
        add_scores(cfg, q_ref, wide, keys_t_ref, score_ref, score_ref, 0, every, active_ref)


def forward_last_kernel(cfg, meta_ref, *refs):
    order, nh, rows_here, hh, depth, kc, chunk, scale = cfg
    q_ref, keys_t_ref, before_ref, logits_ref, score_ref, active_ref, qw_ref, stats_ref, wide = refs
    spread_weights(cfg, q_ref, wide, qw_ref)
    every = len(order) * chunk
    add_scores(cfg, q_ref, wide, keys_t_ref, score_ref, before_ref, 0, every, active_ref)

    limit = row_limits(meta_ref, rows_here)
    lane = lax.broadcasted_iota(jnp.int32, (rows_here, lanes), 1)
    out = jnp.zeros((rows_here, lanes), jnp.float32)

    def piece(i, at):
        if i == 0:
            return score_ref[:, at * chunk : (at + 1) * chunk]
        return logits_ref[:, at * chunk : (at + 1) * chunk].astype(jnp.float32)

    for i in range(2):
        peak = None
        for at, k in enumerate(order):
            allowed = piece_allowed(meta_ref, limit, k, kc, chunk)
            here = jnp.max(jnp.where(allowed, piece(i, at), masked_value), axis=1, keepdims=True)
            peak = here if peak is None else jnp.maximum(peak, here)
        total = None
        for at, k in enumerate(order):
            allowed = piece_allowed(meta_ref, limit, k, kc, chunk)
            here = jnp.where(allowed, jnp.exp(piece(i, at) - peak), 0.0)
            here = jnp.sum(here, axis=1, keepdims=True)
            total = here if total is None else total + here
        out = jnp.where(lane == 2 * i, peak, out)
        out = jnp.where(lane == 2 * i + 1, total, out)
    padded = stats_ref.shape[2]
    if padded > rows_here:
        out = jnp.concatenate([out, jnp.zeros((padded - rows_here, lanes), jnp.float32)], axis=0)
    stats_ref[0] = out.T[:stat_rows]


def score_gradient(cfg, meta_ref, stats, rw_ref, logits_ref, score_ref, cols, grad_ref):
    order, nh, rows_here, hh, depth, kc, chunk, scale = cfg
    for i in range(2):
        peak = functools.reduce(jnp.maximum, [st[2 * i : 2 * i + 1] for st in stats])
        total = functools.reduce(
            jnp.add,
            [st[2 * i + 1 : 2 * i + 2] * jnp.exp(st[2 * i : 2 * i + 1] - peak) for st in stats],
        )
        cols[2 * i : 2 * i + 1, :] = peak
        cols[2 * i + 1 : 2 * i + 2, :] = rw_ref[...] / total
    cols[4:, :] = jnp.zeros((cols.shape[0] - 4, cols.shape[1]), jnp.float32)
    st = cols[...].T[:rows_here]
    limit = row_limits(meta_ref, rows_here)
    for at, k in enumerate(order):
        logits = logits_ref[:, at * chunk : (at + 1) * chunk].astype(jnp.float32)
        score = score_ref[:, at * chunk : (at + 1) * chunk]
        g = jnp.exp(score - st[:, 0:1]) * st[:, 1:2] - jnp.exp(logits - st[:, 2:3]) * st[:, 3:4]
        g = jnp.where(piece_allowed(meta_ref, limit, k, kc, chunk), g, 0.0)
        grad_ref[:, at * chunk : (at + 1) * chunk] = g.astype(jnp.bfloat16)


def backward_kernel(cfg, items, has_before, meta_ref, *refs):
    order, nh, rows_here, hh, depth, kc, chunk, scale = cfg
    n = len(order)
    rows = rows_here * hh
    refs = list(refs)
    take = lambda count: [refs.pop(0) for _ in range(count)]
    is_first = items[0][0] == 1 and items[0][2] is None
    makes_u = any(item[1] for item in items)
    ranges = [item[2] for item in items if item[2] is not None]
    half = ranges[0] if ranges and ranges[0] != "all" else None
    sources = [take(2 if item[0] == 1 else 1) for item in items]
    qw_refs = [take(1)[0] if item[2] is not None else None for item in items]
    (keys_ref,) = take(1)
    if is_first:
        stat_refs = take(nh)
        rw_ref, logits_ref, score_ref = take(3)
    else:
        (grad_ref,) = take(1)
    before_ref = take(1)[0] if has_before else None
    if makes_u:
        (u_ref,) = take(1)
    if ranges:
        kg_refs = take(n // 2 if half == "second" else 1)
    if is_first:
        (grad_ref,) = take(1)
    if half is not None:
        mask_ref, kg_acc = take(2)
    else:
        masks = take(2)
        (u_acc,) = take(1)
    if is_first:
        (cols,) = take(1)
        stats = [ref[0] for ref in stat_refs]
        score_gradient(cfg, meta_ref, stats, rw_ref, logits_ref, score_ref, cols, grad_ref)
    tile = chunk
    chunks = max(1, min(4, hh))
    heads = hh // chunks
    part = heads * rows_here
    side = tile // 2

    todo = []
    for index, (_, is_u, keys_range) in enumerate(items):
        base = 0
        for ref in sources[index]:
            tiles = n // 2 if half is not None else ref.shape[1] // tile
            todo.append((index, is_u, keys_range, ref, base, tiles))
            base += tiles

    for index, is_u, keys_range, source_ref, base, tiles in todo:
        qw_ref = qw_refs[index]
        is_start = index == 0 or items[index - 1][2] is None

        def tile_at(s, first=0, size=tile, base=base):
            if half is None:
                position = s + base
            else:
                position = meta_ref[3 + (n // 2 if half == "second" else 0) + s]
            return pl.ds(pl.multiple_of(position * tile + first, size), size)

        def local(s, first=0, size=tile):
            return pl.ds(pl.multiple_of(s * tile + first, size), size)

        def mask_at(buffer, s, at, first=0, size=tile):
            if half is None:
                return masks[buffer].at[at, first : first + size]
            return mask_ref.at[at, local(s, first, size)]

        def mask_part(buffer, s, i, source_ref=source_ref):
            at = slice(i * part, (i + 1) * part)
            g = grad_ref[:, tile_at(s)]
            value = source_ref[at, local(s)]
            wide = jnp.broadcast_to(g[None], (heads, rows_here, tile)).reshape(part, tile)
            value = jnp.where(value > 0, wide, jnp.zeros_like(wide))
            mask_at(buffer, s, at)[...] = value.astype(jnp.bfloat16)

        def mask(buffer, s):
            for i in range(chunks):
                mask_part(buffer, s, i)

        def step(buffer, s, following):
            for i in range(chunks):
                if following is not None:
                    mask_part(1 - buffer, following, i)
                if is_u:
                    at = slice(i * part, (i + 1) * part)
                    u_acc[at, :] += jnp.dot(
                        mask_at(buffer, s, at)[...],
                        keys_ref[tile_at(s), :],
                        preferred_element_type=jnp.float32,
                    )
                if keys_range is None or i % (chunks // 2) != chunks // 2 - 1:
                    continue
                first = i // (chunks // 2) * side
                more = jnp.dot(
                    qw_ref[...],
                    mask_at(buffer, s, slice(0, rows), first, side)[...],
                    preferred_element_type=jnp.float32,
                )
                here = tile_at(s, first, side)
                if not is_start:
                    more = kg_refs[0][:, here] + more
                elif before_ref is not None:
                    more = before_ref[:, here] + more
                if half is None:
                    kg_refs[0][:, here] = more
                else:
                    kg_acc[:, local(s, first, side)] = more

        if is_u and base == 0:
            u_acc[...] = jnp.zeros_like(u_acc)
        in_pairs(tiles, mask, step)
        if is_u and (base + tiles) == n:
            u_ref[...] = u_acc[...].astype(u_ref.dtype)

    if half is not None:
        for i in range(n // 2):
            value = kg_acc[:, i * chunk : (i + 1) * chunk].T
            if half == "first":
                kg_refs[0][i] = value.astype(kg_refs[0].dtype)
            else:
                kg_refs[i][...] = value


def own_active_kernel(cfg, meta_ref, q_ref, keys_t_ref, first_ref, second_ref):
    order, nh, rows_here, hh, depth, kc, chunk, scale = cfg
    side = min(256, chunk)
    for half, active_ref in enumerate((first_ref, second_ref)):
        for s, k in enumerate(range(1 - half, len(order), 2)):
            for first in range(0, chunk, side):
                column = order.index(k) * chunk + first
                dots = jnp.dot(
                    q_ref[: rows_here * hh, :],
                    keys_t_ref[:, column : column + side],
                    preferred_element_type=jnp.float32,
                )
                active = jnp.maximum(dots, 0.0).astype(jnp.bfloat16)
                active_ref[:, s * chunk + first : s * chunk + first + side] = active


def query_kernel(cfg, meta_ref, first_ref, second_ref, keys_ref, u_ref, u_acc):
    order, chunk = cfg[0], cfg[6]
    for half, mask_ref in enumerate((first_ref, second_ref)):
        for s, k in enumerate(range(1 - half, len(order), 2)):
            position = order.index(k)
            more = jnp.dot(
                mask_ref[:, s * chunk : (s + 1) * chunk],
                keys_ref[position * chunk : (position + 1) * chunk, :],
                preferred_element_type=jnp.float32,
            )
            if half == 0 and s == 0:
                u_acc[...] = more
            else:
                u_acc[...] += more
    u_ref[...] = u_acc[...]


def prepare_kernel(cfg, query_ref, weights_ref, rw_ref, keys_ref, logits_ref, *refs):
    order, nh, rows_here, hh, depth, kc, chunk, scale = cfg
    sends = len(order) // 2
    rows = rows_here * hh
    parts = chunk // lanes
    message_ref, rw_out_ref, key_refs = refs[0], refs[1], refs[2 : 2 + sends]
    query_here, weights_here, rw_here, wide, sems = refs[-5:]
    share = pl.multiple_of(lax.axis_index("head") * chunk, chunk)
    copies = []

    def copy(source, target):
        copies.append(pltpu.make_async_copy(source, target, sems.at[len(copies)]))
        copies[-1].start()

    copy(query_ref, query_here)
    copy(rw_ref, rw_here)
    copy(weights_ref, weights_here)
    for i in reversed(range(sends)):
        copy(keys_ref.at[pl.ds(share, chunk), :], key_refs[i].at[:chunk, :])
        for core in range(2):
            row = pl.multiple_of((lax.axis_index("ctx") ^ (2 * i) ^ core) * rows_here, rows_here)
            for part in range(parts):
                first = chunk + (parts * core + part) * rows_here
                copy(
                    logits_ref.at[pl.ds(row, rows_here), pl.ds(share + part * lanes, lanes)],
                    key_refs[i].at[first : first + rows_here, :],
                )
    for item in copies[:3]:
        item.wait()
    every = jnp.broadcast_to(rw_here[...], (8, rw_here.shape[1]))
    shift = every.shape[1] - lax.axis_index("ctx") * rows_here
    here = pltpu.roll(every, shift, 1)[:1, : rw_out_ref.shape[1]]
    rw_out_ref[...] = here * float(kc * len(order)) ** 0.5
    wide[...] = query_here[...].astype(jnp.float32)
    for head in range(hh):
        at = slice(head * rows_here, (head + 1) * rows_here)
        message_ref[at, :] = wide[:, head, :].astype(jnp.bfloat16)
    message_ref[rows:, :] = jnp.zeros((message_ref.shape[0] - rows, lanes), jnp.bfloat16)
    message_ref[rows : rows + hh, :rows_here] = weights_here[...]
    for item in copies[3:]:
        item.wait()


def add_kernel(u_ref, moving_ref, out_ref):
    out_ref[...] = (u_ref[...] + moving_ref[...].astype(jnp.float32)).astype(out_ref.dtype)


def finish_kernel(cfg, u_ref, moving_ref, q_ref, query_grad_ref, weight_grad_ref):
    order, nh, rows_here, hh, depth, kc, chunk, scale = cfg
    rows = rows_here * hh
    eye = (
        lax.broadcasted_iota(jnp.int32, (rows_here, lanes), 0)
        == lax.broadcasted_iota(jnp.int32, (rows_here, lanes), 1)
    ).astype(jnp.float32)
    lane = lax.broadcasted_iota(jnp.int32, (lanes, lanes), 1)[:rows_here]
    slab = q_ref[rows:, :].astype(jnp.float32)
    out = jnp.zeros((rows_here, lanes), jnp.float32)
    for head in range(hh):
        at = slice(head * rows_here, (head + 1) * rows_here)
        total = u_ref[at, :] + moving_ref[at, :].astype(jnp.float32)
        w = jnp.sum(slab[head : head + 1] * eye, axis=1, keepdims=True) * scale
        query_grad_ref[:, head, :] = total * w
        along = jnp.sum(total * q_ref[at, :].astype(jnp.float32), axis=1, keepdims=True)
        out = jnp.where(lane == head, along * scale, out)
    if rows_here < lanes:
        out = jnp.concatenate([out, jnp.zeros((lanes - rows_here, lanes), jnp.float32)], axis=0)
    weight_grad_ref[...] = out.T[:hh, :rows_here]


def per_device(query, weights, keys, main_logits, row_weight, offset):
    n = lax.axis_size("ctx")
    nh = lax.axis_size("head")
    c = lax.axis_index("ctx")
    h = lax.axis_index("head")
    rows_here, hh, depth = query.shape
    kc = keys.shape[0]
    chunk = kc // nh
    rows = rows_here * hh
    scale = depth ** (-0.5)
    bf16, f32 = jnp.bfloat16, jnp.float32

    groups = [
        [1, 0],
        list(range(3, n - 2, 2)) + list(range(2, n - 2, 2)),
        [n - 1, n - 2],
    ]
    order = sum(groups, [])
    cfg = (order, nh, rows_here, hh, depth, kc, chunk, scale)
    smem = pl.BlockSpec(memory_space=pltpu.SMEM)
    vmem = pl.BlockSpec(memory_space=pltpu.VMEM)
    padded = -(-rows_here // lanes) * lanes
    table = [order.index(k) for k in list(range(1, n, 2)) + list(range(0, n, 2))]
    meta = jnp.concatenate(
        [offset, jnp.stack([c, h]).astype(jnp.int32), jnp.array(table, jnp.int32)]
    )

    far = lambda x: pltpu.with_memory_space_constraint(x, pltpu.HBM)

    slab_rows = -(-hh // 16) * 16
    parts = chunk // lanes
    message, rw, *key_messages = pl.pallas_call(
        functools.partial(prepare_kernel, cfg),
        out_shape=[
            jax.ShapeDtypeStruct((rows + slab_rows, depth), bf16),
            jax.ShapeDtypeStruct((1, padded), f32),
        ]
        + [jax.ShapeDtypeStruct((chunk + 2 * parts * rows_here, depth), bf16)] * (n // 2),
        in_specs=[pl.BlockSpec(memory_space=pltpu.HBM)] * 5,
        out_specs=[vmem] * (2 + n // 2),
        scratch_shapes=[
            pltpu.VMEM((rows_here, hh, depth), bf16),
            pltpu.VMEM((hh, rows_here), bf16),
            pltpu.VMEM((1, rows_here * n), f32),
            pltpu.VMEM((rows_here, hh, depth), f32),
            pltpu.SemaphoreType.DMA((3 + n // 2 * (1 + 2 * parts),)),
        ],
        compiler_params=pltpu.CompilerParams(vmem_limit_bytes=vmem_bytes),
        cost_estimate=pl.CostEstimate(
            flops=rows * depth, bytes_accessed=4 * 1024 * 1024, transcendentals=0
        ),
        name="prepare",
    )(far(query), far(weights.T), far(row_weight[None, :]), far(keys), far(main_logits))
    q_blocks = [message] * nh
    for hop in range(1, nh // 2 + 1):
        q_blocks[hop] = ring_next(q_blocks[hop - 1], "head")
        if nh - hop > hop:
            q_blocks[nh - hop] = ring_next(q_blocks[(nh - hop + 1) % nh], "head", -1)
    arrival = [1]
    for hop in range(1, nh // 2 + 1):
        arrival += [j for j in sorted({hop, nh - hop}) if j not in arrival]

    k_pieces = [None] * n
    k_pieces[0::2] = [key_messages[0]] + [
        swap(key_messages[k // 2], "ctx", k) for k in range(2, n, 2)
    ]
    k_pieces[1] = swap(k_pieces[0], "ctx", 1)
    total_keys = n * chunk
    macs = rows * total_keys * depth
    tile = chunk

    def call(kernel, operands, out_shape, scratch, products, name, aliases={}):
        return pl.pallas_call(
            kernel,
            out_shape=out_shape,
            input_output_aliases=aliases,
            in_specs=[smem] + [vmem] * len(operands),
            out_specs=[vmem] * len(out_shape),
            scratch_shapes=scratch,
            compiler_params=pltpu.CompilerParams(vmem_limit_bytes=vmem_bytes),
            cost_estimate=pl.CostEstimate(
                flops=int(4 * products * macs),
                bytes_accessed=int(4 * products * 2**20),
                transcendentals=0,
            ),
            name=name,
        )(meta, *operands)

    near = lambda x: pltpu.with_memory_space_constraint(x, pltpu.VMEM)

    wide_shape = pltpu.VMEM((hh, rows_here, lanes), f32)
    qw_shape = pltpu.VMEM((depth, rows), bf16)

    def keys_shapes(count):
        return [
            pltpu.VMEM((rows_here, count), f32),
            pltpu.VMEM((count, depth), bf16),
            pltpu.VMEM((depth, count), bf16),
            pltpu.VMEM((rows_here, count), bf16),
        ]

    nears = lambda xs: [near(x) for x in xs]
    early, qw, wides = [], [], []
    for i, group in enumerate(groups[:2]):
        if i == 1:
            far_even = range(2, n - 2, 2)
            wides[0], *came = lax.optimization_barrier((wides[0], *(k_pieces[k] for k in far_even)))
            for k, piece in zip(far_even, came):
                k_pieces[k], k_pieces[k + 1] = piece, swap(piece, "ctx", 1)
        count = (len(group) + i * len(groups[0])) * chunk
        outs = call(
            functools.partial(forward_early_kernel, cfg, groups[0] if i == 1 else [], group),
            q_blocks[: i + 1] + nears(wides) + nears(early) + [k_pieces[k] for k in group],
            keys_shapes(count) + [pltpu.VMEM((rows, count), bf16)] * i + [qw_shape, wide_shape],
            [],
            0.001,
            f"forward_early_{i}",
        )
        early = list(outs[:4])
        qw.append(outs[-2])
        wides.append(outs[-1])
    early_active = outs[4]
    early[0], came = lax.optimization_barrier((early[0], k_pieces[n - 2]))
    k_pieces[n - 2], k_pieces[n - 1] = came, swap(came, "ctx", 1)
    last = len(groups[2]) * chunk
    outs = call(
        functools.partial(forward_middle_kernel, cfg, [groups[0] + groups[1], groups[2]]),
        q_blocks[:2]
        + nears(wides)
        + [q_blocks[j] for j in arrival[1:-1]]
        + nears(early)
        + [k_pieces[k] for k in groups[2]],
        keys_shapes(total_keys)
        + [pltpu.VMEM((rows, last), bf16)]
        + [pltpu.VMEM((rows, total_keys), bf16)] * (nh - 3)
        + [qw_shape] * (nh - 3),
        [pltpu.VMEM((hh, rows_here, lanes), f32)],
        0.001,
        "forward_middle",
    )
    score, keys_all, keys_t, logits = outs[:4]
    active = {1: [early_active, outs[4]]}
    qw = dict(enumerate(qw))
    for i, j in enumerate(arrival[1:-1]):
        active[j], qw[j] = [outs[5 + i]], outs[5 + nh - 3 + i]
    score, last_active, last_qw, stats = call(
        functools.partial(forward_last_kernel, cfg),
        [q_blocks[arrival[-1]], near(keys_t), near(score), near(logits)],
        [
            pltpu.VMEM((rows_here, total_keys), f32),
            pltpu.VMEM((rows, total_keys), bf16),
            qw_shape,
            jax.ShapeDtypeStruct((1, stat_rows, padded), f32),
        ],
        [pltpu.VMEM((hh, rows_here, lanes), f32)],
        1,
        "forward_last",
        {3: 0},
    )
    active[arrival[-1]], qw[arrival[-1]] = [last_active], last_qw

    all_stats = [stats] + [swap(stats, "head", j) for j in range(1, nh)]

    q_own, _ = lax.optimization_barrier((q_blocks[0], stats))
    outs = call(
        functools.partial(own_active_kernel, cfg),
        [q_own, near(keys_t)],
        [pltpu.VMEM((rows, total_keys // 2), bf16)] * 2,
        [],
        1,
        "own_active",
    )
    rw, *outs = lax.optimization_barrier((rw, *outs))
    own_active = {"first": outs[:1], "second": outs[1:]}

    grad = kg = None

    def backward(items, name):
        nonlocal grad, kg
        is_first = grad is None
        ranges = [item[2] for item in items if item[2] is not None]
        makes_u = any(item[1] for item in items)
        has_before = bool(ranges) and kg is not None
        halved = ranges != [] and ranges[0] != "all"
        operands = []
        for item in items:
            operands += nears(own_active[ranges[0]] if halved else active[item[0]])
        operands += [near(qw[item[0]]) for item in items if item[2] is not None]
        operands += [near(keys_all)]
        operands += all_stats + [rw, near(logits), near(score)] if is_first else [near(grad)]
        aliases = {}
        out_shape = [jax.ShapeDtypeStruct((rows, depth), bf16 if is_first else f32)]
        out_shape = out_shape if makes_u else []
        scratch = [pltpu.VMEM((rows, tile), bf16)] * 2 + [pltpu.VMEM((rows, depth), f32)]
        if not halved:
            if ranges:
                if has_before:
                    aliases = {len(operands) + 1: len(out_shape)}
                out_shape += [pltpu.VMEM((depth, total_keys), f32)]
        else:
            if ranges[0] == "first":
                out_shape += [jax.ShapeDtypeStruct((n // 2, chunk, depth), bf16)]
            else:
                out_shape += [jax.ShapeDtypeStruct((chunk, depth), f32)] * (n // 2)
            out_shape += [pltpu.VMEM((rows, total_keys // 2), bf16)]
            scratch = [pltpu.VMEM((depth, total_keys // 2), f32)]
        if has_before:
            operands += [near(kg)]
        if is_first:
            out_shape += [pltpu.VMEM((rows_here, total_keys), bf16)]
            scratch += [pltpu.VMEM((padded, lanes), f32)]
        kernel = functools.partial(backward_kernel, cfg, items, has_before)
        products = 1 if halved else makes_u + len(ranges)
        outs = call(kernel, operands, out_shape, scratch, products, name, aliases)
        if is_first:
            grad = outs[-1]
        if ranges and ranges[0] == "all":
            kg = outs[1 if makes_u else 0]
        return outs

    part = backward([(1, True, None)], "backward_1")[0]
    moving = ring_next(part, "head")
    for j in range(2, nh):
        items = [(j - 1, False, "all"), (j, True, "all" if j == nh - 1 else None)]
        part = backward(items, f"backward_{j}")[0]
        part = pl.pallas_call(
            add_kernel,
            out_shape=jax.ShapeDtypeStruct((rows, depth), bf16),
            in_specs=[vmem] * 2,
            out_specs=vmem,
            compiler_params=pltpu.CompilerParams(vmem_limit_bytes=vmem_bytes),
            cost_estimate=pl.CostEstimate(
                flops=rows * depth, bytes_accessed=8 * rows * depth, transcendentals=0
            ),
            name=f"add_{j}",
        )(part, moving)
        kg, part = lax.optimization_barrier((kg, part))
        moving = ring_next(part, "head")

    odd, mask_first = backward([(0, False, "first")], "backward_0_first")
    other = swap(odd, "ctx", 1)
    *even, mask_second = backward([(0, False, "second")], "backward_0_second")
    even = [even[i] + other[i].astype(f32) for i in range(n // 2)]
    key_grad = even[0]
    sends = [even[i].astype(bf16) for i in range(1, n // 2)]
    keys_all, *sends = lax.optimization_barrier((keys_all, *sends))
    for i in range(1, n // 2):
        key_grad = key_grad + swap(sends[i - 1], "ctx", 2 * i).astype(f32)
    (u_mine,) = call(
        functools.partial(query_kernel, cfg),
        [near(mask_first), near(mask_second), near(keys_all)],
        [jax.ShapeDtypeStruct((rows, depth), f32)],
        [pltpu.VMEM((rows, depth), f32)],
        1,
        "backward_0",
    )

    query_grad, weight_grad = pl.pallas_call(
        functools.partial(finish_kernel, cfg),
        out_shape=[
            jax.ShapeDtypeStruct((rows_here, hh, depth), f32),
            jax.ShapeDtypeStruct((hh, rows_here), f32),
        ],
        in_specs=[vmem] * 3,
        out_specs=[vmem] * 2,
        compiler_params=pltpu.CompilerParams(vmem_limit_bytes=vmem_bytes),
        cost_estimate=pl.CostEstimate(
            flops=8 * rows * depth, bytes_accessed=14 * rows * depth, transcendentals=0
        ),
        name="finish",
    )(u_mine, moving, q_blocks[0])
    return query_grad, key_grad, weight_grad.T


def solution(mesh):
    in_specs = (P("ctx", "head", None), P("ctx", "head"), P("ctx", None), P(None, "ctx"), P(), P())
    out_specs = (P("ctx", "head", None), P(("ctx", "head"), None), P("ctx", "head"))
    return jax.shard_map(
        per_device, mesh=mesh, in_specs=in_specs, out_specs=out_specs, check_vma=False
    )
```

```python
import functools

import jax
import jax.numpy as jnp
from jax import lax
from jax.experimental import pallas as pl
from jax.experimental.pallas import tpu as pltpu
from jax.sharding import PartitionSpec as P

masked_value = -1e30
lanes = 128
stat_rows = 8
vmem_bytes = 6 * 1024 * 1024
contract_last = (((1,), (1,)), ((), ()))


def swap(value, axis, distance):
    size = lax.axis_size(axis)
    return lax.ppermute(value, axis, [(i, i ^ distance) for i in range(size)])


def ring_next(value, axis, hop=1):
    size = lax.axis_size(axis)
    ring = list(range(0, size, 2)) + list(range(1, size, 2))[::-1]
    return lax.ppermute(value, axis, [(ring[i], ring[(i + hop) % size]) for i in range(size)])


def in_pairs(count, first, step):
    first(0, 0)
    if count <= 8:
        for i in range(count):
            step(i % 2, i, i + 1 if i + 1 < count else None)
        return

    def body(i, _):
        step(0, 2 * i, 2 * i + 1)
        step(1, 2 * i + 1, 2 * i + 2)
        return 0

    lax.fori_loop(0, count // 2 - 1, body, 0)
    step(0, count - 2, count - 1)
    step(1, count - 1, None)


def row_limits(meta_ref, rows_here):
    row = lax.broadcasted_iota(jnp.int32, (rows_here, 1), 0)
    return meta_ref[0] + meta_ref[1] * rows_here + row


def piece_allowed(meta_ref, limit, k, kc, chunk):
    first = (meta_ref[1] ^ k) * kc + meta_ref[2] * chunk
    position = first + lax.broadcasted_iota(jnp.int32, (limit.shape[0], chunk), 1)
    return position <= limit


def spread_weights(cfg, q_ref, wide_ref, qw_ref):
    order, nh, rows_here, hh, depth, kc, chunk, scale = cfg
    rows = rows_here * hh
    eye = (
        lax.broadcasted_iota(jnp.int32, (rows_here, lanes), 0)
        == lax.broadcasted_iota(jnp.int32, (rows_here, lanes), 1)
    ).astype(jnp.float32)
    slab = q_ref[rows:, :].astype(jnp.float32)
    for head in range(hh):
        picked = jnp.sum(slab[head : head + 1] * eye, axis=1, keepdims=True)
        wide_ref[head] = jnp.broadcast_to(picked, (rows_here, lanes))
    for head in range(0, hh, 2):
        at = slice(head * rows_here, (head + 2) * rows_here)
        q = q_ref[at, :].astype(jnp.float32)
        w = wide_ref[head : head + 2].reshape(2 * rows_here, lanes) * scale
        qw_ref[:, at] = (q * w).T.astype(jnp.bfloat16)


def unpack(cfg, message_ref, k, at, keys_ref, keys_t_ref, logits_ref):
    order, nh, rows_here, hh, depth, kc, chunk, scale = cfg
    keys = message_ref[:chunk, :]
    keys_ref[at : at + chunk, :] = keys
    keys_t_ref[:, at : at + chunk] = keys.astype(jnp.float32).T.astype(jnp.bfloat16)
    for i in range(chunk // lanes):
        first = chunk + (chunk // lanes * (k % 2) + i) * rows_here
        column = at + i * lanes
        logits_ref[:, column : column + lanes] = message_ref[first : first + rows_here, :]


def add_scores(cfg, q_ref, wide_ref, keys_t_ref, score_ref, before_ref, start, count, active_ref):
    order, nh, rows_here, hh, depth, kc, chunk, scale = cfg
    rows = rows_here * hh
    side = min(256, count)
    tile = next(size * side for size in (16, 12, 8, 6, 4, 2, 1) if count % (size * side) == 0)

    def step(s, _):
        for first in range(0, tile, side):
            local = pl.ds(pl.multiple_of(s * tile + first, side), side)
            columns = pl.ds(pl.multiple_of(start + s * tile + first, side), side)
            dots = jnp.dot(
                q_ref[:rows, :], keys_t_ref[:, columns], preferred_element_type=jnp.float32
            )
            total = [None] * (rows_here // 16)
            for head in range(hh):
                for t in range(rows_here // 16):
                    row = head * rows_here + t * 16
                    w = wide_ref[head, t * 16 : t * 16 + 16, :]
                    w = jnp.concatenate([w] * (side // lanes), axis=1)
                    active = jnp.maximum(dots[row : row + 16, :], 0.0)
                    if active_ref is not None:
                        active_ref[row : row + 16, local] = active.astype(jnp.bfloat16)
                    value = active * w
                    total[t] = value if head == 0 else total[t] + value
            for t, value in enumerate(total):
                at = slice(t * 16, t * 16 + 16)
                value = value * scale
                if before_ref is not None:
                    value = before_ref[at, columns] + value
                score_ref[at, columns] = value
        return 0

    lax.fori_loop(0, count // tile, step, 0)


def forward_early_kernel(cfg, done, pieces, meta_ref, *refs):
    chunk = cfg[6]
    refs = list(refs)
    take = lambda count: [refs.pop(0) for _ in range(count)]
    q_refs = take(2 if done else 1)
    start, count = len(done) * chunk, len(pieces) * chunk
    if done:
        (own_wide_ref,) = take(1)
        part = take(4)
    message_refs = take(len(pieces))
    score_ref, keys_ref, keys_t_ref, logits_ref = take(4)
    active_ref = take(1)[0] if done else None
    qw_ref, wide_ref = take(2)
    spread_weights(cfg, q_refs[-1], wide_ref, qw_ref)
    if done:
        score_ref[:, :start] = part[0][...]
        keys_ref[:start, :] = part[1][...]
        keys_t_ref[:, :start] = part[2][...]
        logits_ref[:, :start] = part[3][...]
    else:
        own_wide_ref = wide_ref
    for i, k in enumerate(pieces):
        unpack(cfg, message_refs[i], k, start + i * chunk, keys_ref, keys_t_ref, logits_ref)
    add_scores(cfg, q_refs[0], own_wide_ref, keys_t_ref, score_ref, None, start, count, None)
    if done:
        count = start + count
        add_scores(cfg, q_refs[1], wide_ref, keys_t_ref, score_ref, score_ref, 0, count, active_ref)


def forward_middle_kernel(cfg, groups, meta_ref, *refs):
    order, nh, rows_here, hh, depth, kc, chunk, scale = cfg
    refs = list(refs)
    take = lambda count: [refs.pop(0) for _ in range(count)]
    q_refs, wide_refs = take(2), take(2)
    new_q_refs = take(nh - 3)
    parts = [take(4) for _ in groups[:-1]]
    message_refs = take(len(groups[-1]))
    whole = take(4)
    score_ref, keys_ref, keys_t_ref, logits_ref = whole
    (last_active_ref,) = take(1)
    active_refs, qw_refs = take(nh - 3), take(nh - 3)
    (wide,) = take(1)
    start = 0
    for group, part in zip(groups, parts):
        end = start + len(group) * chunk
        score_ref[:, start:end] = part[0][...]
        keys_ref[start:end, :] = part[1][...]
        keys_t_ref[:, start:end] = part[2][...]
        logits_ref[:, start:end] = part[3][...]
        start = end
    for i, k in enumerate(groups[-1]):
        unpack(cfg, message_refs[i], k, start + i * chunk, keys_ref, keys_t_ref, logits_ref)
    count = len(groups[-1]) * chunk
    add_scores(cfg, q_refs[0], wide_refs[0], keys_t_ref, score_ref, None, start, count, None)
    add_scores(
        cfg, q_refs[1], wide_refs[1], keys_t_ref, score_ref, score_ref, start, count, last_active_ref
    )
    for q_ref, active_ref, qw_ref in zip(new_q_refs, active_refs, qw_refs):
        spread_weights(cfg, q_ref, wide, qw_ref)
        every = len(order) * chunk
        add_scores(cfg, q_ref, wide, keys_t_ref, score_ref, score_ref, 0, every, active_ref)


def forward_last_kernel(cfg, meta_ref, *refs):
    order, nh, rows_here, hh, depth, kc, chunk, scale = cfg
    q_ref, keys_t_ref, before_ref, logits_ref, score_ref, active_ref, qw_ref, stats_ref, wide = refs
    spread_weights(cfg, q_ref, wide, qw_ref)
    every = len(order) * chunk
    add_scores(cfg, q_ref, wide, keys_t_ref, score_ref, before_ref, 0, every, active_ref)

    limit = row_limits(meta_ref, rows_here)
    lane = lax.broadcasted_iota(jnp.int32, (rows_here, lanes), 1)
    out = jnp.zeros((rows_here, lanes), jnp.float32)

    def piece(i, at):
        if i == 0:
            return score_ref[:, at * chunk : (at + 1) * chunk]
        return logits_ref[:, at * chunk : (at + 1) * chunk].astype(jnp.float32)

    for i in range(2):
        peak = None
        for at, k in enumerate(order):
            allowed = piece_allowed(meta_ref, limit, k, kc, chunk)
            here = jnp.max(jnp.where(allowed, piece(i, at), masked_value), axis=1, keepdims=True)
            peak = here if peak is None else jnp.maximum(peak, here)
        total = None
        for at, k in enumerate(order):
            allowed = piece_allowed(meta_ref, limit, k, kc, chunk)
            here = jnp.where(allowed, jnp.exp(piece(i, at) - peak), 0.0)
            here = jnp.sum(here, axis=1, keepdims=True)
            total = here if total is None else total + here
        out = jnp.where(lane == 2 * i, peak, out)
        out = jnp.where(lane == 2 * i + 1, total, out)
    padded = stats_ref.shape[2]
    if padded > rows_here:
        out = jnp.concatenate([out, jnp.zeros((padded - rows_here, lanes), jnp.float32)], axis=0)
    stats_ref[0] = out.T[:stat_rows]


def score_gradient(cfg, meta_ref, stats, rw_ref, logits_ref, score_ref, cols, grad_ref):
    order, nh, rows_here, hh, depth, kc, chunk, scale = cfg
    for i in range(2):
        peak = functools.reduce(jnp.maximum, [st[2 * i : 2 * i + 1] for st in stats])
        total = functools.reduce(
            jnp.add,
            [st[2 * i + 1 : 2 * i + 2] * jnp.exp(st[2 * i : 2 * i + 1] - peak) for st in stats],
        )
        cols[2 * i : 2 * i + 1, :] = peak
        cols[2 * i + 1 : 2 * i + 2, :] = rw_ref[...] / total
    cols[4:, :] = jnp.zeros((cols.shape[0] - 4, cols.shape[1]), jnp.float32)
    st = cols[...].T[:rows_here]
    limit = row_limits(meta_ref, rows_here)
    for at, k in enumerate(order):
        logits = logits_ref[:, at * chunk : (at + 1) * chunk].astype(jnp.float32)
        score = score_ref[:, at * chunk : (at + 1) * chunk]
        g = jnp.exp(score - st[:, 0:1]) * st[:, 1:2] - jnp.exp(logits - st[:, 2:3]) * st[:, 3:4]
        g = jnp.where(piece_allowed(meta_ref, limit, k, kc, chunk), g, 0.0)
        grad_ref[:, at * chunk : (at + 1) * chunk] = g.astype(jnp.bfloat16)


def backward_kernel(cfg, items, has_before, meta_ref, *refs):
    order, nh, rows_here, hh, depth, kc, chunk, scale = cfg
    n = len(order)
    rows = rows_here * hh
    refs = list(refs)
    take = lambda count: [refs.pop(0) for _ in range(count)]
    is_first = items[0][0] == 1 and items[0][2] is None
    makes_u = any(item[1] for item in items)
    ranges = [item[2] for item in items if item[2] is not None]
    half = ranges[0] if ranges and ranges[0] != "all" else None
    sources = [take(2 if item[0] == 1 else 1) for item in items]
    qw_refs = [take(1)[0] if item[2] is not None else None for item in items]
    (keys_ref,) = take(1)
    if is_first:
        stat_refs = take(nh)
        rw_ref, logits_ref, score_ref = take(3)
    else:
        (grad_ref,) = take(1)
    before_ref = take(1)[0] if has_before else None
    if makes_u:
        (u_ref,) = take(1)
    if ranges:
        kg_refs = take(n // 2 if half == "second" else 1)
    if is_first:
        (grad_ref,) = take(1)
    if half is not None:
        mask_ref, kg_acc = take(2)
    else:
        masks = take(2)
        (u_acc,) = take(1)
    if is_first:
        (cols,) = take(1)
        stats = [ref[0] for ref in stat_refs]
        score_gradient(cfg, meta_ref, stats, rw_ref, logits_ref, score_ref, cols, grad_ref)
    tile = chunk
    chunks = max(1, min(4, hh))
    heads = hh // chunks
    part = heads * rows_here
    side = tile // 2

    todo = []
    for index, (_, is_u, keys_range) in enumerate(items):
        base = 0
        for ref in sources[index]:
            tiles = n // 2 if half is not None else ref.shape[1] // tile
            todo.append((index, is_u, keys_range, ref, base, tiles))
            base += tiles

    for index, is_u, keys_range, source_ref, base, tiles in todo:
        qw_ref = qw_refs[index]
        is_start = index == 0 or items[index - 1][2] is None

        def tile_at(s, first=0, size=tile, base=base):
            if half is None:
                position = s + base
            else:
                position = meta_ref[3 + (n // 2 if half == "second" else 0) + s]
            return pl.ds(pl.multiple_of(position * tile + first, size), size)

        def local(s, first=0, size=tile):
            return pl.ds(pl.multiple_of(s * tile + first, size), size)

        def mask_at(buffer, s, at, first=0, size=tile):
            if half is None:
                return masks[buffer].at[at, first : first + size]
            return mask_ref.at[at, local(s, first, size)]

        def mask_part(buffer, s, i, source_ref=source_ref):
            at = slice(i * part, (i + 1) * part)
            g = grad_ref[:, tile_at(s)]
            value = source_ref[at, local(s)]
            wide = jnp.broadcast_to(g[None], (heads, rows_here, tile)).reshape(part, tile)
            value = jnp.where(value > 0, wide, jnp.zeros_like(wide))
            mask_at(buffer, s, at)[...] = value.astype(jnp.bfloat16)

        def mask(buffer, s):
            for i in range(chunks):
                mask_part(buffer, s, i)

        def step(buffer, s, following):
            for i in range(chunks):
                if following is not None:
                    mask_part(1 - buffer, following, i)
                if is_u:
                    at = slice(i * part, (i + 1) * part)
                    u_acc[at, :] += jnp.dot(
                        mask_at(buffer, s, at)[...],
                        keys_ref[tile_at(s), :],
                        preferred_element_type=jnp.float32,
                    )
                if keys_range is None or i % (chunks // 2) != chunks // 2 - 1:
                    continue
                first = i // (chunks // 2) * side
                more = jnp.dot(
                    qw_ref[...],
                    mask_at(buffer, s, slice(0, rows), first, side)[...],
                    preferred_element_type=jnp.float32,
                )
                here = tile_at(s, first, side)
                if not is_start:
                    more = kg_refs[0][:, here] + more
                elif before_ref is not None:
                    more = before_ref[:, here] + more
                if half is None:
                    kg_refs[0][:, here] = more
                else:
                    kg_acc[:, local(s, first, side)] = more

        if is_u and base == 0:
            u_acc[...] = jnp.zeros_like(u_acc)
        in_pairs(tiles, mask, step)
        if is_u and (base + tiles) == n:
            u_ref[...] = u_acc[...].astype(u_ref.dtype)

    if half is not None:
        for i in range(n // 2):
            value = kg_acc[:, i * chunk : (i + 1) * chunk].T
            if half == "first":
                kg_refs[0][i] = value.astype(kg_refs[0].dtype)
            else:
                kg_refs[i][...] = value


def own_active_kernel(cfg, meta_ref, q_ref, keys_t_ref, first_ref, second_ref):
    order, nh, rows_here, hh, depth, kc, chunk, scale = cfg
    side = min(256, chunk)
    for half, active_ref in enumerate((first_ref, second_ref)):
        for s, k in enumerate(range(1 - half, len(order), 2)):
            for first in range(0, chunk, side):
                column = order.index(k) * chunk + first
                dots = jnp.dot(
                    q_ref[: rows_here * hh, :],
                    keys_t_ref[:, column : column + side],
                    preferred_element_type=jnp.float32,
                )
                active = jnp.maximum(dots, 0.0).astype(jnp.bfloat16)
                active_ref[:, s * chunk + first : s * chunk + first + side] = active


def query_kernel(cfg, meta_ref, first_ref, second_ref, keys_ref, u_ref, u_acc):
    order, chunk = cfg[0], cfg[6]
    for half, mask_ref in enumerate((first_ref, second_ref)):
        for s, k in enumerate(range(1 - half, len(order), 2)):
            position = order.index(k)
            more = jnp.dot(
                mask_ref[:, s * chunk : (s + 1) * chunk],
                keys_ref[position * chunk : (position + 1) * chunk, :],
                preferred_element_type=jnp.float32,
            )
            if half == 0 and s == 0:
                u_acc[...] = more
            else:
                u_acc[...] += more
    u_ref[...] = u_acc[...]


def prepare_kernel(cfg, query_ref, weights_ref, rw_ref, keys_ref, logits_ref, *refs):
    order, nh, rows_here, hh, depth, kc, chunk, scale = cfg
    sends = len(order) // 2
    rows = rows_here * hh
    parts = chunk // lanes
    message_ref, rw_out_ref, key_refs = refs[0], refs[1], refs[2 : 2 + sends]
    query_here, weights_here, rw_here, wide, sems = refs[-5:]
    share = pl.multiple_of(lax.axis_index("head") * chunk, chunk)
    copies = []

    def copy(source, target):
        copies.append(pltpu.make_async_copy(source, target, sems.at[len(copies)]))
        copies[-1].start()

    copy(query_ref, query_here)
    copy(rw_ref, rw_here)
    copy(weights_ref, weights_here)
    for i in reversed(range(sends)):
        copy(keys_ref.at[pl.ds(share, chunk), :], key_refs[i].at[:chunk, :])
        for core in range(2):
            row = pl.multiple_of((lax.axis_index("ctx") ^ (2 * i) ^ core) * rows_here, rows_here)
            for part in range(parts):
                first = chunk + (parts * core + part) * rows_here
                copy(
                    logits_ref.at[pl.ds(row, rows_here), pl.ds(share + part * lanes, lanes)],
                    key_refs[i].at[first : first + rows_here, :],
                )
    for item in copies[:3]:
        item.wait()
    every = jnp.broadcast_to(rw_here[...], (8, rw_here.shape[1]))
    shift = every.shape[1] - lax.axis_index("ctx") * rows_here
    here = pltpu.roll(every, shift, 1)[:1, : rw_out_ref.shape[1]]
    rw_out_ref[...] = here * float(kc * len(order)) ** 0.5
    wide[...] = query_here[...].astype(jnp.float32)
    for head in range(hh):
        at = slice(head * rows_here, (head + 1) * rows_here)
        message_ref[at, :] = wide[:, head, :].astype(jnp.bfloat16)
    message_ref[rows:, :] = jnp.zeros((message_ref.shape[0] - rows, lanes), jnp.bfloat16)
    message_ref[rows : rows + hh, :rows_here] = weights_here[...]
    for item in copies[3:]:
        item.wait()


def add_kernel(u_ref, moving_ref, out_ref):
    out_ref[...] = (u_ref[...] + moving_ref[...].astype(jnp.float32)).astype(out_ref.dtype)


def finish_kernel(cfg, u_ref, moving_ref, q_ref, query_grad_ref, weight_grad_ref):
    order, nh, rows_here, hh, depth, kc, chunk, scale = cfg
    rows = rows_here * hh
    eye = (
        lax.broadcasted_iota(jnp.int32, (rows_here, lanes), 0)
        == lax.broadcasted_iota(jnp.int32, (rows_here, lanes), 1)
    ).astype(jnp.float32)
    lane = lax.broadcasted_iota(jnp.int32, (lanes, lanes), 1)[:rows_here]
    slab = q_ref[rows:, :].astype(jnp.float32)
    out = jnp.zeros((rows_here, lanes), jnp.float32)
    for head in range(hh):
        at = slice(head * rows_here, (head + 1) * rows_here)
        total = u_ref[at, :] + moving_ref[at, :].astype(jnp.float32)
        w = jnp.sum(slab[head : head + 1] * eye, axis=1, keepdims=True) * scale
        query_grad_ref[:, head, :] = total * w
        along = jnp.sum(total * q_ref[at, :].astype(jnp.float32), axis=1, keepdims=True)
        out = jnp.where(lane == head, along * scale, out)
    if rows_here < lanes:
        out = jnp.concatenate([out, jnp.zeros((lanes - rows_here, lanes), jnp.float32)], axis=0)
    weight_grad_ref[...] = out.T[:hh, :rows_here]


def per_device(query, weights, keys, main_logits, row_weight, offset):
    n = lax.axis_size("ctx")
    nh = lax.axis_size("head")
    c = lax.axis_index("ctx")
    h = lax.axis_index("head")
    rows_here, hh, depth = query.shape
    kc = keys.shape[0]
    chunk = kc // nh
    rows = rows_here * hh
    scale = depth ** (-0.5)
    bf16, f32 = jnp.bfloat16, jnp.float32

    groups = [
        [1, 0],
        list(range(3, n - 2, 2)) + list(range(2, n - 2, 2)),
        [n - 1, n - 2],
    ]
    order = sum(groups, [])
    cfg = (order, nh, rows_here, hh, depth, kc, chunk, scale)
    smem = pl.BlockSpec(memory_space=pltpu.SMEM)
    vmem = pl.BlockSpec(memory_space=pltpu.VMEM)
    padded = -(-rows_here // lanes) * lanes
    table = [order.index(k) for k in list(range(1, n, 2)) + list(range(0, n, 2))]
    meta = jnp.concatenate(
        [offset, jnp.stack([c, h]).astype(jnp.int32), jnp.array(table, jnp.int32)]
    )

    far = lambda x: pltpu.with_memory_space_constraint(x, pltpu.HBM)

    slab_rows = -(-hh // 16) * 16
    parts = chunk // lanes
    message, rw, *key_messages = pl.pallas_call(
        functools.partial(prepare_kernel, cfg),
        out_shape=[
            jax.ShapeDtypeStruct((rows + slab_rows, depth), bf16),
            jax.ShapeDtypeStruct((1, padded), f32),
        ]
        + [jax.ShapeDtypeStruct((chunk + 2 * parts * rows_here, depth), bf16)] * (n // 2),
        in_specs=[pl.BlockSpec(memory_space=pltpu.HBM)] * 5,
        out_specs=[vmem] * (2 + n // 2),
        scratch_shapes=[
            pltpu.VMEM((rows_here, hh, depth), bf16),
            pltpu.VMEM((hh, rows_here), bf16),
            pltpu.VMEM((1, rows_here * n), f32),
            pltpu.VMEM((rows_here, hh, depth), f32),
            pltpu.SemaphoreType.DMA((3 + n // 2 * (1 + 2 * parts),)),
        ],
        compiler_params=pltpu.CompilerParams(vmem_limit_bytes=vmem_bytes),
        cost_estimate=pl.CostEstimate(
            flops=rows * depth, bytes_accessed=4 * 1024 * 1024, transcendentals=0
        ),
        name="prepare",
    )(far(query), far(weights.T), far(row_weight[None, :]), far(keys), far(main_logits))
    q_blocks = [message] * nh
    for hop in range(1, nh // 2 + 1):
        q_blocks[hop] = ring_next(q_blocks[hop - 1], "head")
        if nh - hop > hop:
            q_blocks[nh - hop] = ring_next(q_blocks[(nh - hop + 1) % nh], "head", -1)
    arrival = [1]
    for hop in range(1, nh // 2 + 1):
        arrival += [j for j in sorted({hop, nh - hop}) if j not in arrival]

    k_pieces = [None] * n
    k_pieces[0::2] = [key_messages[0]] + [
        swap(key_messages[k // 2], "ctx", k) for k in range(2, n, 2)
    ]
    k_pieces[1] = swap(k_pieces[0], "ctx", 1)
    total_keys = n * chunk
    macs = rows * total_keys * depth
    tile = chunk

    def call(kernel, operands, out_shape, scratch, products, name, aliases={}):
        return pl.pallas_call(
            kernel,
            out_shape=out_shape,
            input_output_aliases=aliases,
            in_specs=[smem] + [vmem] * len(operands),
            out_specs=[vmem] * len(out_shape),
            scratch_shapes=scratch,
            compiler_params=pltpu.CompilerParams(vmem_limit_bytes=vmem_bytes),
            cost_estimate=pl.CostEstimate(
                flops=int(4 * products * macs),
                bytes_accessed=int(4 * products * 2**20),
                transcendentals=0,
            ),
            name=name,
        )(meta, *operands)

    near = lambda x: pltpu.with_memory_space_constraint(x, pltpu.VMEM)

    wide_shape = pltpu.VMEM((hh, rows_here, lanes), f32)
    qw_shape = pltpu.VMEM((depth, rows), bf16)

    def keys_shapes(count):
        return [
            pltpu.VMEM((rows_here, count), f32),
            pltpu.VMEM((count, depth), bf16),
            pltpu.VMEM((depth, count), bf16),
            pltpu.VMEM((rows_here, count), bf16),
        ]

    nears = lambda xs: [near(x) for x in xs]
    early, qw, wides = [], [], []
    for i, group in enumerate(groups[:2]):
        if i == 1:
            far_even = range(2, n - 2, 2)
            wides[0], *came = lax.optimization_barrier((wides[0], *(k_pieces[k] for k in far_even)))
            for k, piece in zip(far_even, came):
                k_pieces[k], k_pieces[k + 1] = piece, swap(piece, "ctx", 1)
        count = (len(group) + i * len(groups[0])) * chunk
        outs = call(
            functools.partial(forward_early_kernel, cfg, groups[0] if i == 1 else [], group),
            q_blocks[: i + 1] + nears(wides) + nears(early) + [k_pieces[k] for k in group],
            keys_shapes(count) + [pltpu.VMEM((rows, count), bf16)] * i + [qw_shape, wide_shape],
            [],
            0.001,
            f"forward_early_{i}",
        )
        early = list(outs[:4])
        qw.append(outs[-2])
        wides.append(outs[-1])
    early_active = outs[4]
    early[0], came = lax.optimization_barrier((early[0], k_pieces[n - 2]))
    k_pieces[n - 2], k_pieces[n - 1] = came, swap(came, "ctx", 1)
    last = len(groups[2]) * chunk
    outs = call(
        functools.partial(forward_middle_kernel, cfg, [groups[0] + groups[1], groups[2]]),
        q_blocks[:2]
        + nears(wides)
        + [q_blocks[j] for j in arrival[1:-1]]
        + nears(early)
        + [k_pieces[k] for k in groups[2]],
        keys_shapes(total_keys)
        + [pltpu.VMEM((rows, last), bf16)]
        + [pltpu.VMEM((rows, total_keys), bf16)] * (nh - 3)
        + [qw_shape] * (nh - 3),
        [pltpu.VMEM((hh, rows_here, lanes), f32)],
        nh - 2.5,
        "forward_middle",
    )
    score, keys_all, keys_t, logits = outs[:4]
    active = {1: [early_active, outs[4]]}
    qw = dict(enumerate(qw))
    for i, j in enumerate(arrival[1:-1]):
        active[j], qw[j] = [outs[5 + i]], outs[5 + nh - 3 + i]
    score, last_active, last_qw, stats = call(
        functools.partial(forward_last_kernel, cfg),
        [q_blocks[arrival[-1]], near(keys_t), near(score), near(logits)],
        [
            pltpu.VMEM((rows_here, total_keys), f32),
            pltpu.VMEM((rows, total_keys), bf16),
            qw_shape,
            jax.ShapeDtypeStruct((1, stat_rows, padded), f32),
        ],
        [pltpu.VMEM((hh, rows_here, lanes), f32)],
        1,
        "forward_last",
        {3: 0},
    )
    active[arrival[-1]], qw[arrival[-1]] = [last_active], last_qw

    all_stats = [stats] + [swap(stats, "head", j) for j in range(1, nh)]

    q_own, _ = lax.optimization_barrier((q_blocks[0], stats))
    outs = call(
        functools.partial(own_active_kernel, cfg),
        [q_own, near(keys_t)],
        [pltpu.VMEM((rows, total_keys // 2), bf16)] * 2,
        [],
        1,
        "own_active",
    )
    rw, *outs = lax.optimization_barrier((rw, *outs))
    own_active = {"first": outs[:1], "second": outs[1:]}

    grad = kg = None

    def backward(items, name):
        nonlocal grad, kg
        is_first = grad is None
        ranges = [item[2] for item in items if item[2] is not None]
        makes_u = any(item[1] for item in items)
        has_before = bool(ranges) and kg is not None
        halved = ranges != [] and ranges[0] != "all"
        operands = []
        for item in items:
            operands += nears(own_active[ranges[0]] if halved else active[item[0]])
        operands += [near(qw[item[0]]) for item in items if item[2] is not None]
        operands += [near(keys_all)]
        operands += all_stats + [rw, near(logits), near(score)] if is_first else [near(grad)]
        aliases = {}
        out_shape = [jax.ShapeDtypeStruct((rows, depth), bf16 if is_first else f32)]
        out_shape = out_shape if makes_u else []
        scratch = [pltpu.VMEM((rows, tile), bf16)] * 2 + [pltpu.VMEM((rows, depth), f32)]
        if not halved:
            if ranges:
                if has_before:
                    aliases = {len(operands) + 1: len(out_shape)}
                out_shape += [pltpu.VMEM((depth, total_keys), f32)]
        else:
            if ranges[0] == "first":
                out_shape += [jax.ShapeDtypeStruct((n // 2, chunk, depth), bf16)]
            else:
                out_shape += [jax.ShapeDtypeStruct((chunk, depth), f32)] * (n // 2)
            out_shape += [pltpu.VMEM((rows, total_keys // 2), bf16)]
            scratch = [pltpu.VMEM((depth, total_keys // 2), f32)]
        if has_before:
            operands += [near(kg)]
        if is_first:
            out_shape += [pltpu.VMEM((rows_here, total_keys), bf16)]
            scratch += [pltpu.VMEM((padded, lanes), f32)]
        kernel = functools.partial(backward_kernel, cfg, items, has_before)
        products = 1 if halved else makes_u + len(ranges)
        outs = call(kernel, operands, out_shape, scratch, products, name, aliases)
        if is_first:
            grad = outs[-1]
        if ranges and ranges[0] == "all":
            kg = outs[1 if makes_u else 0]
        return outs

    part = backward([(1, True, None)], "backward_1")[0]
    moving = ring_next(part, "head")
    for j in range(2, nh):
        items = ([(1, False, "all")] if j == 2 else []) + [(j, True, "all")]
        part = backward(items, f"backward_{j}")[0]
        part = pl.pallas_call(
            add_kernel,
            out_shape=jax.ShapeDtypeStruct((rows, depth), bf16),
            in_specs=[vmem] * 2,
            out_specs=vmem,
            compiler_params=pltpu.CompilerParams(vmem_limit_bytes=vmem_bytes),
            cost_estimate=pl.CostEstimate(
                flops=rows * depth, bytes_accessed=8 * rows * depth, transcendentals=0
            ),
            name=f"add_{j}",
        )(part, moving)
        kg, part = lax.optimization_barrier((kg, part))
        moving = ring_next(part, "head")

    odd, mask_first = backward([(0, False, "first")], "backward_0_first")
    other = swap(odd, "ctx", 1)
    *even, mask_second = backward([(0, False, "second")], "backward_0_second")
    even = [even[i] + other[i].astype(f32) for i in range(n // 2)]
    key_grad = even[0]
    sends = [even[i].astype(bf16) for i in range(1, n // 2)]
    keys_all, *sends = lax.optimization_barrier((keys_all, *sends))
    for i in range(1, n // 2):
        key_grad = key_grad + swap(sends[i - 1], "ctx", 2 * i).astype(f32)
    (u_mine,) = call(
        functools.partial(query_kernel, cfg),
        [near(mask_first), near(mask_second), near(keys_all)],
        [jax.ShapeDtypeStruct((rows, depth), f32)],
        [pltpu.VMEM((rows, depth), f32)],
        1,
        "backward_0",
    )

    query_grad, weight_grad = pl.pallas_call(
        functools.partial(finish_kernel, cfg),
        out_shape=[
            jax.ShapeDtypeStruct((rows_here, hh, depth), f32),
            jax.ShapeDtypeStruct((hh, rows_here), f32),
        ],
        in_specs=[vmem] * 3,
        out_specs=[vmem] * 2,
        compiler_params=pltpu.CompilerParams(vmem_limit_bytes=vmem_bytes),
        cost_estimate=pl.CostEstimate(
            flops=8 * rows * depth, bytes_accessed=14 * rows * depth, transcendentals=0
        ),
        name="finish",
    )(u_mine, moving, q_blocks[0])
    return query_grad, key_grad, weight_grad.T


def solution(mesh):
    in_specs = (P("ctx", "head", None), P("ctx", "head"), P("ctx", None), P(None, "ctx"), P(), P())
    out_specs = (P("ctx", "head", None), P(("ctx", "head"), None), P("ctx", "head"))
    return jax.shard_map(
        per_device, mesh=mesh, in_specs=in_specs, out_specs=out_specs, check_vma=False
    )
```
